256 devices in a mesh: dp: 16 (over y, x), tensor: 16 (over z, core).
Axes of the slice: x: 4, y: 4, z: 8, core: 2. Of those that a mesh axis runs over, the one named last changes fastest.
Arguments:
- inputs: bfloat16 [2048, 7168], P('dp', 'tensor'), may hold values from -6 to 6
- out_grad: bfloat16 [2048, 7168], P('dp', 'tensor'), may hold values from -6 to 6
- w_in: bfloat16 [112, 8, 128, 128], P('tensor'), may hold values from -0.21875 to 0.21875
- w_out: bfloat16 [112, 8, 128, 128], P('tensor'), may hold values from -0.25 to 0.25
- columns: int32 [112, 8], P('tensor'), may hold values from 0 to 55, as said below
- counts: int32 [112], P('tensor'), may hold values from 4 to 8, as said below
Outputs:
- outputs: bfloat16 [2048, 7168], P('dp', 'tensor')
- input_grad: bfloat16 [2048, 7168], P('dp', 'tensor')
- grad_win: float32 [112, 8, 128, 128], P('tensor', None, 'dp')
- grad_wout: float32 [112, 8, 128, 128], P('tensor', None, 'dp')
The draws below stay inside these ranges and needn't reach their ends.
Inputs may be any that keep to these rules, and one draw needn't show every extreme that they name: Within each hidden block-row the 8 listed block-columns are distinct. `counts`: some hidden block-row has all 8 slots live; slots at or past a row's count are ignored.
All inputs are finite; a program needn't handle non-finite values.
Results may differ from the reference program's by a relative error of at most 0.018.
Values may be sent and summed in bfloat16 or wider, within the bound.
A program may use at most 64 MiB of HBM per device.

```python
import jax
import jax.numpy as jnp
from jax import lax

D = 7168
BLK = 128
K = 8
KMIN = 4
TOKENS = 2048
HB = 112
DB = 56
N_TENSOR = 16


def draw_columns(key, part):
    key = jax.random.fold_in(key, 11)
    row_keys = jax.random.split(key, HB)
    orders = jax.vmap(lambda one: jax.random.permutation(one, DB))(row_keys)
    return orders[:, :K].astype(jnp.int32)


def draw_counts(key, part):
    key = jax.random.fold_in(key, 23)
    first, second = jax.random.split(key)
    drawn = jax.random.randint(first, (HB,), KMIN, K + 1).astype(jnp.int32)
    where = jax.random.randint(second, (), 0, HB)
    return drawn.at[where].set(K).astype(jnp.int32)


def level_of(key, extent, pieces, smallest, largest):
    loudness = 1.0
    for dim, parts in pieces:
        draws = jax.random.uniform(jax.random.fold_in(jax.random.fold_in(key, 6), dim), (parts,), jnp.float32, smallest / len(pieces), largest / len(pieces))
        loudness = loudness * jnp.repeat(jnp.exp(draws), extent[dim] // parts).reshape((-1,) + (1,) * (len(extent) - 1 - dim))
    return loudness


def noise(stream_key, shape, scale, bound, cuts=(), held_as=jnp.bfloat16):
    result = jax.random.normal(stream_key, shape, jnp.float32) * scale
    if len(cuts) > 0:
        result = level_of(stream_key, shape, cuts, -0.22, 0.18) * result
    return jnp.clip(result, min=-bound, max=bound).astype(held_as)


def setup_inputs(seed: int = 0) -> dict:
    keys = jax.random.split(jax.random.key(seed), 7)
    return {
        "inputs": noise(keys[0], (TOKENS, D), 1.0, 6.0, ((0, 16), (1, 16))),
        "out_grad": noise(keys[1], (TOKENS, D), 1.0, 6.0, ((0, 16), (1, 16))),
        "w_in": noise(keys[2], (HB, K, BLK, BLK), (BLK * (KMIN + K) // 2) ** -0.5, 0.21875, ((0, 16),)),
        "w_out": noise(keys[3], (HB, K, BLK, BLK), (BLK * 4) ** -0.5, 0.25, ((0, 16),)),
        "columns": draw_columns(jax.random.fold_in(keys[6], 71), 0),
        "counts": draw_counts(jax.random.fold_in(keys[6], 71), 0),
    }


def gelu_tanh(value):
    return jax.nn.gelu(value, approximate=True)

def place_blocks(contrib, onehot):
    placed = jnp.einsum('tjc,jd->tdc', contrib, onehot, precision=lax.Precision.HIGHEST)
    return placed.reshape(contrib.shape[0], -1)

def reference(inputs, out_grad, w_in, w_out, columns, counts):
    groups = N_TENSOR
    per_group = HB // groups
    total = inputs.shape[0]
    live = jnp.arange(K, dtype=jnp.int32)[None, :] < counts[:, None]
    live_b = live.astype(jnp.bfloat16)[:, :, None, None]
    live_f = live.astype(jnp.float32)[:, :, None, None]
    w_in_live = w_in * live_b
    w_out_live = w_out * live_b
    in_three = inputs.reshape(total, DB, BLK)
    grad_three = out_grad.reshape(total, DB, BLK)
    cols_g = columns.reshape(groups, per_group, K)
    win_g = w_in_live.reshape(groups, per_group, K, BLK, BLK)
    wout_g = w_out_live.reshape(groups, per_group, K, BLK, BLK)
    livef_g = live_f.reshape(groups, per_group, K, 1, 1)

    def step(carry, item):
        sum_out, sum_in = carry
        cols, win, wout, livef = item
        flat = cols.reshape(-1).astype(jnp.int32)
        onehot = (flat[:, None] == jnp.arange(DB, dtype=jnp.int32)[None, :]).astype(jnp.float32)
        x_blocks = jnp.take(in_three, flat, axis=1).reshape(total, per_group, K, BLK).astype(jnp.float32)
        g_blocks = jnp.take(grad_three, flat, axis=1).reshape(total, per_group, K, BLK).astype(jnp.float32)
        win_f = win.astype(jnp.float32)
        wout_f = wout.astype(jnp.float32)
        pre = jnp.einsum('tnki,nkib->tnb', x_blocks, win_f)
        hidden = gelu_tanh(pre).astype(jnp.bfloat16)
        contrib = jnp.einsum('tnb,nkbc->tnkc', hidden.astype(jnp.float32), wout_f).reshape(total, per_group * K, BLK)
        part_out = place_blocks(contrib, onehot).astype(jnp.bfloat16)
        grad_hidden = jnp.einsum('tnkc,nkbc->tnb', g_blocks, wout_f)
        grad_wout = jnp.einsum('tnb,tnkc->nkbc', hidden.astype(jnp.float32), g_blocks) * livef
        grad_pre = jax.vjp(gelu_tanh, pre)[1](grad_hidden)[0].astype(jnp.bfloat16)
        grad_win = jnp.einsum('tnki,tnb->nkib', x_blocks, grad_pre.astype(jnp.float32)) * livef
        back = jnp.einsum('tnb,nkib->tnki', grad_pre.astype(jnp.float32), win_f).reshape(total, per_group * K, BLK)
        part_in = place_blocks(back, onehot).astype(jnp.bfloat16)
        sum_out = sum_out + part_out.astype(jnp.float32)
        sum_in = sum_in + part_in.astype(jnp.float32)
        return ((sum_out, sum_in), (grad_win, grad_wout))
    start = (jnp.zeros((total, D), jnp.float32), jnp.zeros((total, D), jnp.float32))
    (sum_out, sum_in), (grad_win, grad_wout) = lax.scan(step, start, (cols_g, win_g, wout_g, livef_g))
    grad_win = grad_win.reshape(HB, K, BLK, BLK)
    grad_wout = grad_wout.reshape(HB, K, BLK, BLK)
    return (sum_out.astype(jnp.bfloat16), sum_in.astype(jnp.bfloat16), grad_win, grad_wout)
```

```python
import functools

import jax
import jax.numpy as jnp
from jax import lax
from jax.experimental import pallas as pl
from jax.experimental.pallas import tpu as pltpu
from jax.sharding import PartitionSpec as P

BLK = 128
SLOTS = 8
ROWS = 7
NB = ROWS * SLOTS
DB = 56
NZ = 8
NQ = 4
CH = 448
BF = jnp.bfloat16
F32 = jnp.float32
MESH = pl.DeviceIdType.MESH
C0 = 0.7978845608028654
C1 = 0.044715


def cat(parts, axis):
    return jnp.concatenate(parts, axis=axis)


def kernel(
    pick_ref, tab_ref, x_ref, g_ref, win_hbm, wout_hbm,
    out_ref, ing_ref, gwin_ref, gwout_ref,
    xg, gg, xb, gb, win, wout, dgelu, hid, gpre, cbuf, part, sib, rp, rm, wgt, wp, red, w2,
    lsem, ag_s, ag_r, sb_s, sb_r, ss_s, ss_r, zs, zr, xs, xr,
):
    dp = lax.axis_index("dp")
    tn = lax.axis_index("tensor")
    yy, xx = dp // NQ, dp % NQ
    z, core = tn // 2, tn % 2

    def zdev(step):
        return {"dp": dp, "tensor": ((z + step + NZ) % NZ) * 2 + core}

    sdev = {"dp": dp, "tensor": z * 2 + (1 - core)}

    def ydev(step):
        return {"dp": ((yy + step + NQ) % NQ) * NQ + xx, "tensor": tn}

    def xdev(step):
        return {"dp": yy * NQ + (xx + step + NQ) % NQ, "tensor": tn}

    sends = []

    def rcopy(src, dst, ssem, rsem, dev):
        return pltpu.make_async_remote_copy(
            src_ref=src, dst_ref=dst, send_sem=ssem, recv_sem=rsem,
            device_id=dev, device_id_type=MESH,
        )

    def go(copy):
        copy.start()
        sends.append(copy)

    wcopies = [
        pltpu.make_async_copy(win_hbm, win, lsem.at[0]),
        pltpu.make_async_copy(wout_hbm, wout, lsem.at[1]),
    ]
    for c in wcopies:
        c.start()

    barrier = pltpu.get_barrier_semaphore()
    for dev in (sdev, zdev(1), zdev(-1), xdev(1), xdev(-1), ydev(1), ydev(-1)):
        pl.semaphore_signal(barrier, inc=1, device_id=dev, device_id_type=MESH)

    def fold(src, dst):
        base = pl.multiple_of(tn * CH, 64)

        @pl.when(core == 0)
        def _():
            v = src[...]
            for k in range(3):
                dst[pl.ds(base + 128 * k, 128), :] = v[:, 128 * k:128 * k + 128]
            h = v[:, 384:448].astype(F32)
            dst[pl.ds(base + 384, 64), :] = cat([h[:64], h[64:]], 1).astype(BF)

        @pl.when(core == 1)
        def _():
            v = src[...].astype(F32)
            for k in range(3):
                dst[pl.ds(base + 128 * k, 128), :] = v[:, 64 + 128 * k:192 + 128 * k].astype(BF)
            h = v[:, 0:64]
            dst[pl.ds(base + 384, 64), :] = cat([h[64:], h[:64]], 1).astype(BF)

    fields = (xg, gg)
    fold(x_ref, xg)
    fold(g_ref, gg)
    pl.semaphore_wait(barrier, 7)

    def rows(ref, t, lo=0, n=CH):
        return ref.at[pl.ds(pl.multiple_of(t * CH + lo, 32), n), :]

    def zchunk(step):
        return ((z + step + 2 * NZ) % NZ) * 2 + core

    def ag_span(way, k):
        if k < 3:
            return 0, CH
        return (0, CH // 2) if way == 0 else (CH // 2, CH // 2)

    def ag_copy(a, way, k, t):
        lo, n = ag_span(way, k)
        i = (a * 2 + way) * 4 + k
        v = rows(fields[a], t, lo, n)
        return rcopy(v, v, ag_s.at[i], ag_r.at[i], zdev(1 if way == 0 else -1))

    def sb_copy(a, j, t, lo=0, n=CH):
        v = rows(fields[a], t, lo, n)
        return rcopy(v, v, sb_s.at[a * 9 + j], sb_r.at[a * 9 + j], sdev)

    def sb_span(j):
        if j == 0:
            return 0, 0, CH
        way, k = (j - 1) // 4, (j - 1) % 4
        lo, n = ag_span(way, k)
        return (-(k + 1) if way == 0 else k + 1), lo, n

    for a in range(2):
        for way in range(2):
            go(ag_copy(a, way, 0, tn))
    for a in range(2):
        go(sb_copy(a, 0, tn))
    for k in range(4):
        for a in range(2):
            for way in range(2):
                step = -(k + 1) if way == 0 else k + 1
                t = zchunk(step)
                ag_copy(a, way, k, t).wait_recv()
                if k < 3:
                    go(ag_copy(a, way, k + 1, t))
                lo, n = ag_span(way, k)
                go(sb_copy(a, 1 + way * 4 + k, t, lo, n))
                if k == 0 and way == 1 and a == 1:
                    xb[DB] = jnp.zeros((BLK, BLK), BF)
                    gb[DB] = jnp.zeros((BLK, BLK), BF)
                    cbuf[NB] = jnp.zeros((BLK, BLK), F32)
                    for c in wcopies:
                        c.wait()

    lane = lax.broadcasted_iota(jnp.int32, (64, 128), 1)

    def gathered(a):
        for j in range(9):
            step, lo, n = sb_span(j)
            t = ((z + step + 2 * NZ) % NZ) * 2 + (1 - core)
            sb_copy(a, j, t, lo, n).wait_recv()
        ref, out = fields[a], (xb, gb)[a]

        def whole(zz, carry):
            one = pl.multiple_of(zz * 2 * CH, 128)
            two = pl.multiple_of(zz * 2 * CH + CH, 64)
            for k in range(3):
                out[zz * 7 + k] = ref[pl.ds(one + 128 * k, 128), :]
                out[zz * 7 + 4 + k] = ref[pl.ds(two + 128 * k, 128), :]
            h0 = ref[pl.ds(one + 384, 64), :].astype(F32)
            h1 = ref[pl.ds(two + 384, 64), :].astype(F32)
            top = jnp.where(lane < 64, h0, h1)
            low = pltpu.roll(jnp.where(lane < 64, h1, h0), 64, 1)
            out[zz * 7 + 3] = cat([top, low], 0).astype(BF)
            return carry

        lax.fori_loop(0, NZ, whole, 0)

    def listed(ref, n):
        return cat([ref[pick_ref[n * SLOTS + s]] for s in range(SLOTS)], 1)

    def wide(ref, n):
        return cat([ref[n * SLOTS + s] for s in range(SLOTS)], 1)

    def tall(ref, n):
        return ref[pl.ds(n * SLOTS, SLOTS)].reshape(SLOTS * BLK, BLK)

    def keep(n, prod):
        for s in range(SLOTS):
            cbuf[n * SLOTS + s] = prod[:, s * BLK:(s + 1) * BLK]

    gathered(0)

    def forward(n, carry):
        pre = jnp.dot(listed(xb, n), tall(win, n), preferred_element_type=F32)
        sq = pre * pre
        th = jnp.tanh(C0 * pre * (1.0 + C1 * sq))
        half = 0.5 * (1.0 + th)
        dgelu[n] = half + 0.5 * pre * (1.0 - th * th) * (C0 * (1.0 + 3.0 * C1 * sq))
        h = (pre * half).astype(BF)
        hid[n] = h
        keep(n, jnp.dot(h, wide(wout, n), preferred_element_type=F32))
        return carry

    lax.fori_loop(0, ROWS, forward, 0)

    def sib_copy(a, zz):
        return rcopy(
            part.at[a, 1 - core, zz], sib.at[a, zz], ss_s.at[a * NZ + zz], ss_r.at[a * NZ + zz], sdev
        )

    ORDER = (4, 3, -3, 2, -2, 1, -1, 0)

    def place(a):
        for step in ORDER:
            zz = (z + step + NZ) % NZ

            def column(k):
                c = zz * 7 + k
                acc = cbuf[tab_ref[c * ROWS]]
                for n in range(1, ROWS):
                    acc = acc + cbuf[tab_ref[c * ROWS + n]]
                return acc

            for k in range(3):
                part[a, 0, zz, 128 * k:128 * k + 128, :] = column(k).astype(BF)
                part[a, 1, zz, 128 * k:128 * k + 128, :] = column(k + 4).astype(BF)
            mid = column(3)
            top = mid[:64]
            low = pltpu.roll(mid[64:], 64, 1)
            part[a, 0, zz, 384:448, :] = jnp.where(lane < 64, top, low).astype(BF)
            part[a, 1, zz, 384:448, :] = jnp.where(lane < 64, low, top).astype(BF)
            go(sib_copy(a, zz))

    def chip_sum(a, step):
        zz = (z + step + 2 * NZ) % NZ
        sib_copy(a, zz).wait_recv()
        return zz, part[a, core, zz].astype(F32) + sib[a, zz].astype(F32)

    def z_copy(src, a, way, r):
        i = (a * 2 + way) * 4 + r
        dst = (rp if way == 0 else rm).at[a, r]
        return rcopy(src, dst, zs.at[i], zr.at[i], zdev(1 if way == 0 else -1))

    def z_first(a, way):
        r = 3 if a == way else 2
        step = r + 1 if way == 0 else -(r + 1)
        zz, total = chip_sum(a, step)
        part[a, core, zz] = total.astype(BF)
        go(z_copy(part.at[a, core, zz], a, way, r))

    def z_next(a, way, r):
        buf = rp if way == 0 else rm
        z_copy(buf.at[a, r], a, way, r).wait_recv()
        zz, total = chip_sum(a, r if way == 0 else -r)
        buf[a, r] = (buf[a, r].astype(F32) + total).astype(BF)
        go(z_copy(buf.at[a, r], a, way, r - 1))

    def unfold(total, dst):
        @pl.when(core == 0)
        def _():
            for k in range(3):
                dst[:, 128 * k:128 * k + 128] = total[128 * k:128 * k + 128].astype(BF)
            h = total[384:448]
            dst[:, 384:448] = cat([h[:, :64], h[:, 64:]], 0).astype(BF)

        @pl.when(core == 1)
        def _():
            h = total[384:448]
            parts = [cat([h[:, 64:], h[:, :64]], 0)]
            for k in range(3):
                parts.append(total[128 * k:128 * k + 128])
            dst[...] = cat(parts, 1).astype(BF)

    def z_last(a, dst):
        for way in range(2):
            buf = rp if way == 0 else rm
            z_copy(buf.at[a, 0], a, way, 0).wait_recv()
        _, total = chip_sum(a, 0)
        unfold(total + rp[a, 0].astype(F32) + rm[a, 0].astype(F32), dst)

    coords = ((yy, xx), (xx, yy))
    devs = ((ydev, xdev), (xdev, ydev))

    def w_copy(src, a, m):
        i = a * 6 + m
        return rcopy(src, wp.at[a, m], xs.at[i], xr.at[i], devs[a][0](1 if m < 3 else -1))

    def at4(i):
        return (i + 2 * NQ) % NQ

    def w_first(a):
        p = coords[a][0]
        go(w_copy(wgt.at[a, at4(p + 2), pl.ds(0, 2)], a, 0))
        go(w_copy(wgt.at[a, at4(p - 2), pl.ds(2, 2)], a, 3))
        go(w_copy(wgt.at[a, at4(p + 1), pl.ds(2, 2)], a, 1))
        go(w_copy(wgt.at[a, at4(p - 1), pl.ds(0, 2)], a, 4))

    def w_second(a):
        p = coords[a][0]
        w_copy(wp.at[a, 0], a, 0).wait_recv()
        for q in range(2):
            wp[a, 0, q] = (wp[a, 0, q].astype(F32) + wgt[a, at4(p + 1), q].astype(F32)).astype(BF)
        go(w_copy(wp.at[a, 0], a, 2))
        w_copy(wp.at[a, 3], a, 3).wait_recv()
        for q in range(2):
            wp[a, 3, q] = (wp[a, 3, q].astype(F32) + wgt[a, at4(p - 1), 2 + q].astype(F32)).astype(BF)
        go(w_copy(wp.at[a, 3], a, 5))

    def w_third(a):
        p = coords[a][0]
        for m in (1, 4, 2, 5):
            w_copy(wp.at[a, m], a, m).wait_recv()
        for q in range(2):
            red[a, q] = (
                wgt[a, p, q].astype(F32) + wp[a, 2, q].astype(F32) + wp[a, 4, q].astype(F32)
            ).astype(BF)
            red[a, 2 + q] = (
                wgt[a, p, 2 + q].astype(F32) + wp[a, 5, q].astype(F32) + wp[a, 1, q].astype(F32)
            ).astype(BF)

    H = CH // 2

    def v_copy(src, a, m):
        i = 12 + a * 6 + m
        return rcopy(src, w2.at[a, m], xs.at[i], xr.at[i], devs[a][1](1 if m < 3 else -1))

    def v_first(a):
        q = coords[a][1]
        go(v_copy(red.at[a, at4(q + 2), pl.ds(0, H)], a, 0))
        go(v_copy(red.at[a, at4(q - 2), pl.ds(H, H)], a, 3))
        go(v_copy(red.at[a, at4(q + 1), pl.ds(H, H)], a, 1))
        go(v_copy(red.at[a, at4(q - 1), pl.ds(0, H)], a, 4))

    def v_second(a):
        q = coords[a][1]
        v_copy(w2.at[a, 0], a, 0).wait_recv()
        w2[a, 0] = (w2[a, 0].astype(F32) + red[a, at4(q + 1), 0:H].astype(F32)).astype(BF)
        go(v_copy(w2.at[a, 0], a, 2))
        v_copy(w2.at[a, 3], a, 3).wait_recv()
        w2[a, 3] = (w2[a, 3].astype(F32) + red[a, at4(q - 1), H:CH].astype(F32)).astype(BF)
        go(v_copy(w2.at[a, 3], a, 5))

    def v_third(a, dst):
        q = coords[a][1]
        for m in (1, 4, 2, 5):
            v_copy(w2.at[a, m], a, m).wait_recv()
        dst[0:H, :] = red[a, q, 0:H].astype(F32) + w2[a, 2].astype(F32) + w2[a, 4].astype(F32)
        dst[H:CH, :] = red[a, q, H:CH].astype(F32) + w2[a, 5].astype(F32) + w2[a, 1].astype(F32)

    place(0)
    gathered(1)
    z_first(0, 0)
    z_first(0, 1)

    def backward_out(n, carry):
        picked = listed(gb, n)
        gh = lax.dot_general(picked, wide(wout, n), (((1,), (1,)), ((), ())), preferred_element_type=F32)
        gpre[n] = (gh * dgelu[n]).astype(BF)
        gw = lax.dot_general(hid[n], picked, (((0,), (0,)), ((), ())), preferred_element_type=F32)
        for s in range(0, SLOTS, 2):
            one = gw[:, s * BLK:(s + 1) * BLK].reshape(16, 8, BLK)
            two = gw[:, (s + 1) * BLK:(s + 2) * BLK].reshape(16, 8, BLK)
            row = pl.multiple_of((n * SLOTS + s) * 8, 16)
            wgt[0, :, :, pl.ds(row, 16), :] = cat([one, two], 1).astype(BF).reshape(4, 4, 16, BLK)
        return carry

    lax.fori_loop(0, ROWS, backward_out, 0)
    w_first(0)

    def backward_in(n, carry):
        picked = listed(xb, n)
        gw = lax.dot_general(picked, gpre[n], (((0,), (0,)), ((), ())), preferred_element_type=F32)
        gw = gw.reshape(SLOTS, 16, 8, BLK)
        for s in range(0, SLOTS, 2):
            both = cat([gw[s], gw[s + 1]], 1).astype(BF).reshape(4, 4, 16, BLK)
            row = pl.multiple_of((n * SLOTS + s) * 8, 16)
            for p in range(4):
                for q in range(4):
                    wgt[1, p, q, pl.ds(row, 16), :] = both[q, p]
        return carry

    lax.fori_loop(0, ROWS, backward_in, 0)
    w_first(1)
    z_next(0, 0, 3)
    z_next(0, 1, 2)

    def backward_x(n, carry):
        keep(n, lax.dot_general(gpre[n], tall(win, n), (((1,), (1,)), ((), ())), preferred_element_type=F32))
        return carry

    lax.fori_loop(0, ROWS, backward_x, 0)
    place(1)
    z_next(0, 0, 2)
    z_next(0, 1, 1)
    z_first(1, 0)
    z_first(1, 1)
    z_next(0, 0, 1)
    w_second(0)
    z_next(1, 0, 2)
    z_next(1, 1, 3)
    w_second(1)
    z_next(1, 0, 1)
    z_next(1, 1, 2)
    z_last(0, out_ref)
    z_next(1, 1, 1)
    w_third(0)
    v_first(0)
    w_third(1)
    v_first(1)
    v_second(0)
    v_second(1)
    z_last(1, ing_ref)
    v_third(0, gwout_ref)
    v_third(1, gwin_ref)
    for c in sends:
        c.wait_send()


def on_device(inputs, out_grad, w_in, w_out, columns, counts):
    nrows, slots = columns.shape
    live = lax.broadcasted_iota(jnp.int32, (nrows, slots), 1) < counts[:, None]
    pick = jnp.where(live, columns, DB).reshape(-1)
    slot = lax.broadcasted_iota(jnp.int32, (nrows, slots), 0) * slots + lax.broadcasted_iota(
        jnp.int32, (nrows, slots), 1
    )
    same = (jnp.where(live, columns, -1)[None] == jnp.arange(DB, dtype=jnp.int32)[:, None, None])
    tab = jnp.min(jnp.where(same, slot[None], NB), axis=2).reshape(-1)

    vm = pl.BlockSpec(memory_space=pltpu.VMEM)
    sm = pl.BlockSpec(memory_space=pltpu.SMEM)
    anyw = pl.BlockSpec(memory_space=pl.ANY)
    dma = pltpu.SemaphoreType.DMA
    out, ing, gwin, gwout = pl.pallas_call(
        kernel,
        out_shape=(
            jax.ShapeDtypeStruct((128, CH), BF),
            jax.ShapeDtypeStruct((128, CH), BF),
            jax.ShapeDtypeStruct((CH, BLK), F32),
            jax.ShapeDtypeStruct((CH, BLK), F32),
        ),
        in_specs=[sm, sm, vm, vm, anyw, anyw],
        out_specs=(vm, vm, vm, vm),
        scratch_shapes=[
            pltpu.VMEM((16 * CH, BLK), BF),
            pltpu.VMEM((16 * CH, BLK), BF),
            pltpu.VMEM((DB + 1, BLK, BLK), BF),
            pltpu.VMEM((DB + 1, BLK, BLK), BF),
            pltpu.VMEM((NB, BLK, BLK), BF),
            pltpu.VMEM((NB, BLK, BLK), BF),
            pltpu.VMEM((ROWS, 128, BLK), F32),
            pltpu.VMEM((ROWS, 128, BLK), BF),
            pltpu.VMEM((ROWS, 128, BLK), BF),
            pltpu.VMEM((NB + 1, 128, BLK), F32),
            pltpu.VMEM((2, 2, NZ, CH, BLK), BF),
            pltpu.VMEM((2, NZ, CH, BLK), BF),
            pltpu.VMEM((2, 4, CH, BLK), BF),
            pltpu.VMEM((2, 4, CH, BLK), BF),
            pltpu.VMEM((2, 4, 4, CH, BLK), BF),
            pltpu.VMEM((2, 6, 2, CH, BLK), BF),
            pltpu.VMEM((2, 4, CH, BLK), BF),
            pltpu.VMEM((2, 6, CH // 2, BLK), BF),
            dma((2,)),
            dma((16,)), dma((16,)),
            dma((18,)), dma((18,)),
            dma((16,)), dma((16,)),
            dma((16,)), dma((16,)),
            dma((24,)), dma((24,)),
        ],
        compiler_params=pltpu.CompilerParams(
            collective_id=0, has_side_effects=True, vmem_limit_bytes=50 * 1024 * 1024
        ),
        cost_estimate=pl.CostEstimate(flops=1_409_286_144, bytes_accessed=8_000_000, transcendentals=114_688),
    )(pick, tab, inputs, out_grad, w_in.reshape(NB, BLK, BLK), w_out.reshape(NB, BLK, BLK))
    return (out, ing, gwin.reshape(ROWS, SLOTS, 8, BLK), gwout.reshape(ROWS, SLOTS, 8, BLK))


def solution(mesh):
    return jax.shard_map(
        on_device,
        mesh=mesh,
        in_specs=(
            P("dp", "tensor"),
            P("dp", "tensor"),
            P("tensor", None, None, None),
            P("tensor", None, None, None),
            P("tensor", None),
            P("tensor"),
        ),
        out_specs=(
            P("dp", "tensor"),
            P("dp", "tensor"),
            P("tensor", None, "dp", None),
            P("tensor", None, "dp", None),
        ),
        check_vma=False,
    )
```

```python
import jax
import jax.numpy as jnp
from jax import lax
from jax.experimental import pallas as pl
from jax.experimental.pallas import tpu as pltpu
from jax.sharding import PartitionSpec as P

BLK = 128
SLOTS = 8
ROWS = 7
NB = ROWS * SLOTS
DB = 56
NZ = 8
NQ = 4
CH = 448
U = 7
SPAN = ((0, 4), (4, 3))
BF = jnp.bfloat16
F32 = jnp.float32
MESH = pl.DeviceIdType.MESH
C0 = 0.7978845608028654
C1 = 0.044715
ORDER = (4, 3, -3, 2, -2, 1, -1, 0)
NT = (((1,), (1,)), ((), ()))


def cat(parts, axis):
    return jnp.concatenate(parts, axis=axis)


def dot(a, b):
    return jnp.dot(a, b, preferred_element_type=F32)


def kernel(
    col_ref, cnt_ref, x_hbm, g_hbm, win_hbm, wout_hbm,
    out_ref, ing_ref, gwin_ref, gwout_ref,
    xg, gg, win, wout, wint, woutt, dgelu, hid, gpre, cbuf, part, sib, rp, rm,
    wgt, wpa, wpb, red, w2a, w2b, tabv, tab,
    lsem, ag_s, ag_r, sb_s, sb_r, ss_s, ss_r, zs, zr, xs, xr,
):
    dp = lax.axis_index("dp")
    tn = lax.axis_index("tensor")
    yy, xx = dp // NQ, dp % NQ
    z, core = tn // 2, tn % 2

    def zdev(step):
        return {"dp": dp, "tensor": ((z + step + NZ) % NZ) * 2 + core}

    sdev = {"dp": dp, "tensor": z * 2 + (1 - core)}

    def ydev(step):
        return {"dp": ((yy + step + NQ) % NQ) * NQ + xx, "tensor": tn}

    def xdev(step):
        return {"dp": yy * NQ + (xx + step + NQ) % NQ, "tensor": tn}

    sends = []

    def rcopy(src, dst, ssem, rsem, dev):
        return pltpu.make_async_remote_copy(
            src_ref=src, dst_ref=dst, send_sem=ssem, recv_sem=rsem,
            device_id=dev, device_id_type=MESH,
        )

    def go(copy):
        copy.start()
        sends.append(copy)

    barrier = pltpu.get_barrier_semaphore()
    for dev in (sdev, zdev(1), zdev(-1), xdev(1), xdev(-1), ydev(1), ydev(-1)):
        pl.semaphore_signal(barrier, inc=1, device_id=dev, device_id_type=MESH)

    fields = (xg, gg)
    own = pl.ds(tn * U, U)
    local = [
        pltpu.make_async_copy(x_hbm, xg.at[own], lsem.at[0]),
        pltpu.make_async_copy(g_hbm, gg.at[own], lsem.at[1]),
        pltpu.make_async_copy(win_hbm, win, lsem.at[2]),
        pltpu.make_async_copy(wout_hbm, wout, lsem.at[3]),
    ]
    for c in local:
        c.start()

    def live_col(n, s):
        return jnp.where(s < cnt_ref[n], col_ref[n, s], DB)

    sub = lax.broadcasted_iota(jnp.int32, (8, 128), 0)
    lan = lax.broadcasted_iota(jnp.int32, (8, 128), 1)
    table = jnp.full((8, 128), NB, jnp.int32)
    for n in range(ROWS):
        for s in range(SLOTS):
            table = jnp.where((sub == n) & (lan == live_col(n, s)), n * SLOTS + s, table)
    table = jnp.where(lan < DB, table, NB)
    tabv[...] = table
    tcopy = pltpu.make_async_copy(tabv, tab, lsem.at[4])
    tcopy.start()
    xg[2 * DB] = jnp.zeros((64, BLK), BF)
    xg[2 * DB + 1] = jnp.zeros((64, BLK), BF)
    gg[2 * DB] = jnp.zeros((64, BLK), BF)
    gg[2 * DB + 1] = jnp.zeros((64, BLK), BF)
    cbuf[NB] = jnp.zeros((BLK, BLK), F32)

    def piece(ref, t, lo=0, n=U):
        return ref.at[pl.ds(t * U + lo, n)]

    def wrap(step):
        return (z + step + 2 * NZ) % NZ

    def ag_copy(a, way, k, h):
        step = -(k + 1) if way == 0 else k + 1
        v = piece(fields[a], wrap(step) * 2 + core, *SPAN[h])
        i = ((a * 2 + way) * 4 + k) * 2 + h
        return rcopy(v, v, ag_s.at[i], ag_r.at[i], zdev(1 if way == 0 else -1))

    def ag_send(a, way, k, h):
        step = -k if way == 0 else k
        v = piece(fields[a], wrap(step) * 2 + core, *SPAN[h])
        i = ((a * 2 + way) * 4 + k) * 2 + h
        return rcopy(v, v, ag_s.at[i], ag_r.at[i], zdev(1 if way == 0 else -1))

    def sb_place(j):
        if j == 0:
            return 0, (0, U)
        if j < 7:
            way, k = (j - 1) // 3, (j - 1) % 3
            return (-(k + 1) if way == 0 else k + 1), (0, U)
        return 4, SPAN[j - 7]

    def sb_copy(a, j, mine):
        step, span = sb_place(j)
        v = piece(fields[a], wrap(step) * 2 + (core if mine else 1 - core), *span)
        return rcopy(v, v, sb_s.at[a * 9 + j], sb_r.at[a * 9 + j], sdev)

    def ag_start(a):
        for h in range(2):
            for way in range(2):
                go(ag_send(a, way, 0, h))
        go(sb_copy(a, 0, True))

    def ag_event(a, k, h):
        for way in range(2):
            if k == 3 and h != way:
                continue
            ag_copy(a, way, k, h).wait_recv()
            if k < 2 or (k == 2 and h == way):
                go(ag_send(a, way, k + 1, h))
        if k < 3 and h == 1:
            go(sb_copy(a, 1 + k, True))
            go(sb_copy(a, 4 + k, True))
        if k == 3:
            go(sb_copy(a, 7 + h, True))

    def gathered(a):
        for j in range(9):
            sb_copy(a, j, False).wait_recv()

    def turn(lo, hi):
        def body(n, carry):
            for s in range(SLOTS):
                i = n * SLOTS + s
                wint[n, :, s * BLK:(s + 1) * BLK] = win[i].T
                woutt[i] = wout[i].T
            return carry

        lax.fori_loop(lo, hi, body, 0)

    def listed(ref, n):
        parts = []
        for s in range(SLOTS):
            i = live_col(n, s) * 2
            parts += [ref[i], ref[i + 1]]
        return cat(parts, 0)

    def tall(ref, n):
        return ref[pl.ds(n * SLOTS, SLOTS)].reshape(SLOTS * BLK, BLK)

    def keep(n, prod):
        cbuf[pl.ds(n * SLOTS, SLOTS)] = prod.reshape(SLOTS, BLK, BLK)

    def forward(lo, hi):
        def body(n, carry):
            pre = dot(wint[n], listed(xg, n))
            sq = pre * pre
            th = jnp.tanh(C0 * pre * (1.0 + C1 * sq))
            half = 0.5 * (1.0 + th)
            dgelu[n] = half + 0.5 * pre * (1.0 - th * th) * (C0 * (1.0 + 3.0 * C1 * sq))
            h = (pre * half).astype(BF)
            hid[n] = h
            keep(n, dot(tall(woutt, n), h))
            return carry

        lax.fori_loop(lo, hi, body, 0)

    def half_of(ref, c):
        return ref.at[pl.ds(pl.multiple_of(c * CH, 64), CH)]

    def sib_copy(a, zz):
        i = a * NZ + zz
        return rcopy(half_of(part.at[a, zz], 1 - core), sib.at[a, zz], ss_s.at[i], ss_r.at[i], sdev)

    def place(a, steps):
        for step in steps:
            zz = wrap(step)
            for k in range(7):
                acc = cbuf[tab[0, zz * 7 + k]]
                for n in range(1, ROWS):
                    acc = acc + cbuf[tab[n, zz * 7 + k]]
                part[a, zz, 128 * k:128 * k + 128, :] = acc.astype(BF)
            go(sib_copy(a, zz))

    def chip_sum(a, step):
        zz = wrap(step)
        sib_copy(a, zz).wait_recv()
        return zz, half_of(part.at[a, zz], core)[...].astype(F32) + sib[a, zz].astype(F32)

    def z_copy(src, a, way, r):
        i = (a * 2 + way) * 4 + r
        dst = (rp if way == 0 else rm).at[a, r]
        return rcopy(src, dst, zs.at[i], zr.at[i], zdev(1 if way == 0 else -1))

    def z_first(a, way):
        r = 3 if a == way else 2
        zz, total = chip_sum(a, r + 1 if way == 0 else -(r + 1))
        src = half_of(part.at[a, zz], core)
        src[...] = total.astype(BF)
        go(z_copy(src, a, way, r))

    def z_next(a, way, r):
        buf = rp if way == 0 else rm
        z_copy(buf.at[a, r], a, way, r).wait_recv()
        zz, total = chip_sum(a, r if way == 0 else -r)
        buf[a, r] = (buf[a, r].astype(F32) + total).astype(BF)
        go(z_copy(buf.at[a, r], a, way, r - 1))

    def z_last(a, dst):
        zz, total = chip_sum(a, 0)
        for way in range(2):
            buf = rp if way == 0 else rm
            z_copy(buf.at[a, 0], a, way, 0).wait_recv()
            total = total + buf[a, 0].astype(F32)
        dst[...] = total.astype(BF)

    coords = ((yy, xx), (xx, yy))
    devs = ((ydev, xdev), (xdev, ydev))
    bufs = ((wpa, w2a), (wpb, w2b))

    def at4(i):
        return (i + 2 * NQ) % NQ

    def lines(h):
        return pl.ds(SPAN[h][0] * 64, SPAN[h][1] * 64)

    def w_copy(src, a, ph, h, m):
        sign = 1 if h == 0 else -1
        i = ((a * 2 + ph) * 2 + h) * 3 + m
        return rcopy(
            src, bufs[h][ph].at[a, m], xs.at[i], xr.at[i], devs[a][ph](sign if m < 2 else -sign)
        )

    def w_src(a, ph, h, step):
        c = at4(coords[a][ph] + step * (1 if h == 0 else -1))
        if ph == 0:
            return wgt.at[a, c, :, lines(h)]
        return red.at[a, c, lines(h)]

    def w_start(a, ph, h):
        go(w_copy(w_src(a, ph, h, 2), a, ph, h, 0))
        go(w_copy(w_src(a, ph, h, -1), a, ph, h, 2))

    def w_pass(a, ph, h):
        buf = bufs[h][ph]
        w_copy(buf.at[a, 0], a, ph, h, 0).wait_recv()
        mine = w_src(a, ph, h, 1)
        if ph == 0:
            for q in range(NQ):
                buf[a, 0, q] = (buf[a, 0, q].astype(F32) + mine[q].astype(F32)).astype(BF)
        else:
            buf[a, 0] = (buf[a, 0].astype(F32) + mine[...].astype(F32)).astype(BF)
        go(w_copy(buf.at[a, 0], a, ph, h, 1))

    def w_done(a, ph, h, dst):
        buf = bufs[h][ph]
        for m in (2, 1):
            w_copy(buf.at[a, m], a, ph, h, m).wait_recv()
        mine = w_src(a, ph, h, 0)
        if ph == 0:
            for q in range(NQ):
                total = mine[q].astype(F32) + buf[a, 1, q].astype(F32) + buf[a, 2, q].astype(F32)
                red[a, q, lines(h)] = total.astype(BF)
        else:
            dst[lines(h), :] = mine[...].astype(F32) + buf[a, 1].astype(F32) + buf[a, 2].astype(F32)

    def backward_out(lo, hi):
        def body(n, carry):
            picked = listed(gg, n)
            gh = dot(cat([wout[n * SLOTS + s] for s in range(SLOTS)], 1), picked)
            gpre[n] = (gh * dgelu[n]).astype(BF)
            gw = lax.dot_general(hid[n], picked, NT, preferred_element_type=F32)
            for s in range(0, SLOTS, 2):
                one = gw[:, s * BLK:(s + 1) * BLK].reshape(16, 8, BLK)
                two = gw[:, (s + 1) * BLK:(s + 2) * BLK].reshape(16, 8, BLK)
                row = pl.multiple_of((n * SLOTS + s) * 8, 16)
                wgt[0, :, :, pl.ds(row, 16), :] = cat([one, two], 1).astype(BF).reshape(4, 4, 16, BLK)
            return carry

        lax.fori_loop(lo, hi, body, 0)

    def backward_in(lo, hi):
        def body(n, carry):
            gw = lax.dot_general(listed(xg, n), gpre[n], NT, preferred_element_type=F32)
            gw = gw.reshape(SLOTS, 16, 8, BLK)
            for s in range(0, SLOTS, 2):
                both = cat([gw[s], gw[s + 1]], 1).astype(BF).reshape(4, 4, 16, BLK)
                row = pl.multiple_of((n * SLOTS + s) * 8, 16)
                for p in range(4):
                    for q in range(4):
                        wgt[1, p, q, pl.ds(row, 16), :] = both[q, p]
            return carry

        lax.fori_loop(lo, hi, body, 0)

    def backward_x(lo, hi):
        def body(n, carry):
            keep(n, dot(tall(win, n), gpre[n]))
            return carry

        lax.fori_loop(lo, hi, body, 0)

    local[0].wait()
    local[1].wait()
    pl.semaphore_wait(barrier, 7)
    ag_start(0)
    local[2].wait()
    local[3].wait()
    tcopy.wait()
    turn(0, 2)
    ag_event(0, 0, 0)
    turn(2, 3)
    ag_event(0, 0, 1)
    turn(3, 4)
    ag_event(0, 1, 0)
    turn(4, 5)
    ag_event(0, 1, 1)
    turn(5, 6)
    ag_event(0, 2, 0)
    turn(6, 7)
    ag_event(0, 2, 1)
    ag_start(1)
    ag_event(0, 3, 0)
    ag_event(0, 3, 1)
    gathered(0)
    forward(0, 3)
    ag_event(1, 0, 0)
    ag_event(1, 0, 1)
    forward(3, 5)
    ag_event(1, 1, 0)
    ag_event(1, 1, 1)
    forward(5, 7)
    place(0, ORDER[:3])
    ag_event(1, 2, 0)
    ag_event(1, 2, 1)
    place(0, ORDER[3:])
    ag_event(1, 3, 0)
    ag_event(1, 3, 1)
    z_first(0, 0)
    z_first(0, 1)
    gathered(1)
    backward_out(0, 4)
    w_start(0, 0, 0)
    backward_out(4, 7)
    w_start(0, 0, 1)
    z_next(0, 0, 3)
    z_next(0, 1, 2)
    backward_in(0, 4)
    w_start(1, 0, 0)
    backward_in(4, 7)
    w_start(1, 0, 1)
    backward_x(0, 7)
    w_pass(0, 0, 0)
    w_pass(0, 0, 1)
    z_next(0, 0, 2)
    z_next(0, 1, 1)
    place(1, ORDER)
    z_first(1, 1)
    z_first(1, 0)
    w_pass(1, 0, 0)
    w_pass(1, 0, 1)
    z_next(0, 0, 1)
    z_next(1, 1, 3)
    z_next(1, 0, 2)
    z_last(0, out_ref)
    w_done(0, 0, 0, None)
    w_start(0, 1, 0)
    w_done(0, 0, 1, None)
    w_start(0, 1, 1)
    z_next(1, 1, 2)
    z_next(1, 0, 1)
    w_done(1, 0, 0, None)
    w_start(1, 1, 0)
    w_done(1, 0, 1, None)
    w_start(1, 1, 1)
    w_pass(0, 1, 0)
    w_pass(0, 1, 1)
    z_next(1, 1, 1)
    w_pass(1, 1, 0)
    w_pass(1, 1, 1)
    z_last(1, ing_ref)
    for a, dst in ((0, gwout_ref), (1, gwin_ref)):
        for h in range(2):
            w_done(a, 1, h, dst)
    for c in sends:
        c.wait_send()


def copy_out(*refs):
    copies = [pltpu.make_async_copy(refs[i], refs[4 + i], refs[8].at[i]) for i in range(4)]
    for c in copies:
        c.start()
    for c in copies:
        c.wait()


def on_device(inputs, out_grad, w_in, w_out, columns, counts):
    vm = pl.BlockSpec(memory_space=pltpu.VMEM)
    sm = pl.BlockSpec(memory_space=pltpu.SMEM)
    hbm = pl.BlockSpec(memory_space=pltpu.HBM)
    anyw = pl.BlockSpec(memory_space=pl.ANY)
    dma = pltpu.SemaphoreType.DMA
    shapes = (
        jax.ShapeDtypeStruct((CH, BLK), BF),
        jax.ShapeDtypeStruct((CH, BLK), BF),
        jax.ShapeDtypeStruct((CH, BLK), F32),
        jax.ShapeDtypeStruct((CH, BLK), F32),
    )
    res = pl.pallas_call(
        kernel,
        out_shape=shapes,
        in_specs=[sm, sm, hbm, hbm, hbm, hbm],
        out_specs=(vm, vm, vm, vm),
        scratch_shapes=[
            pltpu.VMEM((2 * DB + 2, 64, BLK), BF),
            pltpu.VMEM((2 * DB + 2, 64, BLK), BF),
            pltpu.VMEM((NB, BLK, BLK), BF),
            pltpu.VMEM((NB, BLK, BLK), BF),
            pltpu.VMEM((ROWS, BLK, SLOTS * BLK), BF),
            pltpu.VMEM((NB, BLK, BLK), BF),
            pltpu.VMEM((ROWS, BLK, 128), F32),
            pltpu.VMEM((ROWS, BLK, 128), BF),
            pltpu.VMEM((ROWS, BLK, 128), BF),
            pltpu.VMEM((NB + 1, BLK, 128), F32),
            pltpu.VMEM((2, NZ, 2 * CH, BLK), BF),
            pltpu.VMEM((2, NZ, CH, BLK), BF),
            pltpu.VMEM((2, 4, CH, BLK), BF),
            pltpu.VMEM((2, 4, CH, BLK), BF),
            pltpu.VMEM((2, 4, 4, CH, BLK), BF),
            pltpu.VMEM((2, 3, 4, 256, BLK), BF),
            pltpu.VMEM((2, 3, 4, 192, BLK), BF),
            pltpu.VMEM((2, 4, CH, BLK), BF),
            pltpu.VMEM((2, 3, 256, BLK), BF),
            pltpu.VMEM((2, 3, 192, BLK), BF),
            pltpu.VMEM((8, 128), jnp.int32),
            pltpu.SMEM((8, 128), jnp.int32),
            dma((5,)),
            dma((32,)), dma((32,)),
            dma((18,)), dma((18,)),
            dma((16,)), dma((16,)),
            dma((16,)), dma((16,)),
            dma((24,)), dma((24,)),
        ],
        compiler_params=pltpu.CompilerParams(
            collective_id=0, has_side_effects=True, vmem_limit_bytes=52 * 1024 * 1024
        ),
        cost_estimate=pl.CostEstimate(flops=1_409_286_144, bytes_accessed=8_000_000, transcendentals=114_688),
    )(
        columns, counts,
        inputs.T.reshape(U, 64, BLK), out_grad.T.reshape(U, 64, BLK),
        w_in.reshape(NB, BLK, BLK), w_out.reshape(NB, BLK, BLK),
    )
    out, ing, gwin, gwout = pl.pallas_call(
        copy_out,
        out_shape=shapes,
        in_specs=[anyw] * 4,
        out_specs=(anyw,) * 4,
        scratch_shapes=[dma((4,))],
        cost_estimate=pl.CostEstimate(flops=0, bytes_accessed=1_400_000, transcendentals=0),
    )(*res)
    return (out.T, ing.T, gwin.reshape(ROWS, SLOTS, 8, BLK), gwout.reshape(ROWS, SLOTS, 8, BLK))


def solution(mesh):
    return jax.shard_map(
        on_device,
        mesh=mesh,
        in_specs=(
            P("dp", "tensor"),
            P("dp", "tensor"),
            P("tensor", None, None, None),
            P("tensor", None, None, None),
            P("tensor", None),
            P("tensor"),
        ),
        out_specs=(
            P("dp", "tensor"),
            P("dp", "tensor"),
            P("tensor", None, "dp", None),
            P("tensor", None, "dp", None),
        ),
        check_vma=False,
    )
```

```python
import jax
import jax.numpy as jnp
from jax import lax
from jax.experimental import pallas as pl
from jax.experimental.pallas import tpu as pltpu
from jax.sharding import PartitionSpec as P

BLK = 128
SLOTS = 8
ROWS = 7
NB = ROWS * SLOTS
DB = 56
NZ = 8
NQ = 4
CH = 448
U = 7
SPAN = ((0, 4), (4, 3))
H = 224
W = 112
BF = jnp.bfloat16
F32 = jnp.float32
MESH = pl.DeviceIdType.MESH
C0 = 0.7978845608028654
C1 = 0.044715
ORDER = (4, 3, -3, 2, -2, 1, -1, 0)
NT = (((1,), (1,)), ((), ()))


def cat(parts, axis):
    return jnp.concatenate(parts, axis=axis)


def dot(a, b):
    return jnp.dot(a, b, preferred_element_type=F32)


def kernel(
    col_ref, cnt_ref, x_hbm, g_hbm, win_hbm, wout_hbm,
    out_ref, ing_ref, gwin_ref, gwout_ref,
    xg, gg, win, wout, wint, woutt, dgelu, hid, gpre, cbuf, run, part, sib, zb,
    wgt, wp, red, w2, tabv, tab,
    lsem, ag_s, ag_r, sb_s, sb_r, ss_s, ss_r, zs, zr, xs, xr,
):
    dp = lax.axis_index("dp")
    tn = lax.axis_index("tensor")
    yy, xx = dp // NQ, dp % NQ
    z, core = tn // 2, tn % 2

    def zdev(step):
        return {"dp": dp, "tensor": ((z + step + NZ) % NZ) * 2 + core}

    sdev = {"dp": dp, "tensor": z * 2 + (1 - core)}

    def ydev(step):
        return {"dp": ((yy + step + NQ) % NQ) * NQ + xx, "tensor": tn}

    def xdev(step):
        return {"dp": yy * NQ + (xx + step + NQ) % NQ, "tensor": tn}

    sends = []

    def rcopy(src, dst, ssem, rsem, dev):
        return pltpu.make_async_remote_copy(
            src_ref=src, dst_ref=dst, send_sem=ssem, recv_sem=rsem,
            device_id=dev, device_id_type=MESH,
        )

    def go(copy):
        copy.start()
        sends.append(copy)

    barrier = pltpu.get_barrier_semaphore()
    for dev in (sdev, zdev(1), zdev(-1), xdev(1), xdev(-1), ydev(1), ydev(-1)):
        pl.semaphore_signal(barrier, inc=1, device_id=dev, device_id_type=MESH)

    fields = (xg, gg)
    own = pl.ds(tn * U, U)
    local = [
        pltpu.make_async_copy(x_hbm, xg.at[own], lsem.at[0]),
        pltpu.make_async_copy(g_hbm, gg.at[own], lsem.at[1]),
        pltpu.make_async_copy(win_hbm, win, lsem.at[2]),
        pltpu.make_async_copy(wout_hbm, wout, lsem.at[3]),
    ]
    for c in local:
        c.start()

    def live_col(n, s):
        return jnp.where(s < cnt_ref[n], col_ref[n, s], DB)

    def make_table():
        sub = lax.broadcasted_iota(jnp.int32, (8, 128), 0)
        lan = lax.broadcasted_iota(jnp.int32, (8, 128), 1)
        down = []
        across = jnp.full((8, 128), 1000, jnp.int32)
        for n in range(ROWS):
            v = jnp.zeros((8, 128), jnp.int32)
            for s in range(SLOTS):
                c = live_col(n, s)
                v = jnp.where(sub == s, c, v)
                across = jnp.where(lan == n * SLOTS + s, c, across)
            down.append(v)
        across = across * 64 + lan

        def add_rows(parts):
            t = parts[0]
            for v in parts[1:]:
                t = t + v
            for sh in (4, 2, 1):
                t = t + pltpu.roll(t, sh, 0)
            return t

        def count(v):
            return jnp.where(v, 1, 0)

        spots = [jnp.full((8, 128), n * SLOTS, jnp.int32) + sub for n in range(ROWS)]
        ranks = []
        for n in range(ROWS):
            t = count(across < down[n] * 64 + spots[n])
            for sh in (64, 32, 16, 8, 4, 2, 1):
                t = t + pltpu.roll(t, sh, 1)
            ranks.append(t)
        perm = add_rows([jnp.where(ranks[n] == lan, spots[n], 0) for n in range(ROWS)])
        cols = add_rows([jnp.where(ranks[n] == lan, down[n], 0) for n in range(ROWS)])
        same = count((cols == pltpu.roll(cols, 1, 1)) & (lan > 0))
        upto = add_rows([count(down[n] <= lan) for n in range(ROWS)])
        here = add_rows([count(down[n] == lan) for n in range(ROWS)])
        last = jnp.where(here > 0, upto - 1, NB)
        tabv[...] = jnp.where(sub == 0, perm, jnp.where(sub == 1, same, last))

    for ref in fields:
        ref[2 * DB] = jnp.zeros((64, BLK), BF)
        ref[2 * DB + 1] = jnp.zeros((64, BLK), BF)
    run[NB] = jnp.zeros((BLK, BLK), BF)

    def piece(ref, t, lo=0, n=U):
        return ref.at[pl.ds(t * U + lo, n)]

    def wrap(step):
        return (z + step + 2 * NZ) % NZ

    def ag_copy(a, way, k, h):
        step = -(k + 1) if way == 0 else k + 1
        v = piece(fields[a], wrap(step) * 2 + core, *SPAN[h])
        i = ((a * 2 + way) * 4 + k) * 2 + h
        return rcopy(v, v, ag_s.at[i], ag_r.at[i], zdev(1 if way == 0 else -1))

    def ag_send(a, way, k, h):
        step = -k if way == 0 else k
        v = piece(fields[a], wrap(step) * 2 + core, *SPAN[h])
        i = ((a * 2 + way) * 4 + k) * 2 + h
        return rcopy(v, v, ag_s.at[i], ag_r.at[i], zdev(1 if way == 0 else -1))

    def sb_place(j):
        if j == 0:
            return 0, (0, U)
        if j < 7:
            way, k = (j - 1) // 3, (j - 1) % 3
            return (-(k + 1) if way == 0 else k + 1), (0, U)
        return 4, SPAN[j - 7]

    def sb_copy(a, j, mine):
        step, span = sb_place(j)
        v = piece(fields[a], wrap(step) * 2 + (core if mine else 1 - core), *span)
        return rcopy(v, v, sb_s.at[a * 9 + j], sb_r.at[a * 9 + j], sdev)

    def ag_start(a):
        for h in range(2):
            for way in range(2):
                go(ag_send(a, way, 0, h))
        go(sb_copy(a, 0, True))

    def ag_event(a, k, h):
        for way in range(2):
            if k == 3 and h != way:
                continue
            ag_copy(a, way, k, h).wait_recv()
            if k < 2 or (k == 2 and h == way):
                go(ag_send(a, way, k + 1, h))
        if k < 3 and h == 1:
            go(sb_copy(a, 1 + k, True))
            go(sb_copy(a, 4 + k, True))
        if k == 3:
            go(sb_copy(a, 7 + h, True))

    def gathered(a):
        for j in range(9):
            sb_copy(a, j, False).wait_recv()

    def turn():
        def body(n, carry):
            for s in range(SLOTS):
                i = n * SLOTS + s
                wint[n, :, s * BLK:(s + 1) * BLK] = win[i].T
                woutt[i] = wout[i].T
            return carry

        lax.fori_loop(0, ROWS, body, 0)

    def listed(ref, n):
        parts = []
        for s in range(SLOTS):
            i = live_col(n, s) * 2
            parts += [ref[i], ref[i + 1]]
        return cat(parts, 0)

    def tall(ref, n):
        return ref[n * SLOTS:(n + 1) * SLOTS].reshape(SLOTS * BLK, BLK)

    def hidden(lo, hi):
        for n in range(lo, hi):
            pre = dot(wint[n], listed(xg, n))
            sq = pre * pre
            th = jnp.tanh(C0 * pre * (1.0 + C1 * sq))
            half = 0.5 * (1.0 + th)
            dgelu[n] = half + 0.5 * pre * (1.0 - th * th) * (C0 * (1.0 + 3.0 * C1 * sq))
            hid[n] = (pre * half).astype(BF)

    def shares(w, act):
        for n in range(ROWS):
            cbuf[n * SLOTS:(n + 1) * SLOTS] = dot(tall(w, n), act[n]).reshape(SLOTS, BLK, BLK)

    def sib_copy(a, zz):
        i = a * NZ + zz
        src = part.at[a, zz, pl.ds(pl.multiple_of((1 - core) * CH, 64), CH)]
        return rcopy(src, sib.at[a, zz], ss_s.at[i], ss_r.at[i], sdev)

    def place(a):
        def add(r, acc):
            acc = acc * tab[1, r].astype(F32) + cbuf[tab[0, r]]
            run[r] = acc.astype(BF)
            return acc

        lax.fori_loop(0, NB, add, jnp.zeros((BLK, BLK), F32), unroll=4)
        for step in ORDER:
            zz = wrap(step)
            for k in range(7):
                part[a, zz, BLK * k:BLK * (k + 1), :] = run[tab[2, zz * 7 + k]]
            go(sib_copy(a, zz))

    met = set()

    def chip_sum(a, step, h):
        zz = wrap(step)
        if (a, step % NZ) not in met:
            met.add((a, step % NZ))
            sib_copy(a, zz).wait_recv()
        src = part.at[a, zz, pl.ds(pl.multiple_of(core * CH + h * H, 32), H)]
        return src, src[...].astype(F32) + sib[a, zz, h * H:(h + 1) * H].astype(F32)

    def z_copy(src, a, way, r, h):
        i = ((a * 2 + way) * 4 + r) * 2 + h
        dst = zb.at[a, way, r, pl.ds(h * H, H)]
        return rcopy(src, dst, zs.at[i], zr.at[i], zdev(1 if way == 0 else -1))

    def z_first(a):
        for r in (3, 2):
            for way in range(2):
                h = way if r == 3 else 1 - way
                src, total = chip_sum(a, r + 1 if way == 0 else -(r + 1), h)
                src[...] = total.astype(BF)
                go(z_copy(src, a, way, r, h))

    def z_next(a, r, only=None):
        for h2 in range(2):
            for way in range(2):
                h = way if h2 == 0 else 1 - way
                if r == 3 and h2 == 1:
                    continue
                buf = zb.at[a, way, r, pl.ds(h * H, H)]
                z_copy(buf, a, way, r, h).wait_recv()
                src, total = chip_sum(a, r if way == 0 else -r, h)
                buf[...] = (buf[...].astype(F32) + total).astype(BF)
                go(z_copy(buf, a, way, r - 1, h))

    def z_last(a, dst):
        for h in range(2):
            src, total = chip_sum(a, 0, h)
            for way in range(2):
                buf = zb.at[a, way, 0, pl.ds(h * H, H)]
                z_copy(buf, a, way, 0, h).wait_recv()
                total = total + buf[...].astype(F32)
            dst[h * H:(h + 1) * H, :] = total.astype(BF)

    coords = ((yy, xx), (xx, yy))
    devs = ((ydev, xdev), (xdev, ydev))

    def at4(i):
        return (i + 2 * NQ) % NQ

    def lines(p):
        return pl.ds(p * W, W)

    def w_dst(a, ph, p, m):
        return (wp if ph == 0 else w2).at[a, p, m]

    def w_copy(src, a, ph, p, m):
        sign = 1 if p % 2 == 0 else -1
        i = ((a * 2 + ph) * 4 + p) * 3 + m
        return rcopy(
            src, w_dst(a, ph, p, m), xs.at[i], xr.at[i], devs[p // 2][ph](sign if m < 2 else -sign)
        )

    def w_src(a, ph, p, step):
        c = at4(coords[p // 2][ph] + step * (1 if p % 2 == 0 else -1))
        if ph == 0:
            return wgt.at[a, c, :, lines(p)]
        return red.at[a, c, lines(p)]

    def w_start(a, ph, *ps):
        for p in ps:
            go(w_copy(w_src(a, ph, p, 2), a, ph, p, 0))
        for p in ps:
            go(w_copy(w_src(a, ph, p, -1), a, ph, p, 2))

    def w_pass(a, ph, *ps):
        for p in ps:
            buf = w_dst(a, ph, p, 0)
            w_copy(buf, a, ph, p, 0).wait_recv()
            mine = w_src(a, ph, p, 1)
            buf[...] = (buf[...].astype(F32) + mine[...].astype(F32)).astype(BF)
            go(w_copy(buf, a, ph, p, 1))

    def w_done(a, ph, p, dst):
        total = w_src(a, ph, p, 0)[...].astype(F32)
        for m in (2, 1):
            w_copy(w_dst(a, ph, p, m), a, ph, p, m).wait_recv()
            total = total + w_dst(a, ph, p, m)[...].astype(F32)
        if ph == 0:
            red[a, :, lines(p)] = total.astype(BF)
        else:
            dst[lines(p), :] = total

    def w_turn(a, *ps):
        for p in ps:
            w_done(a, 0, p, None)
            w_start(a, 1, p)

    def store(a, row, both):
        both = both.astype(BF).reshape(NQ, NQ, 16, BLK)
        if row < 2 * W:
            wgt[a, :, :, row:row + 16, :] = both
        else:
            for p in range(NQ):
                for q in range(NQ):
                    wgt[a, p, q, row:row + 16, :] = both[q, p]

    def backward_out(lo, hi):
        for n in range(lo, hi):
            picked = listed(gg, n)
            gh = dot(cat([wout[n * SLOTS + s] for s in range(SLOTS)], 1), picked)
            gpre[n] = (gh * dgelu[n]).astype(BF)
            gw = lax.dot_general(hid[n], picked, NT, preferred_element_type=F32)
            for s in range(0, SLOTS, 2):
                one = gw[:, s * BLK:(s + 1) * BLK].reshape(16, 8, BLK)
                two = gw[:, (s + 1) * BLK:(s + 2) * BLK].reshape(16, 8, BLK)
                store(0, (n * SLOTS + s) * 8, cat([one, two], 1))

    def backward_in(lo, hi):
        for n in range(lo, hi):
            gw = lax.dot_general(listed(xg, n), gpre[n], NT, preferred_element_type=F32)
            gw = gw.reshape(SLOTS, 16, 8, BLK)
            for s in range(0, SLOTS, 2):
                store(1, (n * SLOTS + s) * 8, cat([gw[s], gw[s + 1]], 1))

    local[0].wait()
    local[1].wait()
    pl.semaphore_wait(barrier, 7)
    ag_start(0)
    ag_start(1)
    make_table()
    tcopy = pltpu.make_async_copy(tabv, tab, lsem.at[4])
    tcopy.start()
    local[2].wait()
    local[3].wait()
    turn()
    tcopy.wait()
    for k in range(3):
        for a in range(2):
            ag_event(a, k, 0)
            ag_event(a, k, 1)
    ag_event(0, 3, 0)
    ag_event(0, 3, 1)
    gathered(0)
    hidden(0, 4)
    ag_event(1, 3, 0)
    ag_event(1, 3, 1)
    hidden(4, 7)
    gathered(1)
    backward_out(0, 4)
    w_start(0, 0, 0, 1)
    backward_out(4, 7)
    w_start(0, 0, 2, 3)
    shares(woutt, hid)
    place(0)
    backward_in(0, 4)
    w_start(1, 0, 0, 1)
    backward_in(4, 7)
    w_start(1, 0, 2, 3)
    z_first(0)
    w_pass(0, 0, 0, 1)
    shares(win, gpre)
    place(1)
    w_pass(0, 0, 2, 3)
    z_next(0, 3)
    z_first(1)
    w_pass(1, 0, 0, 1)
    z_next(0, 2)
    z_next(1, 3)
    w_pass(1, 0, 2, 3)
    w_turn(0, 0, 1, 2, 3)
    z_next(1, 2)
    z_next(0, 1)
    w_turn(1, 0, 1, 2, 3)
    w_pass(0, 1, 0, 1, 2, 3)
    z_next(1, 1)
    w_pass(1, 1, 0, 1, 2, 3)
    z_last(0, out_ref)
    for p in range(4):
        w_done(0, 1, p, gwout_ref)
    z_last(1, ing_ref)
    for p in range(4):
        w_done(1, 1, p, gwin_ref)
    for c in sends:
        c.wait_send()


def finish(*refs):
    for i in range(4):
        refs[4 + i][...] = refs[i][...]


def on_device(inputs, out_grad, w_in, w_out, columns, counts):
    vm = pl.BlockSpec(memory_space=pltpu.VMEM)
    sm = pl.BlockSpec(memory_space=pltpu.SMEM)
    hbm = pl.BlockSpec(memory_space=pltpu.HBM)
    dma = pltpu.SemaphoreType.DMA
    shapes = (
        jax.ShapeDtypeStruct((CH, BLK), BF),
        jax.ShapeDtypeStruct((CH, BLK), BF),
        jax.ShapeDtypeStruct((CH, BLK), F32),
        jax.ShapeDtypeStruct((CH, BLK), F32),
    )
    res = pl.pallas_call(
        kernel,
        out_shape=shapes,
        in_specs=[sm, sm, hbm, hbm, hbm, hbm],
        out_specs=(vm, vm, vm, vm),
        scratch_shapes=[
            pltpu.VMEM((2 * DB + 2, 64, BLK), BF),
            pltpu.VMEM((2 * DB + 2, 64, BLK), BF),
            pltpu.VMEM((NB, BLK, BLK), BF),
            pltpu.VMEM((NB, BLK, BLK), BF),
            pltpu.VMEM((ROWS, BLK, SLOTS * BLK), BF),
            pltpu.VMEM((NB, BLK, BLK), BF),
            pltpu.VMEM((ROWS, BLK, 128), F32),
            pltpu.VMEM((ROWS, BLK, 128), BF),
            pltpu.VMEM((ROWS, BLK, 128), BF),
            pltpu.VMEM((NB, BLK, 128), F32),
            pltpu.VMEM((NB + 1, BLK, 128), BF),
            pltpu.VMEM((2, NZ, 2 * CH, BLK), BF),
            pltpu.VMEM((2, NZ, CH, BLK), BF),
            pltpu.VMEM((2, 2, 4, CH, BLK), BF),
            pltpu.VMEM((2, NQ, NQ, CH, BLK), BF),
            pltpu.VMEM((2, 4, 3, NQ, W, BLK), BF),
            pltpu.VMEM((2, NQ, CH, BLK), BF),
            pltpu.VMEM((2, 4, 3, W, BLK), BF),
            pltpu.VMEM((8, 128), jnp.int32),
            pltpu.SMEM((8, 128), jnp.int32),
            dma((5,)),
            dma((32,)), dma((32,)),
            dma((18,)), dma((18,)),
            dma((16,)), dma((16,)),
            dma((32,)), dma((32,)),
            dma((48,)), dma((48,)),
        ],
        compiler_params=pltpu.CompilerParams(
            collective_id=0, has_side_effects=True, vmem_limit_bytes=63 * 1024 * 1024
        ),
        cost_estimate=pl.CostEstimate(flops=1_409_286_144, bytes_accessed=8_000_000, transcendentals=114_688),
    )(
        columns, counts,
        inputs.T.reshape(U, 64, BLK), out_grad.T.reshape(U, 64, BLK),
        w_in.reshape(NB, BLK, BLK), w_out.reshape(NB, BLK, BLK),
    )
    out, ing, gwin, gwout = pl.pallas_call(
        finish,
        out_shape=shapes,
        in_specs=[vm] * 4,
        out_specs=(vm,) * 4,
        compiler_params=pltpu.CompilerParams(vmem_limit_bytes=63 * 1024 * 1024),
        cost_estimate=pl.CostEstimate(flops=0, bytes_accessed=1_400_000, transcendentals=0),
    )(*res)
    return (out.T, ing.T, gwin.reshape(ROWS, SLOTS, 8, BLK), gwout.reshape(ROWS, SLOTS, 8, BLK))


def solution(mesh):
    return jax.shard_map(
        on_device,
        mesh=mesh,
        in_specs=(
            P("dp", "tensor"),
            P("dp", "tensor"),
            P("tensor", None, None, None),
            P("tensor", None, None, None),
            P("tensor", None),
            P("tensor"),
        ),
        out_specs=(
            P("dp", "tensor"),
            P("dp", "tensor"),
            P("tensor", None, "dp", None),
            P("tensor", None, "dp", None),
        ),
        check_vma=False,
    )
```

```python
import jax
import jax.numpy as jnp
from jax import lax
from jax.experimental import pallas as pl
from jax.experimental.pallas import tpu as pltpu
from jax.sharding import PartitionSpec as P

BLK = 128
SLOTS = 8
ROWS = 7
NB = ROWS * SLOTS
DB = 56
NZ = 8
NQ = 4
CH = 448
U = 7
SPAN = ((0, 4), (4, 3))
H = 224
W = 112
BF = jnp.bfloat16
F32 = jnp.float32
MESH = pl.DeviceIdType.MESH
C0 = 0.7978845608028654
C1 = 0.044715
ORDER = (4, 3, -3, 2, -2, 1, -1, 0)
NT = (((1,), (1,)), ((), ()))


def cat(parts, axis):
    return jnp.concatenate(parts, axis=axis)


def dot(a, b):
    return jnp.dot(a, b, preferred_element_type=F32)


def kernel(
    col_hbm, cnt_hbm, x_hbm, g_hbm, win_hbm, wout_hbm,
    out_ref, ing_ref, gwin_ref, gwout_ref,
    xg, gg, win, wout, wint, woutt, dgelu, hid, gpre, cbuf, run, part, sib, zb,
    wgt, wp, red, w2, tabv, tab, col_ref, cnt_ref,
    lsem, ag_s, ag_r, sb_s, sb_r, ss_s, ss_r, zs, zr, xs, xr,
):
    dp = lax.axis_index("dp")
    tn = lax.axis_index("tensor")
    yy, xx = dp // NQ, dp % NQ
    z, core = tn // 2, tn % 2

    def zdev(step):
        return {"dp": dp, "tensor": ((z + step + NZ) % NZ) * 2 + core}

    sdev = {"dp": dp, "tensor": z * 2 + (1 - core)}

    def ydev(step):
        return {"dp": ((yy + step + NQ) % NQ) * NQ + xx, "tensor": tn}

    def xdev(step):
        return {"dp": yy * NQ + (xx + step + NQ) % NQ, "tensor": tn}

    sends = []

    def rcopy(src, dst, ssem, rsem, dev):
        return pltpu.make_async_remote_copy(
            src_ref=src, dst_ref=dst, send_sem=ssem, recv_sem=rsem,
            device_id=dev, device_id_type=MESH,
        )

    def go(copy):
        copy.start()
        sends.append(copy)

    barrier = pltpu.get_barrier_semaphore()
    for dev in (sdev, zdev(1), zdev(-1), xdev(1), xdev(-1), ydev(1), ydev(-1)):
        pl.semaphore_signal(barrier, inc=1, device_id=dev, device_id_type=MESH)

    fields = (xg, gg)
    own = pl.ds(tn * U, U)
    local = [
        pltpu.make_async_copy(x_hbm, xg.at[own], lsem.at[0]),
        pltpu.make_async_copy(g_hbm, gg.at[own], lsem.at[1]),
        pltpu.make_async_copy(win_hbm, win, lsem.at[2]),
        pltpu.make_async_copy(wout_hbm, wout, lsem.at[3]),
        pltpu.make_async_copy(col_hbm, col_ref, lsem.at[5]),
        pltpu.make_async_copy(cnt_hbm, cnt_ref, lsem.at[6]),
    ]
    for c in local:
        c.start()

    def live_col(n, s):
        return jnp.where(s < cnt_ref[n], col_ref[n, s], DB)

    def make_table():
        sub = lax.broadcasted_iota(jnp.int32, (8, 128), 0)
        lan = lax.broadcasted_iota(jnp.int32, (8, 128), 1)
        down = []
        across = jnp.full((8, 128), 1000, jnp.int32)
        for n in range(ROWS):
            v = jnp.zeros((8, 128), jnp.int32)
            for s in range(SLOTS):
                c = live_col(n, s)
                v = jnp.where(sub == s, c, v)
                across = jnp.where(lan == n * SLOTS + s, c, across)
            down.append(v)
        across = across * 64 + lan

        def add_rows(parts):
            t = parts[0]
            for v in parts[1:]:
                t = t + v
            for sh in (4, 2, 1):
                t = t + pltpu.roll(t, sh, 0)
            return t

        def count(v):
            return jnp.where(v, 1, 0)

        spots = [jnp.full((8, 128), n * SLOTS, jnp.int32) + sub for n in range(ROWS)]
        ranks = []
        for n in range(ROWS):
            t = count(across < down[n] * 64 + spots[n])
            for sh in (64, 32, 16, 8, 4, 2, 1):
                t = t + pltpu.roll(t, sh, 1)
            ranks.append(t)
        perm = add_rows([jnp.where(ranks[n] == lan, spots[n], 0) for n in range(ROWS)])
        cols = add_rows([jnp.where(ranks[n] == lan, down[n], 0) for n in range(ROWS)])
        same = count((cols == pltpu.roll(cols, 1, 1)) & (lan > 0))
        upto = add_rows([count(down[n] <= lan) for n in range(ROWS)])
        here = add_rows([count(down[n] == lan) for n in range(ROWS)])
        last = jnp.where(here > 0, upto - 1, NB)
        tabv[...] = jnp.where(sub == 0, perm, jnp.where(sub == 1, same, last))

    for ref in fields:
        ref[2 * DB] = jnp.zeros((64, BLK), BF)
        ref[2 * DB + 1] = jnp.zeros((64, BLK), BF)
    run[NB] = jnp.zeros((BLK, BLK), BF)

    def piece(ref, t, lo=0, n=U):
        return ref.at[pl.ds(t * U + lo, n)]

    def wrap(step):
        return (z + step + 2 * NZ) % NZ

    def ag_copy(a, way, k, h):
        step = -(k + 1) if way == 0 else k + 1
        v = piece(fields[a], wrap(step) * 2 + core, *SPAN[h])
        i = ((a * 2 + way) * 4 + k) * 2 + h
        return rcopy(v, v, ag_s.at[i], ag_r.at[i], zdev(1 if way == 0 else -1))

    def ag_send(a, way, k, h):
        step = -k if way == 0 else k
        v = piece(fields[a], wrap(step) * 2 + core, *SPAN[h])
        i = ((a * 2 + way) * 4 + k) * 2 + h
        return rcopy(v, v, ag_s.at[i], ag_r.at[i], zdev(1 if way == 0 else -1))

    def sb_place(j):
        if j == 0:
            return 0, (0, U)
        if j < 7:
            way, k = (j - 1) // 3, (j - 1) % 3
            return (-(k + 1) if way == 0 else k + 1), (0, U)
        return 4, SPAN[j - 7]

    def sb_copy(a, j, mine):
        step, span = sb_place(j)
        v = piece(fields[a], wrap(step) * 2 + (core if mine else 1 - core), *span)
        return rcopy(v, v, sb_s.at[a * 9 + j], sb_r.at[a * 9 + j], sdev)

    def part_of(way, i):
        return way if i == 0 else 1 - way

    def ag_start(a):
        for i in range(2):
            for way in range(2):
                go(ag_send(a, way, 0, part_of(way, i)))
        go(sb_copy(a, 0, True))

    def ag_pass(a, k, i):
        for way in range(2):
            go(ag_send(a, way, k + 1, part_of(way, i)))

    def ag_take(a, k, i, on=True):
        for way in range(2):
            h = part_of(way, i)
            ag_copy(a, way, k, h).wait_recv()
            if on and (k < 2 or (k == 2 and i == 0)):
                go(ag_send(a, way, k + 1, h))
            if k == 3:
                go(sb_copy(a, 7 + h, True))
        if k < 3 and i == 1:
            go(sb_copy(a, 1 + k, True))
            go(sb_copy(a, 4 + k, True))

    def gathered(a):
        for j in range(9):
            sb_copy(a, j, False).wait_recv()

    def turn():
        def body(n, carry):
            for s in range(SLOTS):
                i = n * SLOTS + s
                wint[n, :, s * BLK:(s + 1) * BLK] = win[i].T
                woutt[i] = wout[i].T
            return carry

        lax.fori_loop(0, ROWS, body, 0)

    def listed(ref, n):
        parts = []
        for s in range(SLOTS):
            i = live_col(n, s) * 2
            parts += [ref[i], ref[i + 1]]
        return cat(parts, 0)

    def tall(ref, n):
        return ref[n * SLOTS:(n + 1) * SLOTS].reshape(SLOTS * BLK, BLK)

    def hidden(lo, hi):
        for n in range(lo, hi):
            pre = dot(wint[n], listed(xg, n))
            sq = pre * pre
            th = jnp.tanh(C0 * pre * (1.0 + C1 * sq))
            half = 0.5 * (1.0 + th)
            dgelu[n] = half + 0.5 * pre * (1.0 - th * th) * (C0 * (1.0 + 3.0 * C1 * sq))
            hid[n] = (pre * half).astype(BF)

    def shares(w, act):
        for n in range(ROWS):
            cbuf[n * SLOTS:(n + 1) * SLOTS] = dot(tall(w, n), act[n]).reshape(SLOTS, BLK, BLK)

    def sib_copy(a, zz):
        i = a * NZ + zz
        src = part.at[a, zz, pl.ds(pl.multiple_of((1 - core) * CH, 64), CH)]
        return rcopy(src, sib.at[a, zz], ss_s.at[i], ss_r.at[i], sdev)

    def place(a):
        def add(r, acc):
            acc = acc * tab[1, r].astype(F32) + cbuf[tab[0, r]]
            run[r] = acc.astype(BF)
            return acc

        lax.fori_loop(0, NB, add, jnp.zeros((BLK, BLK), F32), unroll=4)
        for step in ORDER:
            zz = wrap(step)
            for k in range(7):
                part[a, zz, BLK * k:BLK * (k + 1), :] = run[tab[2, zz * 7 + k]]
            go(sib_copy(a, zz))

    met = set()

    def chip_sum(a, step, h):
        zz = wrap(step)
        if (a, step % NZ) not in met:
            met.add((a, step % NZ))
            sib_copy(a, zz).wait_recv()
        src = part.at[a, zz, pl.ds(pl.multiple_of(core * CH + h * H, 32), H)]
        return src, src[...].astype(F32) + sib[a, zz, h * H:(h + 1) * H].astype(F32)

    def z_copy(src, a, way, r, h):
        i = ((a * 2 + way) * 4 + r) * 2 + h
        dst = zb.at[a, way, r, pl.ds(h * H, H)]
        return rcopy(src, dst, zs.at[i], zr.at[i], zdev(1 if way == 0 else -1))

    def z_first(a):
        for r in (3, 2):
            for way in range(2):
                h = way if r == 3 else 1 - way
                src, total = chip_sum(a, r + 1 if way == 0 else -(r + 1), h)
                src[...] = total.astype(BF)
                go(z_copy(src, a, way, r, h))

    def z_next(a, r, only=None):
        for h2 in range(2):
            for way in range(2):
                h = way if h2 == 0 else 1 - way
                if r == 3 and h2 == 1:
                    continue
                buf = zb.at[a, way, r, pl.ds(h * H, H)]
                z_copy(buf, a, way, r, h).wait_recv()
                src, total = chip_sum(a, r if way == 0 else -r, h)
                buf[...] = (buf[...].astype(F32) + total).astype(BF)
                go(z_copy(buf, a, way, r - 1, h))

    def z_last(a, dst):
        for h in range(2):
            src, total = chip_sum(a, 0, h)
            for way in range(2):
                buf = zb.at[a, way, 0, pl.ds(h * H, H)]
                z_copy(buf, a, way, 0, h).wait_recv()
                total = total + buf[...].astype(F32)
            dst[h * H:(h + 1) * H, :] = total.astype(BF)

    coords = ((yy, xx), (xx, yy))
    devs = ((ydev, xdev), (xdev, ydev))

    def at4(i):
        return (i + 2 * NQ) % NQ

    def lines(p):
        return pl.ds(p * W, W)

    def w_dst(a, ph, p, m):
        return (wp if ph == 0 else w2).at[a, p, m]

    def w_copy(src, a, ph, p, m):
        sign = 1 if p % 2 == 0 else -1
        i = ((a * 2 + ph) * 4 + p) * 3 + m
        return rcopy(
            src, w_dst(a, ph, p, m), xs.at[i], xr.at[i], devs[p // 2][ph](sign if m < 2 else -sign)
        )

    def w_src(a, ph, p, step):
        c = at4(coords[p // 2][ph] + step * (1 if p % 2 == 0 else -1))
        if ph == 0:
            return wgt.at[a, c, :, lines(p)]
        return red.at[a, c, lines(p)]

    def w_start(a, ph, *ps):
        for p in ps:
            go(w_copy(w_src(a, ph, p, 2), a, ph, p, 0))
        for p in ps:
            go(w_copy(w_src(a, ph, p, -1), a, ph, p, 2))

    def w_pass(a, ph, *ps):
        for p in ps:
            buf = w_dst(a, ph, p, 0)
            w_copy(buf, a, ph, p, 0).wait_recv()
            mine = w_src(a, ph, p, 1)
            buf[...] = (buf[...].astype(F32) + mine[...].astype(F32)).astype(BF)
            go(w_copy(buf, a, ph, p, 1))

    def w_done(a, ph, p, dst):
        total = w_src(a, ph, p, 0)[...].astype(F32)
        for m in (2, 1):
            w_copy(w_dst(a, ph, p, m), a, ph, p, m).wait_recv()
            total = total + w_dst(a, ph, p, m)[...].astype(F32)
        if ph == 0:
            red[a, :, lines(p)] = total.astype(BF)
        else:
            dst[lines(p), :] = total

    def w_turn(a, *ps):
        for p in ps:
            w_done(a, 0, p, None)
            w_start(a, 1, p)

    def store(a, row, both):
        both = both.astype(BF).reshape(NQ, NQ, 16, BLK)
        if row < 2 * W:
            wgt[a, :, :, row:row + 16, :] = both
        else:
            for p in range(NQ):
                for q in range(NQ):
                    wgt[a, p, q, row:row + 16, :] = both[q, p]

    def backward_hidden():
        for n in range(ROWS):
            gh = dot(cat([wout[n * SLOTS + s] for s in range(SLOTS)], 1), listed(gg, n))
            gpre[n] = (gh * dgelu[n]).astype(BF)

    def backward_out(lo, hi):
        for n in range(lo, hi):
            gw = lax.dot_general(hid[n], listed(gg, n), NT, preferred_element_type=F32)
            for s in range(0, SLOTS, 2):
                one = gw[:, s * BLK:(s + 1) * BLK].reshape(16, 8, BLK)
                two = gw[:, (s + 1) * BLK:(s + 2) * BLK].reshape(16, 8, BLK)
                store(0, (n * SLOTS + s) * 8, cat([one, two], 1))

    def backward_in(lo, hi):
        for n in range(lo, hi):
            gw = lax.dot_general(listed(xg, n), gpre[n], NT, preferred_element_type=F32)
            gw = gw.reshape(SLOTS, 16, 8, BLK)
            for s in range(0, SLOTS, 2):
                store(1, (n * SLOTS + s) * 8, cat([gw[s], gw[s + 1]], 1))

    waited = [0]

    def drain(upto):
        for c in sends[waited[0]:upto]:
            c.wait_send()
        waited[0] = upto

    local[0].wait()
    local[1].wait()
    pl.semaphore_wait(barrier, 7)
    ag_start(0)
    ag_start(1)
    local[4].wait()
    local[5].wait()
    make_table()
    tcopy = pltpu.make_async_copy(tabv, tab, lsem.at[4])
    tcopy.start()
    local[2].wait()
    local[3].wait()
    turn()
    tcopy.wait()
    for i in range(2):
        ag_take(0, 0, i)
    for i in range(2):
        ag_take(1, 0, i)
    for i in range(2):
        ag_take(0, 1, i)
    ag_take(1, 1, 0)
    ag_take(1, 1, 1, on=False)
    ag_take(0, 2, 0)
    ag_pass(1, 1, 1)
    ag_take(0, 2, 1)
    ag_take(1, 2, 0)
    ag_take(0, 3, 0)
    ag_take(1, 2, 1)
    ag_take(1, 3, 0)
    gather_sends = len(sends)
    gathered(0)
    hidden(0, ROWS)
    gathered(1)
    backward_hidden()
    backward_out(0, 4)
    w_start(0, 0, 0, 1)
    backward_out(4, 7)
    w_start(0, 0, 2, 3)
    shares(woutt, hid)
    place(0)
    shares(win, gpre)
    place(1)
    z_first(0)
    backward_in(0, 4)
    w_start(1, 0, 0, 1)
    z_first(1)
    backward_in(4, 7)
    w_start(1, 0, 2, 3)
    w_pass(0, 0, 0, 1, 2, 3)
    drain(gather_sends)
    z_next(0, 3)
    z_next(1, 3)
    w_pass(1, 0, 0, 1)
    first_sends = len(sends)
    z_next(0, 2)
    w_pass(1, 0, 2, 3)
    z_next(1, 2)
    w_turn(0, 0, 1, 2, 3)
    drain(first_sends)
    z_next(0, 1)
    z_next(1, 1)
    w_turn(1, 0, 1, 2, 3)
    w_pass(0, 1, 0, 1, 2, 3)
    second_sends = len(sends)
    z_last(0, out_ref)
    w_pass(1, 1, 0, 1, 2, 3)
    z_last(1, ing_ref)
    for p in range(4):
        w_done(0, 1, p, gwout_ref)
    drain(second_sends)
    for p in range(4):
        w_done(1, 1, p, gwin_ref)
    drain(len(sends))


def finish(*refs):
    for i in range(4):
        refs[4 + i][...] = refs[i][...]


def on_device(inputs, out_grad, w_in, w_out, columns, counts):
    vm = pl.BlockSpec(memory_space=pltpu.VMEM)
    hbm = pl.BlockSpec(memory_space=pltpu.HBM)
    dma = pltpu.SemaphoreType.DMA
    shapes = (
        jax.ShapeDtypeStruct((CH, BLK), BF),
        jax.ShapeDtypeStruct((CH, BLK), BF),
        jax.ShapeDtypeStruct((CH, BLK), F32),
        jax.ShapeDtypeStruct((CH, BLK), F32),
    )
    res = pl.pallas_call(
        kernel,
        out_shape=shapes,
        in_specs=[hbm] * 6,
        out_specs=(vm, vm, vm, vm),
        scratch_shapes=[
            pltpu.VMEM((2 * DB + 2, 64, BLK), BF),
            pltpu.VMEM((2 * DB + 2, 64, BLK), BF),
            pltpu.VMEM((NB, BLK, BLK), BF),
            pltpu.VMEM((NB, BLK, BLK), BF),
            pltpu.VMEM((ROWS, BLK, SLOTS * BLK), BF),
            pltpu.VMEM((NB, BLK, BLK), BF),
            pltpu.VMEM((ROWS, BLK, 128), F32),
            pltpu.VMEM((ROWS, BLK, 128), BF),
            pltpu.VMEM((ROWS, BLK, 128), BF),
            pltpu.VMEM((NB, BLK, 128), F32),
            pltpu.VMEM((NB + 1, BLK, 128), BF),
            pltpu.VMEM((2, NZ, 2 * CH, BLK), BF),
            pltpu.VMEM((2, NZ, CH, BLK), BF),
            pltpu.VMEM((2, 2, 4, CH, BLK), BF),
            pltpu.VMEM((2, NQ, NQ, CH, BLK), BF),
            pltpu.VMEM((2, 4, 3, NQ, W, BLK), BF),
            pltpu.VMEM((2, NQ, CH, BLK), BF),
            pltpu.VMEM((2, 4, 3, W, BLK), BF),
            pltpu.VMEM((8, 128), jnp.int32),
            pltpu.SMEM((8, 128), jnp.int32),
            pltpu.SMEM((ROWS, SLOTS), jnp.int32),
            pltpu.SMEM((ROWS,), jnp.int32),
            dma((7,)),
            dma((32,)), dma((32,)),
            dma((18,)), dma((18,)),
            dma((16,)), dma((16,)),
            dma((32,)), dma((32,)),
            dma((48,)), dma((48,)),
        ],
        compiler_params=pltpu.CompilerParams(
            collective_id=0, has_side_effects=True, vmem_limit_bytes=63 * 1024 * 1024
        ),
        cost_estimate=pl.CostEstimate(flops=1_409_286_144, bytes_accessed=8_000_000, transcendentals=114_688),
    )(
        columns, counts,
        inputs.T.reshape(U, 64, BLK), out_grad.T.reshape(U, 64, BLK),
        w_in.reshape(NB, BLK, BLK), w_out.reshape(NB, BLK, BLK),
    )
    out, ing, gwin, gwout = pl.pallas_call(
        finish,
        out_shape=shapes,
        in_specs=[vm] * 4,
        out_specs=(vm,) * 4,
        compiler_params=pltpu.CompilerParams(vmem_limit_bytes=63 * 1024 * 1024),
        cost_estimate=pl.CostEstimate(flops=0, bytes_accessed=1_400_000, transcendentals=0),
    )(*res)
    return (out.T, ing.T, gwin.reshape(ROWS, SLOTS, 8, BLK), gwout.reshape(ROWS, SLOTS, 8, BLK))


def solution(mesh):
    return jax.shard_map(
        on_device,
        mesh=mesh,
        in_specs=(
            P("dp", "tensor"),
            P("dp", "tensor"),
            P("tensor", None, None, None),
            P("tensor", None, None, None),
            P("tensor", None),
            P("tensor"),
        ),
        out_specs=(
            P("dp", "tensor"),
            P("dp", "tensor"),
            P("tensor", None, "dp", None),
            P("tensor", None, "dp", None),
        ),
        check_vma=False,
    )
```

```python
import jax
import jax.numpy as jnp
from jax import lax
from jax.experimental import pallas as pl
from jax.experimental.pallas import tpu as pltpu
from jax.sharding import PartitionSpec as P

BLK = 128
SLOTS = 8
ROWS = 7
NB = ROWS * SLOTS
DB = 56
NZ = 8
NQ = 4
CH = 448
U = 7
SPAN = ((0, 4), (4, 3))
H = 224
W = 112
GROUPS = ((0, 4), (4, 7))
BF = jnp.bfloat16
F32 = jnp.float32
MESH = pl.DeviceIdType.MESH
C0 = 0.7978845608028654
C1 = 0.044715
ORDER = (4, 3, -3, 2, -2, 1, -1, 0)
NT = (((1,), (1,)), ((), ()))
PLAN = (
    ("ag0", 0, 0), ("own", 0), ("ag0", 0, 1), ("ag0", 1, 0), ("own", 1), ("agw", 0, 0, 0), ("agf", 0, 0, 0),
    ("agw", 0, 0, 1), ("agf", 0, 0, 1), ("agw", 1, 0, 0), ("ag0", 1, 1), ("tabl",), ("agf", 1, 0, 0),
    ("agw", 0, 1, 0), ("agf", 0, 1, 0), ("turn",), ("agw", 0, 1, 1), ("agf", 0, 1, 1), ("ags", 0, 0),
    ("agw", 1, 0, 1), ("ags", 1, 0), ("ags", 0, 1), ("agf", 1, 0, 1), ("agw", 0, 2, 0), ("agf", 0, 2, 0),
    ("agw", 1, 1, 0), ("agw", 0, 2, 1), ("agf", 1, 1, 0), ("agw", 1, 1, 1), ("ags", 1, 1), ("ags", 0, 2),
    ("agf", 1, 1, 1), ("agw", 0, 3, 0), ("ags", 0, 3), ("agw", 1, 2, 0), ("agf", 1, 2, 0), ("gath", 0), ("H", 0, 4),
    ("agw", 1, 2, 1), ("ags", 1, 2), ("H", 4, 7), ("agw", 1, 3, 0), ("ags", 1, 3), ("S", 0), ("tab",), ("P", 0),
    ("gath", 1), ("GO", 0), ("wm", 0, 0, 0, 0), ("GO", 1), ("wm", 0, 0, 1, 0), ("zf", 0, 3), ("wm", 0, 0, 0, 2),
    ("GH",), ("zf", 0, 2), ("GI", 0), ("wm", 1, 0, 0, 2), ("S", 1), ("wm", 1, 0, 0, 0), ("zn", 0, 3, 0), ("P", 1),
    ("zn", 0, 2, 1), ("wm", 0, 0, 1, 2), ("GI", 1), ("wm", 1, 0, 1, 0), ("zf", 1, 3), ("zn", 0, 2, 0), ("zf", 1, 2),
    ("wp", 0, 0, 1), ("wp", 1, 0, 0), ("wp", 0, 0, 0), ("wm", 1, 0, 1, 2), ("zn", 1, 3, 0), ("zn", 0, 1, 0),
    ("wp", 1, 0, 1), ("zn", 1, 2, 1), ("wd", 1, 0, 0), ("wm", 1, 1, 0, 0), ("zn", 1, 2, 0), ("zn", 0, 1, 1),
    ("wd", 0, 0, 0), ("wm", 0, 1, 0, 0), ("wd", 0, 0, 1), ("wm", 0, 1, 1, 0), ("wd", 1, 0, 1), ("wm", 1, 1, 1, 0),
    ("zn", 1, 1, 1), ("wm", 1, 1, 0, 2), ("drain", ("GI", 1)), ("wp", 1, 1, 0), ("wm", 0, 1, 0, 2),
    ("wm", 0, 1, 1, 2), ("zn", 1, 1, 0), ("wp", 0, 1, 0), ("wp", 0, 1, 1), ("wm", 1, 1, 1, 2), ("wp", 1, 1, 1),
    ("drain", ("wd", 1, 0, 0)), ("zl", 0), ("wd", 0, 1, 0), ("drain", ("wp", 1, 1, 0)), ("wd", 1, 1, 0),
    ("wd", 0, 1, 1), ("zl", 1), ("wd", 1, 1, 1),
)


def cat(parts, axis):
    return jnp.concatenate(parts, axis=axis)


def dot(a, b):
    return jnp.dot(a, b, preferred_element_type=F32)


def kernel(
    col_hbm, cnt_hbm, x_hbm, g_hbm, win_hbm, wout_hbm,
    out_ref, ing_ref, gwin_ref, gwout_ref,
    xg, gg, win, wout, wint, woutt, dgelu, hid, gpre, cbuf, run, part, sib, zb,
    wgt, wp, red, w2, tabv, tab, col_ref, cnt_ref,
    lsem, ag_s, ag_r, sb_s, sb_r, ss_s, ss_r, zs, zr, xs, xr,
):
    dp = lax.axis_index("dp")
    tn = lax.axis_index("tensor")
    yy, xx = dp // NQ, dp % NQ
    z, core = tn // 2, tn % 2

    def zdev(step):
        return {"dp": dp, "tensor": ((z + step + NZ) % NZ) * 2 + core}

    sdev = {"dp": dp, "tensor": z * 2 + (1 - core)}

    def ydev(step):
        return {"dp": ((yy + step + NQ) % NQ) * NQ + xx, "tensor": tn}

    def xdev(step):
        return {"dp": yy * NQ + (xx + step + NQ) % NQ, "tensor": tn}

    sends = []

    def rcopy(src, dst, ssem, rsem, dev):
        return pltpu.make_async_remote_copy(
            src_ref=src, dst_ref=dst, send_sem=ssem, recv_sem=rsem,
            device_id=dev, device_id_type=MESH,
        )

    def go(copy):
        copy.start()
        sends.append(copy)

    barrier = pltpu.get_barrier_semaphore()
    for dev in (sdev, zdev(1), zdev(-1), xdev(1), xdev(-1), ydev(1), ydev(-1)):
        pl.semaphore_signal(barrier, inc=1, device_id=dev, device_id_type=MESH)

    fields = (xg, gg)
    own = pl.ds(tn * U, U)
    local = [
        pltpu.make_async_copy(x_hbm, xg.at[own], lsem.at[0]),
        pltpu.make_async_copy(g_hbm, gg.at[own], lsem.at[1]),
        pltpu.make_async_copy(win_hbm, win, lsem.at[2]),
        pltpu.make_async_copy(wout_hbm, wout, lsem.at[3]),
        pltpu.make_async_copy(col_hbm, col_ref, lsem.at[5]),
        pltpu.make_async_copy(cnt_hbm, cnt_ref, lsem.at[6]),
    ]
    for c in local:
        c.start()

    def live_col(n, s):
        return jnp.where(s < cnt_ref[n], col_ref[n, s], DB)

    def make_table():
        sub = lax.broadcasted_iota(jnp.int32, (8, 128), 0)
        lan = lax.broadcasted_iota(jnp.int32, (8, 128), 1)
        down = []
        across = jnp.full((8, 128), 1000, jnp.int32)
        for n in range(ROWS):
            v = jnp.zeros((8, 128), jnp.int32)
            for s in range(SLOTS):
                c = live_col(n, s)
                v = jnp.where(sub == s, c, v)
                across = jnp.where(lan == n * SLOTS + s, c, across)
            down.append(v)
        across = across * 64 + lan

        def add_rows(parts):
            t = parts[0]
            for v in parts[1:]:
                t = t + v
            for sh in (4, 2, 1):
                t = t + pltpu.roll(t, sh, 0)
            return t

        def count(v):
            return jnp.where(v, 1, 0)

        spots = [jnp.full((8, 128), n * SLOTS, jnp.int32) + sub for n in range(ROWS)]
        ranks = []
        for n in range(ROWS):
            t = count(across < down[n] * 64 + spots[n])
            for sh in (64, 32, 16, 8, 4, 2, 1):
                t = t + pltpu.roll(t, sh, 1)
            ranks.append(t)
        perm = add_rows([jnp.where(ranks[n] == lan, spots[n], 0) for n in range(ROWS)])
        cols = add_rows([jnp.where(ranks[n] == lan, down[n], 0) for n in range(ROWS)])
        same = count((cols == pltpu.roll(cols, 1, 1)) & (lan > 0))
        upto = add_rows([count(down[n] <= lan) for n in range(ROWS)])
        here = add_rows([count(down[n] == lan) for n in range(ROWS)])
        last = jnp.where(here > 0, upto - 1, NB)
        tabv[...] = jnp.where(sub == 0, perm, jnp.where(sub == 1, same, last))

    for ref in fields:
        ref[2 * DB] = jnp.zeros((64, BLK), BF)
        ref[2 * DB + 1] = jnp.zeros((64, BLK), BF)
    run[NB] = jnp.zeros((BLK, BLK), BF)

    def piece(ref, t, lo=0, n=U):
        return ref.at[pl.ds(t * U + lo, n)]

    def wrap(step):
        return (z + step + 2 * NZ) % NZ

    def ag_copy(a, way, k, h):
        step = -(k + 1) if way == 0 else k + 1
        v = piece(fields[a], wrap(step) * 2 + core, *SPAN[h])
        i = ((a * 2 + way) * 4 + k) * 2 + h
        return rcopy(v, v, ag_s.at[i], ag_r.at[i], zdev(1 if way == 0 else -1))

    def ag_send(a, way, k, h):
        step = -k if way == 0 else k
        v = piece(fields[a], wrap(step) * 2 + core, *SPAN[h])
        i = ((a * 2 + way) * 4 + k) * 2 + h
        return rcopy(v, v, ag_s.at[i], ag_r.at[i], zdev(1 if way == 0 else -1))

    def sb_place(j):
        if j == 0:
            return 0, (0, U)
        if j < 7:
            way, k = (j - 1) // 3, (j - 1) % 3
            return (-(k + 1) if way == 0 else k + 1), (0, U)
        return 4, SPAN[j - 7]

    def sb_copy(a, j, mine):
        step, span = sb_place(j)
        v = piece(fields[a], wrap(step) * 2 + (core if mine else 1 - core), *span)
        return rcopy(v, v, sb_s.at[a * 9 + j], sb_r.at[a * 9 + j], sdev)

    def part_of(way, i):
        return way if i == 0 else 1 - way

    def ag_first(a, i):
        for way in range(2):
            go(ag_send(a, way, 0, part_of(way, i)))

    def ag_wait(a, k, i):
        for way in range(2):
            ag_copy(a, way, k, part_of(way, i)).wait_recv()

    def ag_pass(a, k, i):
        for way in range(2):
            go(ag_send(a, way, k + 1, part_of(way, i)))

    def ag_own(a):
        go(sb_copy(a, 0, True))

    def ag_sib(a, k):
        for way in range(2):
            go(sb_copy(a, 7 + way if k == 3 else 1 + 3 * way + k, True))

    def gathered(a):
        for j in range(9):
            sb_copy(a, j, False).wait_recv()

    def turn():
        def body(n, carry):
            for s in range(SLOTS):
                i = n * SLOTS + s
                wint[n, :, s * BLK:(s + 1) * BLK] = win[i].T
                woutt[i] = wout[i].T
            return carry

        lax.fori_loop(0, ROWS, body, 0)

    def listed(ref, n):
        parts = []
        for s in range(SLOTS):
            i = live_col(n, s) * 2
            parts += [ref[i], ref[i + 1]]
        return cat(parts, 0)

    def tall(ref, n):
        return ref[n * SLOTS:(n + 1) * SLOTS].reshape(SLOTS * BLK, BLK)

    def hidden(lo, hi):
        for n in range(lo, hi):
            pre = dot(wint[n], listed(xg, n))
            sq = pre * pre
            th = jnp.tanh(C0 * pre * (1.0 + C1 * sq))
            half = 0.5 * (1.0 + th)
            dgelu[n] = half + 0.5 * pre * (1.0 - th * th) * (C0 * (1.0 + 3.0 * C1 * sq))
            hid[n] = (pre * half).astype(BF)

    def shares(a):
        w, act = ((woutt, hid), (win, gpre))[a]
        for n in range(ROWS):
            cbuf[n * SLOTS:(n + 1) * SLOTS] = dot(tall(w, n), act[n]).reshape(SLOTS, BLK, BLK)

    def sib_copy(a, zz):
        i = a * NZ + zz
        src = part.at[a, zz, pl.ds(pl.multiple_of((1 - core) * CH, 64), CH)]
        return rcopy(src, sib.at[a, zz], ss_s.at[i], ss_r.at[i], sdev)

    def place(a):
        def add(r, acc):
            acc = acc * tab[1, r].astype(F32) + cbuf[tab[0, r]]
            run[r] = acc.astype(BF)
            return acc

        lax.fori_loop(0, NB, add, jnp.zeros((BLK, BLK), F32), unroll=4)
        for step in ORDER:
            zz = wrap(step)
            for k in range(7):
                part[a, zz, BLK * k:BLK * (k + 1), :] = run[tab[2, zz * 7 + k]]
            go(sib_copy(a, zz))

    met = set()

    def chip_sum(a, step, h):
        zz = wrap(step)
        if (a, step % NZ) not in met:
            met.add((a, step % NZ))
            sib_copy(a, zz).wait_recv()
        src = part.at[a, zz, pl.ds(pl.multiple_of(core * CH + h * H, 32), H)]
        return src, src[...].astype(F32) + sib[a, zz, h * H:(h + 1) * H].astype(F32)

    def z_copy(src, a, way, r, h):
        i = ((a * 2 + way) * 4 + r) * 2 + h
        dst = zb.at[a, way, r, pl.ds(h * H, H)]
        return rcopy(src, dst, zs.at[i], zr.at[i], zdev(1 if way == 0 else -1))

    def z_first(a, r):
        for way in range(2):
            h = way if r == 3 else 1 - way
            src, total = chip_sum(a, r + 1 if way == 0 else -(r + 1), h)
            src[...] = total.astype(BF)
            go(z_copy(src, a, way, r, h))

    def z_next(a, r, i):
        for way in range(2):
            h = way if i == 0 else 1 - way
            buf = zb.at[a, way, r, pl.ds(h * H, H)]
            z_copy(buf, a, way, r, h).wait_recv()
            src, total = chip_sum(a, r if way == 0 else -r, h)
            buf[...] = (buf[...].astype(F32) + total).astype(BF)
            go(z_copy(buf, a, way, r - 1, h))

    def z_last(a):
        dst = (out_ref, ing_ref)[a]
        for h in range(2):
            src, total = chip_sum(a, 0, h)
            for way in range(2):
                buf = zb.at[a, way, 0, pl.ds(h * H, H)]
                z_copy(buf, a, way, 0, h).wait_recv()
                total = total + buf[...].astype(F32)
            dst[h * H:(h + 1) * H, :] = total.astype(BF)

    coords = ((yy, xx), (xx, yy))
    devs = ((ydev, xdev), (xdev, ydev))

    def at4(i):
        return (i + 2 * NQ) % NQ

    def lines(p, g):
        lo, hi = GROUPS[g]
        return pl.ds(p * W + lo * 16, (hi - lo) * 16)

    def w_dst(a, ph, p, g, m):
        return wp.at[a, m, :, lines(p, g)] if ph == 0 else w2.at[a, m, lines(p, g)]

    def w_copy(src, a, ph, p, g, m):
        sign = 1 if p % 2 == 0 else -1
        i = (((a * 2 + ph) * 2 + g) * 4 + p) * 3 + m
        return rcopy(
            src, w_dst(a, ph, p, g, m), xs.at[i], xr.at[i], devs[p // 2][ph](sign if m < 2 else -sign)
        )

    def w_src(a, ph, p, g, step):
        c = at4(coords[p // 2][ph] + step * (1 if p % 2 == 0 else -1))
        if ph == 0:
            return wgt.at[a, c, :, lines(p, g)]
        return red.at[a, c, lines(p, g)]

    def w_send(a, ph, g, m):
        for p in range(4):
            go(w_copy(w_src(a, ph, p, g, 2 if m == 0 else -1), a, ph, p, g, m))

    def w_pass(a, ph, g):
        for p in range(4):
            buf = w_dst(a, ph, p, g, 0)
            w_copy(buf, a, ph, p, g, 0).wait_recv()
            mine = w_src(a, ph, p, g, 1)
            buf[...] = (buf[...].astype(F32) + mine[...].astype(F32)).astype(BF)
            go(w_copy(buf, a, ph, p, g, 1))

    def w_done(a, ph, g):
        dst = (gwout_ref, gwin_ref)[a]
        lo, hi = GROUPS[g]
        for p in range(4):
            total = w_src(a, ph, p, g, 0)[...].astype(F32)
            for m in (2, 1):
                buf = w_dst(a, ph, p, g, m)
                w_copy(buf, a, ph, p, g, m).wait_recv()
                total = total + buf[...].astype(F32)
            if ph == 0:
                red[a, :, lines(p, g)] = total.astype(BF)
            else:
                for n in range(lo, hi):
                    dst[n * 64 + p * 16:n * 64 + p * 16 + 16, :] = total[(n - lo) * 16:(n - lo) * 16 + 16]

    def store(a, n, p, both):
        both = both.astype(BF).reshape(NQ, NQ, 16, BLK)
        row = p * W + n * 16
        if p < 2:
            wgt[a, :, :, row:row + 16, :] = both
        else:
            for i in range(NQ):
                for j in range(NQ):
                    wgt[a, i, j, row:row + 16, :] = both[j, i]

    def backward_hidden():
        for n in range(ROWS):
            gh = dot(cat([wout[n * SLOTS + s] for s in range(SLOTS)], 1), listed(gg, n))
            gpre[n] = (gh * dgelu[n]).astype(BF)

    def backward_out(g):
        for n in range(*GROUPS[g]):
            gw = lax.dot_general(hid[n], listed(gg, n), NT, preferred_element_type=F32)
            for p in range(4):
                one = gw[:, 2 * p * BLK:(2 * p + 1) * BLK].reshape(16, 8, BLK)
                two = gw[:, (2 * p + 1) * BLK:(2 * p + 2) * BLK].reshape(16, 8, BLK)
                store(0, n, p, cat([one, two], 1))

    def backward_in(g):
        for n in range(*GROUPS[g]):
            gw = lax.dot_general(listed(xg, n), gpre[n], NT, preferred_element_type=F32)
            gw = gw.reshape(SLOTS, 16, 8, BLK)
            for p in range(4):
                store(1, n, p, cat([gw[2 * p], gw[2 * p + 1]], 1))

    waited = [0]

    def drain(upto):
        if isinstance(upto, tuple):
            upto = marks[PLAN.index(upto)]
        for c in sends[waited[0]:upto]:
            c.wait_send()
        waited[0] = upto

    def make():
        local[4].wait()
        local[5].wait()
        make_table()
        tcopy.start()

    def turned():
        local[2].wait()
        local[3].wait()
        turn()

    tcopy = pltpu.make_async_copy(tabv, tab, lsem.at[4])
    tasks = {
        "ag0": ag_first, "agw": ag_wait, "agf": ag_pass, "own": ag_own, "ags": ag_sib, "gath": gathered,
        "tabl": make, "turn": turned, "H": hidden, "GH": backward_hidden, "GO": backward_out,
        "GI": backward_in, "S": shares, "P": place, "zf": z_first, "zn": z_next, "zl": z_last,
        "wm": w_send, "wp": w_pass, "wd": w_done, "tab": tcopy.wait, "drain": drain,
    }
    marks = []
    local[0].wait()
    local[1].wait()
    pl.semaphore_wait(barrier, 7)
    for name, *args in PLAN:
        marks.append(len(sends))
        tasks[name](*args)
    drain(len(sends))


def finish(*refs):
    for i in range(4):
        refs[4 + i][...] = refs[i][...]


def on_device(inputs, out_grad, w_in, w_out, columns, counts):
    vm = pl.BlockSpec(memory_space=pltpu.VMEM)
    hbm = pl.BlockSpec(memory_space=pltpu.HBM)
    dma = pltpu.SemaphoreType.DMA
    shapes = (
        jax.ShapeDtypeStruct((CH, BLK), BF),
        jax.ShapeDtypeStruct((CH, BLK), BF),
        jax.ShapeDtypeStruct((CH, BLK), F32),
        jax.ShapeDtypeStruct((CH, BLK), F32),
    )
    res = pl.pallas_call(
        kernel,
        out_shape=shapes,
        in_specs=[hbm] * 6,
        out_specs=(vm, vm, vm, vm),
        scratch_shapes=[
            pltpu.VMEM((2 * DB + 2, 64, BLK), BF),
            pltpu.VMEM((2 * DB + 2, 64, BLK), BF),
            pltpu.VMEM((NB, BLK, BLK), BF),
            pltpu.VMEM((NB, BLK, BLK), BF),
            pltpu.VMEM((ROWS, BLK, SLOTS * BLK), BF),
            pltpu.VMEM((NB, BLK, BLK), BF),
            pltpu.VMEM((ROWS, BLK, 128), F32),
            pltpu.VMEM((ROWS, BLK, 128), BF),
            pltpu.VMEM((ROWS, BLK, 128), BF),
            pltpu.VMEM((NB, BLK, 128), F32),
            pltpu.VMEM((NB + 1, BLK, 128), BF),
            pltpu.VMEM((2, NZ, 2 * CH, BLK), BF),
            pltpu.VMEM((2, NZ, CH, BLK), BF),
            pltpu.VMEM((2, 2, 4, CH, BLK), BF),
            pltpu.VMEM((2, NQ, NQ, CH, BLK), BF),
            pltpu.VMEM((2, 3, NQ, CH, BLK), BF),
            pltpu.VMEM((2, NQ, CH, BLK), BF),
            pltpu.VMEM((2, 3, CH, BLK), BF),
            pltpu.VMEM((8, 128), jnp.int32),
            pltpu.SMEM((8, 128), jnp.int32),
            pltpu.SMEM((ROWS, SLOTS), jnp.int32),
            pltpu.SMEM((ROWS,), jnp.int32),
            dma((7,)),
            dma((32,)), dma((32,)),
            dma((18,)), dma((18,)),
            dma((16,)), dma((16,)),
            dma((32,)), dma((32,)),
            dma((96,)), dma((96,)),
        ],
        compiler_params=pltpu.CompilerParams(
            collective_id=0, has_side_effects=True, vmem_limit_bytes=63 * 1024 * 1024
        ),
        cost_estimate=pl.CostEstimate(flops=1_409_286_144, bytes_accessed=8_000_000, transcendentals=114_688),
    )(
        columns, counts,
        inputs.T.reshape(U, 64, BLK), out_grad.T.reshape(U, 64, BLK),
        w_in.reshape(NB, BLK, BLK), w_out.reshape(NB, BLK, BLK),
    )
    out, ing, gwin, gwout = pl.pallas_call(
        finish,
        out_shape=shapes,
        in_specs=[vm] * 4,
        out_specs=(vm,) * 4,
        compiler_params=pltpu.CompilerParams(vmem_limit_bytes=63 * 1024 * 1024),
        cost_estimate=pl.CostEstimate(flops=0, bytes_accessed=1_400_000, transcendentals=0),
    )(*res)
    return (out.T, ing.T, gwin.reshape(ROWS, SLOTS, 8, BLK), gwout.reshape(ROWS, SLOTS, 8, BLK))


def solution(mesh):
    return jax.shard_map(
        on_device,
        mesh=mesh,
        in_specs=(
            P("dp", "tensor"),
            P("dp", "tensor"),
            P("tensor", None, None, None),
            P("tensor", None, None, None),
            P("tensor", None),
            P("tensor"),
        ),
        out_specs=(
            P("dp", "tensor"),
            P("dp", "tensor"),
            P("tensor", None, "dp", None),
            P("tensor", None, "dp", None),
        ),
        check_vma=False,
    )
```

```python
import jax
import jax.numpy as jnp
from jax import lax
from jax.experimental import pallas as pl
from jax.experimental.pallas import tpu as pltpu
from jax.sharding import PartitionSpec as P

BLK = 128
SLOTS = 8
ROWS = 7
NB = ROWS * SLOTS
DB = 56
NZ = 8
NQ = 4
CH = 448
U = 7
SPAN = ((0, 4), (4, 3))
H = 224
W = 112
GROUPS = ((0, 4), (4, 7))
BF = jnp.bfloat16
F32 = jnp.float32
MESH = pl.DeviceIdType.MESH
C0 = 0.7978845608028654
C1 = 0.044715
ORDER = (4, 3, -3, 2, -2, 1, -1, 0)
NT = (((1,), (1,)), ((), ()))
PLAN = (
    ("ag0", 0, 0), ("own", 0), ("ag0", 0, 1), ("ag0", 1, 0), ("own", 1), ("agw", 0, 0, 0), ("agf", 0, 0, 0),
    ("agw", 0, 0, 1), ("agf", 0, 0, 1), ("agw", 1, 0, 0), ("ag0", 1, 1), ("tabl",), ("agf", 1, 0, 0),
    ("agw", 0, 1, 0), ("agf", 0, 1, 0), ("turn",), ("agw", 0, 1, 1), ("agf", 0, 1, 1), ("ags", 0, 0),
    ("agw", 1, 0, 1), ("ags", 1, 0), ("ags", 0, 1), ("agf", 1, 0, 1), ("agw", 0, 2, 0), ("agf", 0, 2, 0),
    ("agw", 1, 1, 0), ("agw", 0, 2, 1), ("agf", 1, 1, 0), ("agw", 1, 1, 1), ("ags", 1, 1), ("ags", 0, 2),
    ("agf", 1, 1, 1), ("agw", 0, 3, 0), ("ags", 0, 3), ("agw", 1, 2, 0), ("agf", 1, 2, 0), ("gath", 0), ("H", 0, 4),
    ("agw", 1, 2, 1), ("ags", 1, 2), ("H", 4, 7), ("agw", 1, 3, 0), ("ags", 1, 3), ("S", 0), ("tab",), ("P", 0),
    ("gath", 1), ("GO", 0), ("wm", 0, 0, 0, 0), ("GO", 1), ("wm", 0, 0, 1, 0), ("zf", 0, 3), ("wm", 0, 0, 0, 2),
    ("GH",), ("zf", 0, 2), ("GI", 0), ("wm", 1, 0, 0, 2), ("S", 1), ("wm", 1, 0, 0, 0), ("zn", 0, 3, 0), ("P", 1),
    ("zn", 0, 2, 1), ("wm", 0, 0, 1, 2), ("GI", 1), ("wm", 1, 0, 1, 0), ("zf", 1, 3), ("zn", 0, 2, 0), ("zf", 1, 2),
    ("wp", 0, 0, 1), ("wp", 1, 0, 0), ("wp", 0, 0, 0), ("wm", 1, 0, 1, 2), ("zn", 1, 3, 0), ("zn", 0, 1, 0),
    ("wp", 1, 0, 1), ("zn", 1, 2, 1), ("wd", 1, 0, 0), ("wm", 1, 1, 0, 0), ("zn", 1, 2, 0), ("zn", 0, 1, 1),
    ("wd", 0, 0, 0), ("wm", 0, 1, 0, 0), ("wd", 0, 0, 1), ("wm", 0, 1, 1, 0), ("wd", 1, 0, 1), ("wm", 1, 1, 1, 0),
    ("zn", 1, 1, 1), ("wm", 1, 1, 0, 2), ("drain", ("GI", 1)), ("wp", 1, 1, 0), ("wm", 0, 1, 0, 2),
    ("wm", 0, 1, 1, 2), ("zn", 1, 1, 0), ("wp", 0, 1, 0), ("wp", 0, 1, 1), ("wm", 1, 1, 1, 2), ("wp", 1, 1, 1),
    ("drain", ("wd", 1, 0, 0)), ("zl", 0), ("wd", 0, 1, 0), ("drain", ("wp", 1, 1, 0)), ("wd", 1, 1, 0),
    ("wd", 0, 1, 1), ("zl", 1), ("wd", 1, 1, 1),
)


def cat(parts, axis):
    return jnp.concatenate(parts, axis=axis)


def dot(a, b):
    return jnp.dot(a, b, preferred_element_type=F32)


def kernel(
    col_hbm, cnt_hbm, x_hbm, g_hbm, win_hbm, wout_hbm,
    out_ref, ing_ref, gwin_ref, gwout_ref,
    xg, gg, win, wout, wint, woutt, dgelu, hid, gpre, cbuf, run, part, sib, zb,
    wgt, wp, red, w2, tabv, tab, col_ref, cnt_ref,
    lsem, ag_s, ag_r, sb_s, sb_r, ss_s, ss_r, zs, zr, xs, xr,
):
    dp = lax.axis_index("dp")
    tn = lax.axis_index("tensor")
    yy, xx = dp // NQ, dp % NQ
    z, core = tn // 2, tn % 2

    zat = [z] + [(z + i) % NZ for i in range(1, NZ)]
    yat = [yy] + [(yy + i) % NQ for i in range(1, NQ)]
    xat = [xx] + [(xx + i) % NQ for i in range(1, NQ)]
    other = 1 - core
    chunk = [[zat[i] * 2 + core for i in range(NZ)], [zat[i] * 2 + other for i in range(NZ)]]
    first = [[t * U for t in half] for half in chunk]
    zdevs = {i: {"dp": dp, "tensor": chunk[0][i % NZ]} for i in (1, -1)}
    sdev = {"dp": dp, "tensor": chunk[1][0]}
    ydevs = {i: {"dp": yat[i % NQ] * NQ + xx, "tensor": tn} for i in (1, -1)}
    xdevs = {i: {"dp": yy * NQ + xat[i % NQ], "tensor": tn} for i in (1, -1)}
    zdev, ydev, xdev = zdevs.get, ydevs.get, xdevs.get
    own_row, sib_row = core * CH, other * CH

    sends = []

    def rcopy(src, dst, ssem, rsem, dev):
        return pltpu.make_async_remote_copy(
            src_ref=src, dst_ref=dst, send_sem=ssem, recv_sem=rsem,
            device_id=dev, device_id_type=MESH,
        )

    def go(copy):
        copy.start()
        sends.append(copy)

    barrier = pltpu.get_barrier_semaphore()
    for dev in (sdev, zdev(1), zdev(-1), xdev(1), xdev(-1), ydev(1), ydev(-1)):
        pl.semaphore_signal(barrier, inc=1, device_id=dev, device_id_type=MESH)

    fields = (xg, gg)
    own = pl.ds(first[0][0], U)
    local = [
        pltpu.make_async_copy(x_hbm, xg.at[own], lsem.at[0]),
        pltpu.make_async_copy(g_hbm, gg.at[own], lsem.at[1]),
        pltpu.make_async_copy(win_hbm, win, lsem.at[2]),
        pltpu.make_async_copy(wout_hbm, wout, lsem.at[3]),
        pltpu.make_async_copy(col_hbm, col_ref, lsem.at[5]),
        pltpu.make_async_copy(cnt_hbm, cnt_ref, lsem.at[6]),
    ]
    for c in local:
        c.start()

    def live_col(n, s):
        return jnp.where(s < cnt_ref[n], col_ref[n, s], DB)

    def make_table():
        sub = lax.broadcasted_iota(jnp.int32, (8, 128), 0)
        lan = lax.broadcasted_iota(jnp.int32, (8, 128), 1)
        down = []
        across = jnp.full((8, 128), 1000, jnp.int32)
        for n in range(ROWS):
            v = jnp.zeros((8, 128), jnp.int32)
            for s in range(SLOTS):
                c = live_col(n, s)
                v = jnp.where(sub == s, c, v)
                across = jnp.where(lan == n * SLOTS + s, c, across)
            down.append(v)
        across = across * 64 + lan

        def add_rows(parts):
            t = parts[0]
            for v in parts[1:]:
                t = t + v
            for sh in (4, 2, 1):
                t = t + pltpu.roll(t, sh, 0)
            return t

        def count(v):
            return jnp.where(v, 1, 0)

        spots = [jnp.full((8, 128), n * SLOTS, jnp.int32) + sub for n in range(ROWS)]
        ranks = []
        for n in range(ROWS):
            t = count(across < down[n] * 64 + spots[n])
            for sh in (64, 32, 16, 8, 4, 2, 1):
                t = t + pltpu.roll(t, sh, 1)
            ranks.append(t)
        perm = add_rows([jnp.where(ranks[n] == lan, spots[n], 0) for n in range(ROWS)])
        cols = add_rows([jnp.where(ranks[n] == lan, down[n], 0) for n in range(ROWS)])
        same = count((cols == pltpu.roll(cols, 1, 1)) & (lan > 0))
        upto = add_rows([count(down[n] <= lan) for n in range(ROWS)])
        here = add_rows([count(down[n] == lan) for n in range(ROWS)])
        last = jnp.where(here > 0, upto - 1, NB)
        tabv[...] = jnp.where(sub == 0, perm, jnp.where(sub == 1, same, last))

    for ref in fields:
        ref[2 * DB] = jnp.zeros((64, BLK), BF)
        ref[2 * DB + 1] = jnp.zeros((64, BLK), BF)
    run[NB] = jnp.zeros((BLK, BLK), BF)

    def piece(ref, side, step, lo=0, n=U):
        return ref.at[pl.ds(first[side][step % NZ] + lo, n)]

    def wrap(step):
        return zat[step % NZ]

    def ag_copy(a, way, k, h):
        step = -(k + 1) if way == 0 else k + 1
        v = piece(fields[a], 0, step, *SPAN[h])
        i = ((a * 2 + way) * 4 + k) * 2 + h
        return rcopy(v, v, ag_s.at[i], ag_r.at[i], zdev(1 if way == 0 else -1))

    def ag_send(a, way, k, h):
        step = -k if way == 0 else k
        v = piece(fields[a], 0, step, *SPAN[h])
        i = ((a * 2 + way) * 4 + k) * 2 + h
        return rcopy(v, v, ag_s.at[i], ag_r.at[i], zdev(1 if way == 0 else -1))

    def sb_place(j):
        if j == 0:
            return 0, (0, U)
        if j < 7:
            way, k = (j - 1) // 3, (j - 1) % 3
            return (-(k + 1) if way == 0 else k + 1), (0, U)
        return 4, SPAN[j - 7]

    def sb_copy(a, j, mine):
        step, span = sb_place(j)
        v = piece(fields[a], 0 if mine else 1, step, *span)
        return rcopy(v, v, sb_s.at[a * 9 + j], sb_r.at[a * 9 + j], sdev)

    def part_of(way, i):
        return way if i == 0 else 1 - way

    def ag_first(a, i):
        for way in range(2):
            go(ag_send(a, way, 0, part_of(way, i)))

    def ag_wait(a, k, i):
        for way in range(2):
            ag_copy(a, way, k, part_of(way, i)).wait_recv()

    def ag_pass(a, k, i):
        for way in range(2):
            go(ag_send(a, way, k + 1, part_of(way, i)))

    def ag_own(a):
        go(sb_copy(a, 0, True))

    def ag_sib(a, k):
        for way in range(2):
            go(sb_copy(a, 7 + way if k == 3 else 1 + 3 * way + k, True))

    def gathered(a):
        for j in range(9):
            sb_copy(a, j, False).wait_recv()

    def turn():
        def body(n, carry):
            for s in range(SLOTS):
                i = n * SLOTS + s
                wint[n, :, s * BLK:(s + 1) * BLK] = win[i].T
                woutt[i] = wout[i].T
            return carry

        lax.fori_loop(0, ROWS, body, 0)

    def listed(ref, n):
        parts = []
        for s in range(SLOTS):
            i = live_col(n, s) * 2
            parts += [ref[i], ref[i + 1]]
        return cat(parts, 0)

    def tall(ref, n):
        return ref[n * SLOTS:(n + 1) * SLOTS].reshape(SLOTS * BLK, BLK)

    def hidden(lo, hi):
        for n in range(lo, hi):
            pre = dot(wint[n], listed(xg, n))
            sq = pre * pre
            th = jnp.tanh(C0 * pre * (1.0 + C1 * sq))
            half = 0.5 * (1.0 + th)
            dgelu[n] = half + 0.5 * pre * (1.0 - th * th) * (C0 * (1.0 + 3.0 * C1 * sq))
            hid[n] = (pre * half).astype(BF)

    def shares(a):
        w, act = ((woutt, hid), (win, gpre))[a]
        for n in range(ROWS):
            cbuf[n * SLOTS:(n + 1) * SLOTS] = dot(tall(w, n), act[n]).reshape(SLOTS, BLK, BLK)

    def sib_copy(a, zz):
        i = a * NZ + zz
        src = part.at[a, zz, pl.ds(pl.multiple_of(sib_row, 64), CH)]
        return rcopy(src, sib.at[a, zz], ss_s.at[i], ss_r.at[i], sdev)

    def place(a):
        def add(r, acc):
            acc = acc * tab[1, r].astype(F32) + cbuf[tab[0, r]]
            run[r] = acc.astype(BF)
            return acc

        lax.fori_loop(0, NB, add, jnp.zeros((BLK, BLK), F32), unroll=4)
        for step in ORDER:
            zz = wrap(step)
            for k in range(7):
                part[a, zz, BLK * k:BLK * (k + 1), :] = run[tab[2, zz * 7 + k]]
            go(sib_copy(a, zz))

    met = set()

    def chip_sum(a, step, h):
        zz = wrap(step)
        if (a, step % NZ) not in met:
            met.add((a, step % NZ))
            sib_copy(a, zz).wait_recv()
        src = part.at[a, zz, pl.ds(pl.multiple_of(own_row + h * H, 32), H)]
        return src, src[...].astype(F32) + sib[a, zz, h * H:(h + 1) * H].astype(F32)

    def z_copy(src, a, way, r, h):
        i = ((a * 2 + way) * 4 + r) * 2 + h
        dst = zb.at[a, way, r, pl.ds(h * H, H)]
        return rcopy(src, dst, zs.at[i], zr.at[i], zdev(1 if way == 0 else -1))

    def z_first(a, r):
        for way in range(2):
            h = way if r == 3 else 1 - way
            src, total = chip_sum(a, r + 1 if way == 0 else -(r + 1), h)
            src[...] = total.astype(BF)
            go(z_copy(src, a, way, r, h))

    def z_next(a, r, i):
        for way in range(2):
            h = way if i == 0 else 1 - way
            buf = zb.at[a, way, r, pl.ds(h * H, H)]
            z_copy(buf, a, way, r, h).wait_recv()
            src, total = chip_sum(a, r if way == 0 else -r, h)
            buf[...] = (buf[...].astype(F32) + total).astype(BF)
            go(z_copy(buf, a, way, r - 1, h))

    def z_last(a):
        dst = (out_ref, ing_ref)[a]
        for h in range(2):
            src, total = chip_sum(a, 0, h)
            for way in range(2):
                buf = zb.at[a, way, 0, pl.ds(h * H, H)]
                z_copy(buf, a, way, 0, h).wait_recv()
                total = total + buf[...].astype(F32)
            dst[h * H:(h + 1) * H, :] = total.astype(BF)

    coords = ((yat, xat), (xat, yat))
    devs = ((ydev, xdev), (xdev, ydev))

    def lines(p, g):
        lo, hi = GROUPS[g]
        return pl.ds(p * W + lo * 16, (hi - lo) * 16)

    def w_dst(a, ph, p, g, m):
        return wp.at[a, m, :, lines(p, g)] if ph == 0 else w2.at[a, m, lines(p, g)]

    def w_copy(src, a, ph, p, g, m):
        sign = 1 if p % 2 == 0 else -1
        i = (((a * 2 + ph) * 2 + g) * 4 + p) * 3 + m
        return rcopy(
            src, w_dst(a, ph, p, g, m), xs.at[i], xr.at[i], devs[p // 2][ph](sign if m < 2 else -sign)
        )

    def w_src(a, ph, p, g, step):
        c = coords[p // 2][ph][(step if p % 2 == 0 else -step) % NQ]
        if ph == 0:
            return wgt.at[a, c, :, lines(p, g)]
        return red.at[a, c, lines(p, g)]

    def w_send(a, ph, g, m):
        for p in range(4):
            go(w_copy(w_src(a, ph, p, g, 2 if m == 0 else -1), a, ph, p, g, m))

    def w_pass(a, ph, g):
        for p in range(4):
            buf = w_dst(a, ph, p, g, 0)
            w_copy(buf, a, ph, p, g, 0).wait_recv()
            mine = w_src(a, ph, p, g, 1)
            buf[...] = (buf[...].astype(F32) + mine[...].astype(F32)).astype(BF)
            go(w_copy(buf, a, ph, p, g, 1))

    def w_done(a, ph, g):
        dst = (gwout_ref, gwin_ref)[a]
        lo, hi = GROUPS[g]
        for p in range(4):
            total = w_src(a, ph, p, g, 0)[...].astype(F32)
            for m in (2, 1):
                buf = w_dst(a, ph, p, g, m)
                w_copy(buf, a, ph, p, g, m).wait_recv()
                total = total + buf[...].astype(F32)
            if ph == 0:
                red[a, :, lines(p, g)] = total.astype(BF)
            else:
                for n in range(lo, hi):
                    dst[n * 64 + p * 16:n * 64 + p * 16 + 16, :] = total[(n - lo) * 16:(n - lo) * 16 + 16]

    def store(a, n, p, both):
        both = both.astype(BF).reshape(NQ, NQ, 16, BLK)
        row = p * W + n * 16
        if p < 2:
            wgt[a, :, :, row:row + 16, :] = both
        else:
            for i in range(NQ):
                for j in range(NQ):
                    wgt[a, i, j, row:row + 16, :] = both[j, i]

    def backward_hidden():
        for n in range(ROWS):
            gh = dot(cat([wout[n * SLOTS + s] for s in range(SLOTS)], 1), listed(gg, n))
            gpre[n] = (gh * dgelu[n]).astype(BF)

    def backward_out(g):
        for n in range(*GROUPS[g]):
            gw = lax.dot_general(hid[n], listed(gg, n), NT, preferred_element_type=F32)
            for p in range(4):
                one = gw[:, 2 * p * BLK:(2 * p + 1) * BLK].reshape(16, 8, BLK)
                two = gw[:, (2 * p + 1) * BLK:(2 * p + 2) * BLK].reshape(16, 8, BLK)
                store(0, n, p, cat([one, two], 1))

    def backward_in(g):
        for n in range(*GROUPS[g]):
            gw = lax.dot_general(listed(xg, n), gpre[n], NT, preferred_element_type=F32)
            gw = gw.reshape(SLOTS, 16, 8, BLK)
            for p in range(4):
                store(1, n, p, cat([gw[2 * p], gw[2 * p + 1]], 1))

    waited = [0]

    def drain(upto):
        if isinstance(upto, tuple):
            upto = marks[PLAN.index(upto)]
        for c in sends[waited[0]:upto]:
            c.wait_send()
        waited[0] = upto

    def make():
        local[4].wait()
        local[5].wait()
        make_table()
        tcopy.start()

    def turned():
        local[2].wait()
        local[3].wait()
        turn()

    tcopy = pltpu.make_async_copy(tabv, tab, lsem.at[4])
    tasks = {
        "ag0": ag_first, "agw": ag_wait, "agf": ag_pass, "own": ag_own, "ags": ag_sib, "gath": gathered,
        "tabl": make, "turn": turned, "H": hidden, "GH": backward_hidden, "GO": backward_out,
        "GI": backward_in, "S": shares, "P": place, "zf": z_first, "zn": z_next, "zl": z_last,
        "wm": w_send, "wp": w_pass, "wd": w_done, "tab": tcopy.wait, "drain": drain,
    }
    marks = []
    local[0].wait()
    local[1].wait()
    pl.semaphore_wait(barrier, 7)
    for name, *args in PLAN:
        marks.append(len(sends))
        tasks[name](*args)
    drain(len(sends))


def finish(*refs):
    for i in range(4):
        refs[4 + i][...] = refs[i][...]


def on_device(inputs, out_grad, w_in, w_out, columns, counts):
    vm = pl.BlockSpec(memory_space=pltpu.VMEM)
    hbm = pl.BlockSpec(memory_space=pltpu.HBM)
    dma = pltpu.SemaphoreType.DMA
    shapes = (
        jax.ShapeDtypeStruct((CH, BLK), BF),
        jax.ShapeDtypeStruct((CH, BLK), BF),
        jax.ShapeDtypeStruct((CH, BLK), F32),
        jax.ShapeDtypeStruct((CH, BLK), F32),
    )
    res = pl.pallas_call(
        kernel,
        out_shape=shapes,
        in_specs=[hbm] * 6,
        out_specs=(vm, vm, vm, vm),
        scratch_shapes=[
            pltpu.VMEM((2 * DB + 2, 64, BLK), BF),
            pltpu.VMEM((2 * DB + 2, 64, BLK), BF),
            pltpu.VMEM((NB, BLK, BLK), BF),
            pltpu.VMEM((NB, BLK, BLK), BF),
            pltpu.VMEM((ROWS, BLK, SLOTS * BLK), BF),
            pltpu.VMEM((NB, BLK, BLK), BF),
            pltpu.VMEM((ROWS, BLK, 128), F32),
            pltpu.VMEM((ROWS, BLK, 128), BF),
            pltpu.VMEM((ROWS, BLK, 128), BF),
            pltpu.VMEM((NB, BLK, 128), F32),
            pltpu.VMEM((NB + 1, BLK, 128), BF),
            pltpu.VMEM((2, NZ, 2 * CH, BLK), BF),
            pltpu.VMEM((2, NZ, CH, BLK), BF),
            pltpu.VMEM((2, 2, 4, CH, BLK), BF),
            pltpu.VMEM((2, NQ, NQ, CH, BLK), BF),
            pltpu.VMEM((2, 3, NQ, CH, BLK), BF),
            pltpu.VMEM((2, NQ, CH, BLK), BF),
            pltpu.VMEM((2, 3, CH, BLK), BF),
            pltpu.VMEM((8, 128), jnp.int32),
            pltpu.SMEM((8, 128), jnp.int32),
            pltpu.SMEM((ROWS, SLOTS), jnp.int32),
            pltpu.SMEM((ROWS,), jnp.int32),
            dma((7,)),
            dma((32,)), dma((32,)),
            dma((18,)), dma((18,)),
            dma((16,)), dma((16,)),
            dma((32,)), dma((32,)),
            dma((96,)), dma((96,)),
        ],
        compiler_params=pltpu.CompilerParams(
            collective_id=0, has_side_effects=True, vmem_limit_bytes=63 * 1024 * 1024
        ),
        cost_estimate=pl.CostEstimate(flops=1_409_286_144, bytes_accessed=8_000_000, transcendentals=114_688),
    )(
        columns, counts,
        inputs.T.reshape(U, 64, BLK), out_grad.T.reshape(U, 64, BLK),
        w_in.reshape(NB, BLK, BLK), w_out.reshape(NB, BLK, BLK),
    )
    out, ing, gwin, gwout = pl.pallas_call(
        finish,
        out_shape=shapes,
        in_specs=[vm] * 4,
        out_specs=(vm,) * 4,
        compiler_params=pltpu.CompilerParams(vmem_limit_bytes=63 * 1024 * 1024),
        cost_estimate=pl.CostEstimate(flops=0, bytes_accessed=1_400_000, transcendentals=0),
    )(*res)
    return (out.T, ing.T, gwin.reshape(ROWS, SLOTS, 8, BLK), gwout.reshape(ROWS, SLOTS, 8, BLK))


def solution(mesh):
    return jax.shard_map(
        on_device,
        mesh=mesh,
        in_specs=(
            P("dp", "tensor"),
            P("dp", "tensor"),
            P("tensor", None, None, None),
            P("tensor", None, None, None),
            P("tensor", None),
            P("tensor"),
        ),
        out_specs=(
            P("dp", "tensor"),
            P("dp", "tensor"),
            P("tensor", None, "dp", None),
            P("tensor", None, "dp", None),
        ),
        check_vma=False,
    )
```

```python
import jax
import jax.numpy as jnp
from jax import lax
from jax.experimental import pallas as pl
from jax.experimental.pallas import tpu as pltpu
from jax.sharding import PartitionSpec as P

BLK = 128
SLOTS = 8
ROWS = 7
NB = ROWS * SLOTS
DB = 56
NZ = 8
NQ = 4
CH = 448
U = 7
SPAN = ((0, 4), (4, 3))
H = 224
W = 112
GROUPS = ((0, 7),)
BF = jnp.bfloat16
F32 = jnp.float32
MESH = pl.DeviceIdType.MESH
C0 = 0.7978845608028654
C1 = 0.044715
ORDER = (4, 3, -3, 2, -2, 1, -1, 0)
FIRST = 3
NT = (((1,), (1,)), ((), ()))
PLAN = (
    ("ag0", 0, 0), ("ag0", 0, 1), ("turn",), ("ag0", 1, 0), ("ag0", 1, 1), ("agw", 0, 0, 0), ("agf", 0, 0, 0),
    ("agw", 0, 0, 1), ("agw", 1, 0, 0), ("agf", 1, 0, 0), ("agf", 0, 0, 1), ("agw", 0, 1, 0), ("agf", 0, 1, 0),
    ("agw", 1, 0, 1), ("agf", 1, 0, 1), ("own", 0), ("agw", 1, 1, 0), ("agf", 1, 1, 0), ("tabl",), ("ags", 1, 0),
    ("agw", 0, 1, 1), ("own", 1), ("ags", 0, 0), ("agf", 0, 1, 1), ("agw", 0, 2, 0), ("agf", 0, 2, 0),
    ("agw", 1, 1, 1), ("ags", 0, 1), ("agf", 1, 1, 1), ("agw", 1, 2, 0), ("agf", 1, 2, 0), ("agw", 0, 2, 1),
    ("ags", 0, 2), ("ags", 1, 1), ("agw", 0, 3, 0), ("ags", 0, 3), ("agw", 1, 2, 1), ("ags", 1, 2), ("agw", 1, 3, 0),
    ("ags", 1, 3), ("gath", 0), ("H", 0, 4), ("H", 4, 7), ("S", 0), ("tab",), ("P", 0), ("gath", 1), ("GH",),
    ("GO", 0), ("wm", 0, 0, 0, 0), ("S", 1), ("P", 1), ("zf", 0), ("wm", 0, 0, 0, 2), ("GI", 0), ("zf", 1),
    ("wm", 1, 0, 0, 0), ("wm", 1, 0, 0, 2), ("zn", 0, 3), ("zn", 1, 3), ("wp", 0, 0, 0), ("wp", 1, 0, 0),
    ("zn", 0, 2), ("zn", 1, 2), ("wd", 0, 0, 0), ("wm", 0, 1, 0, 0), ("wm", 0, 1, 0, 2), ("zn", 0, 1),
    ("wd", 1, 0, 0), ("wm", 1, 1, 0, 0), ("zn", 1, 1), ("wp", 0, 1, 0), ("wm", 1, 1, 0, 2), ("wp", 1, 1, 0),
    ("ag_sent",), ("w_sent", 0, 0), ("w_sent", 1, 0), ("wd", 0, 1, 0), ("zl", 0), ("zl", 1), ("wd", 1, 1, 0),
    ("z_sent", 0), ("z_sent", 1), ("w_sent", 0, 1), ("w_sent", 1, 1),
)


def cat(parts, axis):
    return jnp.concatenate(parts, axis=axis)


def dot(a, b):
    return jnp.dot(a, b, preferred_element_type=F32)


def kernel(
    col_hbm, cnt_hbm, x_hbm, g_hbm, win_hbm, wout_hbm,
    out_ref, ing_ref, gwin_ref, gwout_ref,
    xg, gg, win, wout, wint, woutt, dgelu, hid, gpre, cbuf, run, part, sib, zb,
    wgt, wp, red, w2, tabv, tab, col_ref, cnt_ref,
    lsem, ag_s, ag_r, sb_s, sb_r, ss_s, ss_r, zs, zr, xs, xr,
):
    dp = lax.axis_index("dp")
    tn = lax.axis_index("tensor")
    yy, xx = dp // NQ, dp % NQ
    z, core = tn // 2, tn % 2

    zat = [z] + [(z + i) % NZ for i in range(1, NZ)]
    yat = [yy] + [(yy + i) % NQ for i in range(1, NQ)]
    xat = [xx] + [(xx + i) % NQ for i in range(1, NQ)]
    other = 1 - core
    chunk = [[zat[i] * 2 + core for i in range(NZ)], [zat[i] * 2 + other for i in range(NZ)]]
    first = [[t * U for t in half] for half in chunk]
    zdevs = {i: {"dp": dp, "tensor": chunk[0][i % NZ]} for i in (1, -1)}
    sdev = {"dp": dp, "tensor": chunk[1][0]}
    ydevs = {i: {"dp": yat[i % NQ] * NQ + xx, "tensor": tn} for i in (1, -1)}
    xdevs = {i: {"dp": yy * NQ + xat[i % NQ], "tensor": tn} for i in (1, -1)}
    zdev, ydev, xdev = zdevs.get, ydevs.get, xdevs.get
    own_row, sib_row = core * CH, other * CH

    def landed(view, rsem):
        rcopy(view, view, lsem.at[0], rsem, sdev).wait_recv()

    def sent(view, ssem):
        rcopy(view, view, ssem, lsem.at[0], sdev).wait_send()

    def rcopy(src, dst, ssem, rsem, dev):
        return pltpu.make_async_remote_copy(
            src_ref=src, dst_ref=dst, send_sem=ssem, recv_sem=rsem,
            device_id=dev, device_id_type=MESH,
        )

    def go(copy):
        copy.start()

    barrier = pltpu.get_barrier_semaphore()
    for dev in (sdev, zdev(1), zdev(-1), xdev(1), xdev(-1), ydev(1), ydev(-1)):
        pl.semaphore_signal(barrier, inc=1, device_id=dev, device_id_type=MESH)

    fields = (xg, gg)
    own = pl.ds(first[0][0], U)
    local = [
        pltpu.make_async_copy(x_hbm, xg.at[own], lsem.at[0]),
        pltpu.make_async_copy(g_hbm, gg.at[own], lsem.at[1]),
        pltpu.make_async_copy(win_hbm, win, lsem.at[2]),
        pltpu.make_async_copy(wout_hbm, wout, lsem.at[3]),
        pltpu.make_async_copy(col_hbm, col_ref, lsem.at[5]),
        pltpu.make_async_copy(cnt_hbm, cnt_ref, lsem.at[6]),
    ]
    for c in local:
        c.start()

    def live_col(n, s):
        return jnp.where(s < cnt_ref[n], col_ref[n, s], DB)

    def make_table():
        sub = lax.broadcasted_iota(jnp.int32, (8, 128), 0)
        lan = lax.broadcasted_iota(jnp.int32, (8, 128), 1)
        down = []
        across = jnp.full((8, 128), 1000, jnp.int32)
        for n in range(ROWS):
            v = jnp.zeros((8, 128), jnp.int32)
            for s in range(SLOTS):
                c = live_col(n, s)
                v = jnp.where(sub == s, c, v)
                across = jnp.where(lan == n * SLOTS + s, c, across)
            down.append(v)
        across = across * 64 + lan

        def add_rows(parts):
            t = parts[0]
            for v in parts[1:]:
                t = t + v
            for sh in (4, 2, 1):
                t = t + pltpu.roll(t, sh, 0)
            return t

        def count(v):
            return jnp.where(v, 1, 0)

        spots = [jnp.full((8, 128), n * SLOTS, jnp.int32) + sub for n in range(ROWS)]
        ranks = []
        for n in range(ROWS):
            t = count(across < down[n] * 64 + spots[n])
            for sh in (64, 32, 16, 8, 4, 2, 1):
                t = t + pltpu.roll(t, sh, 1)
            ranks.append(t)
        perm = add_rows([jnp.where(ranks[n] == lan, spots[n], 0) for n in range(ROWS)])
        cols = add_rows([jnp.where(ranks[n] == lan, down[n], 0) for n in range(ROWS)])
        same = count((cols == pltpu.roll(cols, 1, 1)) & (lan > 0))
        upto = add_rows([count(down[n] <= lan) for n in range(ROWS)])
        here = add_rows([count(down[n] == lan) for n in range(ROWS)])
        last = jnp.where(here > 0, upto - 1, NB)
        tabv[...] = jnp.where(sub == 0, perm, jnp.where(sub == 1, same, last))

    for ref in fields:
        ref[2 * DB] = jnp.zeros((64, BLK), BF)
        ref[2 * DB + 1] = jnp.zeros((64, BLK), BF)
    run[NB] = jnp.zeros((BLK, BLK), BF)

    def piece(ref, side, step, lo=0, n=U):
        return ref.at[pl.ds(first[side][step % NZ] + lo, n)]

    def wrap(step):
        return zat[step % NZ]

    def ag_copy(a, way, k, h):
        step = -(k + 1) if way == 0 else k + 1
        v = piece(fields[a], 0, step, *SPAN[h])
        i = ((a * 2 + way) * 4 + k) * 2 + h
        return rcopy(v, v, ag_s.at[a], ag_r.at[i], zdev(1 if way == 0 else -1))

    def ag_send(a, way, k, h):
        step = -k if way == 0 else k
        v = piece(fields[a], 0, step, *SPAN[h])
        i = ((a * 2 + way) * 4 + k) * 2 + h
        return rcopy(v, v, ag_s.at[a], ag_r.at[i], zdev(1 if way == 0 else -1))

    def sb_place(j):
        if j == 0:
            return 0, (0, U)
        if j < 7:
            way, k = (j - 1) // 3, (j - 1) % 3
            return (-(k + 1) if way == 0 else k + 1), (0, U)
        return 4, SPAN[j - 7]

    def sb_copy(a, j, mine):
        step, span = sb_place(j)
        v = piece(fields[a], 0 if mine else 1, step, *span)
        return rcopy(v, v, sb_s.at[a], sb_r.at[a], sdev)

    def part_of(way, i):
        return way if i == 0 else 1 - way

    def ag_first(a, i):
        for way in range(2):
            go(ag_send(a, way, 0, part_of(way, i)))

    def ag_wait(a, k, i):
        for way in range(2):
            ag_copy(a, way, k, part_of(way, i)).wait_recv()

    def ag_pass(a, k, i):
        for way in range(2):
            go(ag_send(a, way, k + 1, part_of(way, i)))

    def ag_own(a):
        go(sb_copy(a, 0, True))

    def ag_sib(a, k):
        for way in range(2):
            go(sb_copy(a, 7 + way if k == 3 else 1 + 3 * way + k, True))

    def gathered(a):
        landed(fields[a].at[pl.ds(0, NZ * U)], sb_r.at[a])

    def turn():
        def body(n, carry):
            for s in range(SLOTS):
                i = n * SLOTS + s
                wint[n, :, s * BLK:(s + 1) * BLK] = win[i].T
                woutt[i] = wout[i].T
            return carry

        lax.fori_loop(0, ROWS, body, 0)

    def listed(ref, n):
        parts = []
        for s in range(SLOTS):
            i = live_col(n, s) * 2
            parts += [ref[i], ref[i + 1]]
        return cat(parts, 0)

    def tall(ref, n):
        return ref[n * SLOTS:(n + 1) * SLOTS].reshape(SLOTS * BLK, BLK)

    def hidden(lo, hi):
        for n in range(lo, hi):
            pre = dot(wint[n], listed(xg, n))
            sq = pre * pre
            th = jnp.tanh(C0 * pre * (1.0 + C1 * sq))
            half = 0.5 * (1.0 + th)
            dgelu[n] = half + 0.5 * pre * (1.0 - th * th) * (C0 * (1.0 + 3.0 * C1 * sq))
            hid[n] = (pre * half).astype(BF)

    def shares(a):
        w, act = ((woutt, hid), (win, gpre))[a]
        for n in range(ROWS):
            cbuf[n * SLOTS:(n + 1) * SLOTS] = dot(tall(w, n), act[n]).reshape(SLOTS, BLK, BLK)

    def sib_copy(a, g):
        span = pl.ds(0, FIRST) if g == 0 else pl.ds(FIRST, NZ - FIRST)
        src = part.at[a, span, pl.ds(pl.multiple_of(sib_row, 64), CH)]
        return rcopy(src, sib.at[a, span], ss_s.at[a], ss_r.at[a * 2 + g], sdev)

    def place(a):
        def add(r, acc):
            acc = acc * tab[1, r].astype(F32) + cbuf[tab[0, r]]
            run[r] = acc.astype(BF)
            return acc

        lax.fori_loop(0, NB, add, jnp.zeros((BLK, BLK), F32), unroll=4)
        for j, step in enumerate(ORDER):
            zz = wrap(step)
            for k in range(7):
                part[a, j, BLK * k:BLK * (k + 1), :] = run[tab[2, zz * 7 + k]]
            if j == FIRST - 1:
                go(sib_copy(a, 0))
        go(sib_copy(a, 1))

    met = set()

    def chip_sum(a, step, h):
        j = ORDER.index(step if step in ORDER else step + NZ)
        g = 0 if j < FIRST else 1
        if (a, g) not in met:
            met.add((a, g))
            sib_copy(a, g).wait_recv()
        src = part.at[a, j, pl.ds(pl.multiple_of(own_row + h * H, 32), H)]
        return src, src[...].astype(F32) + sib[a, j, h * H:(h + 1) * H].astype(F32)

    def z_copy(src, a, way, r):
        dst = zb.at[a, way, r]
        if r == 3:
            dst = dst.at[pl.ds(way * H, H)]
        return rcopy(src, dst, zs.at[a], zr.at[a * 4 + r], zdev(1 if way == 0 else -1))

    def z_first(a):
        for way in range(2):
            src, total = chip_sum(a, 4 if way == 0 else -4, way)
            src[...] = total.astype(BF)
            go(z_copy(src, a, way, 3))

    def z_next(a, r):
        if r == 3:
            landed(zb.at[a, :, r, pl.ds(0, H)], zr.at[a * 4 + r])
        else:
            landed(zb.at[a, :, r], zr.at[a * 4 + r])
        for way in range(2):
            for h in range(2):
                src, total = chip_sum(a, r if way == 0 else -r, h)
                buf = zb.at[a, way, r, pl.ds(h * H, H)]
                if r < 3 or h == way:
                    total = total + buf[...].astype(F32)
                buf[...] = total.astype(BF)
            go(z_copy(zb.at[a, way, r], a, way, r - 1))

    def z_last(a):
        dst = (out_ref, ing_ref)[a]
        landed(zb.at[a, :, 0], zr.at[a * 4])
        for h in range(2):
            src, total = chip_sum(a, 0, h)
            for way in range(2):
                total = total + zb[a, way, 0, h * H:(h + 1) * H].astype(F32)
            dst[h * H:(h + 1) * H, :] = total.astype(BF)

    coords = ((yat, xat), (xat, yat))
    devs = ((ydev, xdev), (xdev, ydev))

    def lines(p, g):
        lo, hi = GROUPS[g]
        return pl.ds(p * W + lo * 16, (hi - lo) * 16)

    def w_dst(a, ph, p, g, m):
        return wp.at[a, m, :, lines(p, g)] if ph == 0 else w2.at[a, m, lines(p, g)]

    def w_copy(src, a, ph, p, g, m):
        sign = 1 if p % 2 == 0 else -1
        i = ((a * 2 + ph) * len(GROUPS) + g) * 2 + (0 if m == 0 else 1)
        return rcopy(
            src, w_dst(a, ph, p, g, m), xs.at[a * 2 + ph], xr.at[i], devs[p // 2][ph](sign if m < 2 else -sign)
        )

    def w_landed(a, ph, g, m):
        i = ((a * 2 + ph) * len(GROUPS) + g) * 2 + (0 if m == 0 else 1)
        lo, hi = GROUPS[g]
        span = pl.ds(0, (hi - lo) * 64)
        if m == 0:
            view = wp.at[a, 0, :, span] if ph == 0 else w2.at[a, 0, span]
        else:
            view = wp.at[a, pl.ds(1, 2), :, span] if ph == 0 else w2.at[a, pl.ds(1, 2), span]
        landed(view, xr.at[i])

    def w_src(a, ph, p, g, step):
        c = coords[p // 2][ph][(step if p % 2 == 0 else -step) % NQ]
        if ph == 0:
            return wgt.at[a, c, :, lines(p, g)]
        return red.at[a, c, lines(p, g)]

    def w_send(a, ph, g, m):
        for p in range(4):
            go(w_copy(w_src(a, ph, p, g, 2 if m == 0 else -1), a, ph, p, g, m))

    def w_pass(a, ph, g):
        w_landed(a, ph, g, 0)
        for p in range(4):
            buf = w_dst(a, ph, p, g, 0)
            mine = w_src(a, ph, p, g, 1)
            buf[...] = (buf[...].astype(F32) + mine[...].astype(F32)).astype(BF)
            go(w_copy(buf, a, ph, p, g, 1))

    def w_done(a, ph, g):
        dst = (gwout_ref, gwin_ref)[a]
        lo, hi = GROUPS[g]
        w_landed(a, ph, g, 1)
        for p in range(4):
            total = w_src(a, ph, p, g, 0)[...].astype(F32)
            for m in (2, 1):
                buf = w_dst(a, ph, p, g, m)
                total = total + buf[...].astype(F32)
            if ph == 0:
                red[a, :, lines(p, g)] = total.astype(BF)
            else:
                for n in range(lo, hi):
                    dst[n * 64 + p * 16:n * 64 + p * 16 + 16, :] = total[(n - lo) * 16:(n - lo) * 16 + 16]

    def store(a, n, p, both):
        both = both.astype(BF).reshape(NQ, NQ, 16, BLK)
        row = p * W + n * 16
        if p < 2:
            wgt[a, :, :, row:row + 16, :] = both
        else:
            for i in range(NQ):
                for j in range(NQ):
                    wgt[a, i, j, row:row + 16, :] = both[j, i]

    def backward_hidden():
        for n in range(ROWS):
            gh = dot(cat([wout[n * SLOTS + s] for s in range(SLOTS)], 1), listed(gg, n))
            gpre[n] = (gh * dgelu[n]).astype(BF)

    def backward_out(g):
        for n in range(*GROUPS[g]):
            gw = lax.dot_general(hid[n], listed(gg, n), NT, preferred_element_type=F32)
            for p in range(4):
                one = gw[:, 2 * p * BLK:(2 * p + 1) * BLK].reshape(16, 8, BLK)
                two = gw[:, (2 * p + 1) * BLK:(2 * p + 2) * BLK].reshape(16, 8, BLK)
                store(0, n, p, cat([one, two], 1))

    def backward_in(g):
        for n in range(*GROUPS[g]):
            gw = lax.dot_general(listed(xg, n), gpre[n], NT, preferred_element_type=F32)
            gw = gw.reshape(SLOTS, 16, 8, BLK)
            for p in range(4):
                store(1, n, p, cat([gw[2 * p], gw[2 * p + 1]], 1))

    def ag_sent():
        for a in range(2):
            sent(fields[a].at[pl.ds(0, 7 * U)], ag_s.at[a])
            sent(fields[a].at[pl.ds(0, NZ * U)], sb_s.at[a])

    def z_sent(a):
        sent(sib.at[a], ss_s.at[a])
        sent(sib.at[a, pl.ds(0, 7)], zs.at[a])

    def w_sent(a, ph):
        sent(wp.at[a] if ph == 0 else w2.at[a], xs.at[a * 2 + ph])

    def make():
        local[4].wait()
        local[5].wait()
        make_table()
        tcopy.start()

    def turned():
        local[2].wait()
        local[3].wait()
        turn()

    tcopy = pltpu.make_async_copy(tabv, tab, lsem.at[4])
    tasks = {
        "ag0": ag_first, "agw": ag_wait, "agf": ag_pass, "own": ag_own, "ags": ag_sib, "gath": gathered,
        "tabl": make, "turn": turned, "H": hidden, "GH": backward_hidden, "GO": backward_out,
        "GI": backward_in, "S": shares, "P": place, "zf": z_first, "zn": z_next, "zl": z_last,
        "wm": w_send, "wp": w_pass, "wd": w_done, "tab": tcopy.wait, "ag_sent": ag_sent, "z_sent": z_sent, "w_sent": w_sent,
    }
    local[0].wait()
    local[1].wait()
    pl.semaphore_wait(barrier, 7)
    for name, *args in PLAN:
        tasks[name](*args)


def finish(*refs):
    for i in range(4):
        refs[4 + i][...] = refs[i][...]


def on_device(inputs, out_grad, w_in, w_out, columns, counts):
    vm = pl.BlockSpec(memory_space=pltpu.VMEM)
    hbm = pl.BlockSpec(memory_space=pltpu.HBM)
    dma = pltpu.SemaphoreType.DMA
    shapes = (
        jax.ShapeDtypeStruct((CH, BLK), BF),
        jax.ShapeDtypeStruct((CH, BLK), BF),
        jax.ShapeDtypeStruct((CH, BLK), F32),
        jax.ShapeDtypeStruct((CH, BLK), F32),
    )
    res = pl.pallas_call(
        kernel,
        out_shape=shapes,
        in_specs=[hbm] * 6,
        out_specs=(vm, vm, vm, vm),
        scratch_shapes=[
            pltpu.VMEM((2 * DB + 2, 64, BLK), BF),
            pltpu.VMEM((2 * DB + 2, 64, BLK), BF),
            pltpu.VMEM((NB, BLK, BLK), BF),
            pltpu.VMEM((NB, BLK, BLK), BF),
            pltpu.VMEM((ROWS, BLK, SLOTS * BLK), BF),
            pltpu.VMEM((NB, BLK, BLK), BF),
            pltpu.VMEM((ROWS, BLK, 128), F32),
            pltpu.VMEM((ROWS, BLK, 128), BF),
            pltpu.VMEM((ROWS, BLK, 128), BF),
            pltpu.VMEM((NB, BLK, 128), F32),
            pltpu.VMEM((NB + 1, BLK, 128), BF),
            pltpu.VMEM((2, NZ, 2 * CH, BLK), BF),
            pltpu.VMEM((2, NZ, CH, BLK), BF),
            pltpu.VMEM((2, 2, 4, CH, BLK), BF),
            pltpu.VMEM((2, NQ, NQ, CH, BLK), BF),
            pltpu.VMEM((2, 3, NQ, CH, BLK), BF),
            pltpu.VMEM((2, NQ, CH, BLK), BF),
            pltpu.VMEM((2, 3, CH, BLK), BF),
            pltpu.VMEM((8, 128), jnp.int32),
            pltpu.SMEM((8, 128), jnp.int32),
            pltpu.SMEM((ROWS, SLOTS), jnp.int32),
            pltpu.SMEM((ROWS,), jnp.int32),
            dma((7,)),
            dma((2,)), dma((32,)),
            dma((2,)), dma((2,)),
            dma((2,)), dma((4,)),
            dma((2,)), dma((8,)),
            dma((4,)), dma((8,)),
        ],
        compiler_params=pltpu.CompilerParams(
            collective_id=0, has_side_effects=True, vmem_limit_bytes=63 * 1024 * 1024
        ),
        cost_estimate=pl.CostEstimate(flops=1_409_286_144, bytes_accessed=8_000_000, transcendentals=114_688),
    )(
        columns, counts,
        inputs.T.reshape(U, 64, BLK), out_grad.T.reshape(U, 64, BLK),
        w_in.reshape(NB, BLK, BLK), w_out.reshape(NB, BLK, BLK),
    )
    out, ing, gwin, gwout = pl.pallas_call(
        finish,
        out_shape=shapes,
        in_specs=[vm] * 4,
        out_specs=(vm,) * 4,
        compiler_params=pltpu.CompilerParams(vmem_limit_bytes=63 * 1024 * 1024),
        cost_estimate=pl.CostEstimate(flops=0, bytes_accessed=1_400_000, transcendentals=0),
    )(*res)
    return (out.T, ing.T, gwin.reshape(ROWS, SLOTS, 8, BLK), gwout.reshape(ROWS, SLOTS, 8, BLK))


def solution(mesh):
    return jax.shard_map(
        on_device,
        mesh=mesh,
        in_specs=(
            P("dp", "tensor"),
            P("dp", "tensor"),
            P("tensor", None, None, None),
            P("tensor", None, None, None),
            P("tensor", None),
            P("tensor"),
        ),
        out_specs=(
            P("dp", "tensor"),
            P("dp", "tensor"),
            P("tensor", None, "dp", None),
            P("tensor", None, "dp", None),
        ),
        check_vma=False,
    )
```

```python
import jax
import jax.numpy as jnp
from jax import lax
from jax.experimental import pallas as pl
from jax.experimental.pallas import tpu as pltpu
from jax.sharding import PartitionSpec as P

BLK = 128
SLOTS = 8
ROWS = 7
NB = ROWS * SLOTS
DB = 56
NZ = 8
NQ = 4
CH = 448
U = 7
SPAN = ((0, 4), (4, 3))
H = 224
GROUPS = ((0, 4), (4, 7))
BF = jnp.bfloat16
F32 = jnp.float32
MESH = pl.DeviceIdType.MESH
C0 = 0.7978845608028654
C1 = 0.044715
ORDER = (4, 3, -3, 2, -2, 1, -1, 0)
HALVES = (True, True)
FIRST = 3
NT = (((1,), (1,)), ((), ()))
PLAN = (
    ("ag0", 0, 0), ("ag0", 1, 0), ("ag0", 0, 1), ("turn",), ("ag0", 1, 1), ("agw", 0, 0, 0), ("agf", 0, 0, 0),
    ("own", 1), ("agw", 1, 0, 0), ("agf", 1, 0, 0), ("own", 0), ("agw", 1, 0, 1), ("agw", 0, 0, 1), ("agf", 0, 0, 1),
    ("agw", 0, 1, 0), ("agf", 0, 1, 0), ("tabl",), ("agf", 1, 0, 1), ("agw", 1, 1, 0), ("agf", 1, 1, 0),
    ("agw", 0, 1, 1), ("agf", 0, 1, 1), ("agw", 0, 2, 0), ("agf", 0, 2, 0), ("agw", 1, 1, 1), ("agf", 1, 1, 1),
    ("ags", 0, 0), ("agw", 1, 2, 0), ("agf", 1, 2, 0), ("ags", 1, 1), ("agw", 0, 2, 1), ("ags", 1, 0), ("ags", 0, 2),
    ("ags", 0, 1), ("agw", 0, 3, 0), ("ags", 0, 3), ("agw", 1, 2, 1), ("ags", 1, 2), ("agw", 1, 3, 0), ("ags", 1, 3),
    ("gath", 0), ("H", 0, 4), ("H", 4, 7), ("S", 0), ("tab",), ("P", 0), ("gath", 1), ("GH",), ("GI", 0),
    ("wm", 1, 0, 0, 2), ("GO", 0), ("zf", 0), ("wm", 0, 0, 0, 2), ("S", 1), ("wm", 0, 0, 0, 0), ("P", 1), ("zg", 0),
    ("wm", 1, 0, 0, 0), ("GO", 1), ("wm", 0, 0, 1, 0), ("zn", 0, 3, 0), ("GI", 1), ("zf", 1), ("wm", 1, 0, 1, 0),
    ("zg", 1), ("wp", 0, 0, 0), ("zn", 0, 2, 1), ("wp", 1, 0, 0), ("zn", 0, 2, 0), ("wm", 0, 0, 1, 2),
    ("wp", 0, 0, 1), ("zn", 1, 3, 0), ("wm", 1, 0, 1, 2), ("zn", 1, 2, 1), ("wp", 1, 0, 1), ("wd", 0, 0, 0),
    ("wm", 0, 1, 0, 0), ("wd", 1, 0, 0), ("wm", 1, 1, 0, 0), ("zn", 0, 1, 1), ("wm", 1, 1, 0, 2), ("zn", 1, 2, 0),
    ("wd", 0, 0, 1), ("wm", 0, 1, 0, 2), ("wm", 0, 1, 1, 0), ("zn", 0, 1, 0), ("zn", 1, 1, 1), ("wd", 1, 0, 1),
    ("wm", 1, 1, 1, 0), ("wp", 0, 1, 0), ("wm", 1, 1, 1, 2), ("wm", 0, 1, 1, 2), ("zn", 1, 1, 0), ("wp", 0, 1, 1),
    ("wp", 1, 1, 0), ("wp", 1, 1, 1), ("ag_sent",), ("w_sent", 0, 0), ("w_sent", 1, 0), ("wd", 0, 1, 0), ("zl", 0),
    ("wd", 0, 1, 1), ("zl", 1), ("wd", 1, 1, 0), ("wd", 1, 1, 1), ("z_sent", 0), ("z_sent", 1), ("w_sent", 0, 1),
    ("w_sent", 1, 1),
)


def cat(parts, axis):
    return jnp.concatenate(parts, axis=axis)


def dot(a, b):
    return jnp.dot(a, b, preferred_element_type=F32)


def kernel(
    col_hbm, cnt_hbm, x_hbm, g_hbm, win_hbm, wout_hbm,
    out_ref, ing_ref, gwin_ref, gwout_ref,
    xg, gg, win, wout, wint, woutt, dgelu, hid, gpre, cbuf, run, part, sib, zb,
    wgts, wps, reds, w2s, tabv, tab, col_ref, cnt_ref,
    lsem, ag_s, ag_r, sb_s, sb_r, ss_s, ss_r, zs, zr, xs, xr,
):
    dp = lax.axis_index("dp")
    tn = lax.axis_index("tensor")
    yy, xx = dp // NQ, dp % NQ
    z, core = tn // 2, tn % 2

    zat = [z] + [(z + i) % NZ for i in range(1, NZ)]
    yat = [yy] + [(yy + i) % NQ for i in range(1, NQ)]
    xat = [xx] + [(xx + i) % NQ for i in range(1, NQ)]
    other = 1 - core
    chunk = [[zat[i] * 2 + core for i in range(NZ)], [zat[i] * 2 + other for i in range(NZ)]]
    first = [[t * U for t in half] for half in chunk]
    zdevs = {i: {"dp": dp, "tensor": chunk[0][i % NZ]} for i in (1, -1)}
    sdev = {"dp": dp, "tensor": chunk[1][0]}
    ydevs = {i: {"dp": yat[i % NQ] * NQ + xx, "tensor": tn} for i in (1, -1)}
    xdevs = {i: {"dp": yy * NQ + xat[i % NQ], "tensor": tn} for i in (1, -1)}
    zdev, ydev, xdev = zdevs.get, ydevs.get, xdevs.get
    own_row, sib_row = core * CH, other * CH

    def landed(view, rsem):
        rcopy(view, view, lsem.at[0], rsem, sdev).wait_recv()

    def sent(view, ssem):
        rcopy(view, view, ssem, lsem.at[0], sdev).wait_send()

    def rcopy(src, dst, ssem, rsem, dev):
        return pltpu.make_async_remote_copy(
            src_ref=src, dst_ref=dst, send_sem=ssem, recv_sem=rsem,
            device_id=dev, device_id_type=MESH,
        )

    def go(copy):
        copy.start()

    barrier = pltpu.get_barrier_semaphore()
    for dev in (sdev, zdev(1), zdev(-1), xdev(1), xdev(-1), ydev(1), ydev(-1)):
        pl.semaphore_signal(barrier, inc=1, device_id=dev, device_id_type=MESH)

    fields = (xg, gg)
    own = pl.ds(first[0][0], U)
    local = [
        pltpu.make_async_copy(x_hbm, xg.at[own], lsem.at[0]),
        pltpu.make_async_copy(g_hbm, gg.at[own], lsem.at[1]),
        pltpu.make_async_copy(win_hbm, win, lsem.at[2]),
        pltpu.make_async_copy(wout_hbm, wout, lsem.at[3]),
        pltpu.make_async_copy(col_hbm, col_ref, lsem.at[5]),
        pltpu.make_async_copy(cnt_hbm, cnt_ref, lsem.at[6]),
    ]
    for c in local:
        c.start()

    def live_col(n, s):
        return jnp.where(s < cnt_ref[n], col_ref[n, s], DB)

    def make_table():
        sub = lax.broadcasted_iota(jnp.int32, (8, 128), 0)
        lan = lax.broadcasted_iota(jnp.int32, (8, 128), 1)
        down = []
        across = jnp.full((8, 128), 1000, jnp.int32)
        for n in range(ROWS):
            v = jnp.zeros((8, 128), jnp.int32)
            for s in range(SLOTS):
                c = live_col(n, s)
                v = jnp.where(sub == s, c, v)
                across = jnp.where(lan == n * SLOTS + s, c, across)
            down.append(v)
        across = across * 64 + lan

        def add_rows(parts):
            t = parts[0]
            for v in parts[1:]:
                t = t + v
            for sh in (4, 2, 1):
                t = t + pltpu.roll(t, sh, 0)
            return t

        def count(v):
            return jnp.where(v, 1, 0)

        spots = [jnp.full((8, 128), n * SLOTS, jnp.int32) + sub for n in range(ROWS)]
        ranks = []
        for n in range(ROWS):
            t = count(across < down[n] * 64 + spots[n])
            for sh in (64, 32, 16, 8, 4, 2, 1):
                t = t + pltpu.roll(t, sh, 1)
            ranks.append(t)
        perm = add_rows([jnp.where(ranks[n] == lan, spots[n], 0) for n in range(ROWS)])
        cols = add_rows([jnp.where(ranks[n] == lan, down[n], 0) for n in range(ROWS)])
        same = count((cols == pltpu.roll(cols, 1, 1)) & (lan > 0))
        upto = add_rows([count(down[n] <= lan) for n in range(ROWS)])
        here = add_rows([count(down[n] == lan) for n in range(ROWS)])
        last = jnp.where(here > 0, upto - 1, NB)
        tabv[...] = jnp.where(sub == 0, perm, jnp.where(sub == 1, same, last))

    for ref in fields:
        ref[2 * DB] = jnp.zeros((64, BLK), BF)
        ref[2 * DB + 1] = jnp.zeros((64, BLK), BF)
    run[NB] = jnp.zeros((BLK, BLK), BF)

    def piece(ref, side, step, lo=0, n=U):
        return ref.at[pl.ds(first[side][step % NZ] + lo, n)]

    def wrap(step):
        return zat[step % NZ]

    def ag_copy(a, way, k, h):
        step = -(k + 1) if way == 0 else k + 1
        v = piece(fields[a], 0, step, *SPAN[h])
        i = ((a * 2 + way) * 4 + k) * 2 + h
        return rcopy(v, v, ag_s.at[a], ag_r.at[i], zdev(1 if way == 0 else -1))

    def ag_send(a, way, k, h):
        step = -k if way == 0 else k
        v = piece(fields[a], 0, step, *SPAN[h])
        i = ((a * 2 + way) * 4 + k) * 2 + h
        src = (x_hbm, g_hbm)[a].at[pl.ds(*SPAN[h])] if k == 0 else v
        return rcopy(src, v, ag_s.at[a], ag_r.at[i], zdev(1 if way == 0 else -1))

    def sb_place(j):
        if j == 0:
            return 0, (0, U)
        if j < 7:
            way, k = (j - 1) // 3, (j - 1) % 3
            return (-(k + 1) if way == 0 else k + 1), (0, U)
        return 4, SPAN[j - 7]

    def sb_copy(a, j, mine):
        step, span = sb_place(j)
        v = piece(fields[a], 0 if mine else 1, step, *span)
        src = (x_hbm, g_hbm)[a] if j == 0 else v
        return rcopy(src, v, sb_s.at[a], sb_r.at[a], sdev)

    def part_of(way, i):
        return way if i == 0 else 1 - way

    def ag_first(a, i):
        for way in range(2):
            go(ag_send(a, way, 0, part_of(way, i)))

    def ag_wait(a, k, i):
        for way in range(2):
            ag_copy(a, way, k, part_of(way, i)).wait_recv()

    def ag_pass(a, k, i):
        for way in range(2):
            go(ag_send(a, way, k + 1, part_of(way, i)))

    def ag_own(a):
        go(sb_copy(a, 0, True))

    def ag_sib(a, k):
        for way in range(2):
            go(sb_copy(a, 7 + way if k == 3 else 1 + 3 * way + k, True))

    def gathered(a):
        local[a].wait()
        landed(fields[a].at[pl.ds(0, NZ * U)], sb_r.at[a])

    def turn():
        def body(n, carry):
            for s in range(SLOTS):
                i = n * SLOTS + s
                wint[n, :, s * BLK:(s + 1) * BLK] = win[i].T
                woutt[i] = wout[i].T
            return carry

        lax.fori_loop(0, ROWS, body, 0)

    def listed(ref, n):
        parts = []
        for s in range(SLOTS):
            i = live_col(n, s) * 2
            parts += [ref[i], ref[i + 1]]
        return cat(parts, 0)

    def tall(ref, n):
        return ref[n * SLOTS:(n + 1) * SLOTS].reshape(SLOTS * BLK, BLK)

    def hidden(lo, hi):
        for n in range(lo, hi):
            pre = dot(wint[n], listed(xg, n))
            sq = pre * pre
            th = jnp.tanh(C0 * pre * (1.0 + C1 * sq))
            half = 0.5 * (1.0 + th)
            dgelu[n] = half + 0.5 * pre * (1.0 - th * th) * (C0 * (1.0 + 3.0 * C1 * sq))
            hid[n] = (pre * half).astype(BF)

    def shares(a):
        w, act = ((woutt, hid), (win, gpre))[a]
        for n in range(ROWS):
            cbuf[n * SLOTS:(n + 1) * SLOTS] = dot(tall(w, n), act[n]).reshape(SLOTS, BLK, BLK)

    def sib_copy(a, g):
        span = pl.ds(0, FIRST) if g == 0 else pl.ds(FIRST, NZ - FIRST)
        src = part.at[a, span, pl.ds(pl.multiple_of(sib_row, 64), CH)]
        return rcopy(src, sib.at[a, span], ss_s.at[a], ss_r.at[a * 2 + g], sdev)

    def place(a):
        def add(r, acc):
            acc = acc * tab[1, r].astype(F32) + cbuf[tab[0, r]]
            run[r] = acc.astype(BF)
            return acc

        lax.fori_loop(0, NB, add, jnp.zeros((BLK, BLK), F32), unroll=4)
        for j, step in enumerate(ORDER):
            zz = wrap(step)
            for k in range(7):
                part[a, j, BLK * k:BLK * (k + 1), :] = run[tab[2, zz * 7 + k]]
            if j == FIRST - 1:
                go(sib_copy(a, 0))
        go(sib_copy(a, 1))

    met = set()

    def chip_sum(a, step, h):
        j = ORDER.index(step if step in ORDER else step + NZ)
        g = 0 if j < FIRST else 1
        if (a, g) not in met:
            met.add((a, g))
            sib_copy(a, g).wait_recv()
        src = part.at[a, j, pl.ds(pl.multiple_of(own_row + h * H, 32), H)]
        return src, src[...].astype(F32) + sib[a, j, h * H:(h + 1) * H].astype(F32)

    def z_half(ref, way, i):
        if i is None:
            return ref
        return ref.at[pl.ds((way if i == 0 else 1 - way) * H, H)]

    def z_sem(a, r, i):
        return zr.at[(a * 4 + r) * 2 + (i or 0)]

    def z_copy(src, a, way, r, i):
        dst = z_half(zb.at[a, way, r], way, i)
        return rcopy(src, dst, zs.at[a], z_sem(a, r, i), zdev(1 if way == 0 else -1))

    def z_wait(a, r, i):
        view = zb.at[a, :, r] if i is None else zb.at[a, :, r, pl.ds(0, H)]
        landed(view, z_sem(a, r, i))

    def z_start(a, r):
        for way in range(2):
            src, total = chip_sum(a, r + 1 if way == 0 else -(r + 1), way if r == 3 else 1 - way)
            src[...] = total.astype(BF)
            go(z_copy(src, a, way, r, 3 - r))

    def z_first(a):
        z_start(a, 3)

    def z_near(a):
        z_start(a, 2)

    def z_next(a, r, i=None):
        z_wait(a, r, 0 if r == 3 else i)
        for way in range(2):
            for h in range(2):
                if i is not None and h != (way if i == 0 else 1 - way):
                    continue
                src, total = chip_sum(a, r if way == 0 else -r, h)
                buf = zb.at[a, way, r, pl.ds(h * H, H)]
                if r < 3 or h == way:
                    total = total + buf[...].astype(F32)
                buf[...] = total.astype(BF)
            go(z_copy(z_half(zb.at[a, way, r], way, i), a, way, r - 1, i))

    def z_last(a):
        dst = (out_ref, ing_ref)[a]
        for i in (0, 1) if HALVES[a] else (None,):
            z_wait(a, 0, i)
        for h in range(2):
            src, total = chip_sum(a, 0, h)
            for way in range(2):
                total = total + zb[a, way, 0, h * H:(h + 1) * H].astype(F32)
            dst[h * H:(h + 1) * H, :] = total.astype(BF)

    coords = ((yat, xat), (xat, yat))
    devs = ((ydev, xdev), (xdev, ydev))

    def w_dst(a, ph, p, g, m):
        return wps[g].at[a, m, p] if ph == 0 else w2s[g].at[a, m, p]

    def w_sem(a, ph, g, m):
        return xr.at[((a * 2 + ph) * len(GROUPS) + g) * 2 + (0 if m == 0 else 1)]

    def w_copy(src, a, ph, p, g, m):
        sign = 1 if p % 2 == 0 else -1
        return rcopy(
            src, w_dst(a, ph, p, g, m), xs.at[(a * 2 + ph) * len(GROUPS) + g], w_sem(a, ph, g, m),
            devs[p // 2][ph](sign if m < 2 else -sign)
        )

    def w_landed(a, ph, g, m):
        ref = (wps if ph == 0 else w2s)[g]
        landed(ref.at[a, 0] if m == 0 else ref.at[a, pl.ds(1, 2)], w_sem(a, ph, g, m))

    def w_src(a, ph, p, g, step):
        c = coords[p // 2][ph][(step if p % 2 == 0 else -step) % NQ]
        return (wgts if ph == 0 else reds)[g].at[a, p, c]

    def w_send(a, ph, g, m):
        for p in range(4):
            go(w_copy(w_src(a, ph, p, g, 2 if m == 0 else -1), a, ph, p, g, m))

    def w_pass(a, ph, g):
        w_landed(a, ph, g, 0)
        for p in range(4):
            buf = w_dst(a, ph, p, g, 0)
            mine = w_src(a, ph, p, g, 1)
            buf[...] = (buf[...].astype(F32) + mine[...].astype(F32)).astype(BF)
            go(w_copy(buf, a, ph, p, g, 1))

    def w_done(a, ph, g):
        dst = (gwout_ref, gwin_ref)[a]
        lo, hi = GROUPS[g]
        w_landed(a, ph, g, 1)
        for p in range(4):
            total = w_src(a, ph, p, g, 0)[...].astype(F32)
            for m in (2, 1):
                buf = w_dst(a, ph, p, g, m)
                total = total + buf[...].astype(F32)
            if ph == 0:
                reds[g][a, p] = total.astype(BF)
            else:
                for n in range(lo, hi):
                    dst[n * 64 + p * 16:n * 64 + p * 16 + 16, :] = total[(n - lo) * 16:(n - lo) * 16 + 16]

    def store(a, n, p, both):
        both = both.astype(BF).reshape(NQ, NQ, 16, BLK)
        g = [lo <= n < hi for lo, hi in GROUPS].index(True)
        row = (n - GROUPS[g][0]) * 16
        if p < 2:
            wgts[g][a, p, :, :, row:row + 16, :] = both
        else:
            for i in range(NQ):
                for j in range(NQ):
                    wgts[g][a, p, i, j, row:row + 16, :] = both[j, i]

    def backward_hidden():
        for n in range(ROWS):
            gh = dot(cat([wout[n * SLOTS + s] for s in range(SLOTS)], 1), listed(gg, n))
            gpre[n] = (gh * dgelu[n]).astype(BF)

    def backward_out(g):
        for n in range(*GROUPS[g]):
            gw = lax.dot_general(hid[n], listed(gg, n), NT, preferred_element_type=F32)
            for p in range(4):
                one = gw[:, 2 * p * BLK:(2 * p + 1) * BLK].reshape(16, 8, BLK)
                two = gw[:, (2 * p + 1) * BLK:(2 * p + 2) * BLK].reshape(16, 8, BLK)
                store(0, n, p, cat([one, two], 1))

    def backward_in(g):
        for n in range(*GROUPS[g]):
            gw = lax.dot_general(listed(xg, n), gpre[n], NT, preferred_element_type=F32)
            gw = gw.reshape(SLOTS, 16, 8, BLK)
            for p in range(4):
                store(1, n, p, cat([gw[2 * p], gw[2 * p + 1]], 1))

    def ag_sent():
        for a in range(2):
            sent(fields[a].at[pl.ds(0, 7 * U)], ag_s.at[a])
            sent(fields[a].at[pl.ds(0, NZ * U)], sb_s.at[a])

    def z_sent(a):
        sent(sib.at[a], ss_s.at[a])
        sent(sib.at[a, pl.ds(0, 7)], zs.at[a])

    def w_sent(a, ph):
        for g in range(len(GROUPS)):
            sent((wps if ph == 0 else w2s)[g].at[a], xs.at[(a * 2 + ph) * len(GROUPS) + g])

    def make():
        local[4].wait()
        local[5].wait()
        make_table()
        tcopy.start()

    def turned():
        local[2].wait()
        local[3].wait()
        turn()

    tcopy = pltpu.make_async_copy(tabv, tab, lsem.at[4])
    tasks = {
        "ag0": ag_first, "agw": ag_wait, "agf": ag_pass, "own": ag_own, "ags": ag_sib, "gath": gathered,
        "tabl": make, "turn": turned, "H": hidden, "GH": backward_hidden, "GO": backward_out,
        "GI": backward_in, "S": shares, "P": place, "zf": z_first, "zg": z_near, "zn": z_next, "zl": z_last,
        "wm": w_send, "wp": w_pass, "wd": w_done, "tab": tcopy.wait, "ag_sent": ag_sent, "z_sent": z_sent, "w_sent": w_sent,
    }
    pl.semaphore_wait(barrier, 7)
    for name, *args in PLAN:
        tasks[name](*args)


def finish(*refs):
    for i in range(4):
        refs[4 + i][...] = refs[i][...]


def on_device(inputs, out_grad, w_in, w_out, columns, counts):
    vm = pl.BlockSpec(memory_space=pltpu.VMEM)
    hbm = pl.BlockSpec(memory_space=pltpu.HBM)
    dma = pltpu.SemaphoreType.DMA
    heights = [(hi - lo) * 16 for lo, hi in GROUPS]
    shapes = (
        jax.ShapeDtypeStruct((CH, BLK), BF),
        jax.ShapeDtypeStruct((CH, BLK), BF),
        jax.ShapeDtypeStruct((CH, BLK), F32),
        jax.ShapeDtypeStruct((CH, BLK), F32),
    )
    res = pl.pallas_call(
        kernel,
        out_shape=shapes,
        in_specs=[hbm] * 6,
        out_specs=(vm, vm, vm, vm),
        scratch_shapes=[
            pltpu.VMEM((2 * DB + 2, 64, BLK), BF),
            pltpu.VMEM((2 * DB + 2, 64, BLK), BF),
            pltpu.VMEM((NB, BLK, BLK), BF),
            pltpu.VMEM((NB, BLK, BLK), BF),
            pltpu.VMEM((ROWS, BLK, SLOTS * BLK), BF),
            pltpu.VMEM((NB, BLK, BLK), BF),
            pltpu.VMEM((ROWS, BLK, 128), F32),
            pltpu.VMEM((ROWS, BLK, 128), BF),
            pltpu.VMEM((ROWS, BLK, 128), BF),
            pltpu.VMEM((NB, BLK, 128), F32),
            pltpu.VMEM((NB + 1, BLK, 128), BF),
            pltpu.VMEM((2, NZ, 2 * CH, BLK), BF),
            pltpu.VMEM((2, NZ, CH, BLK), BF),
            pltpu.VMEM((2, 2, 4, CH, BLK), BF),
            [pltpu.VMEM((2, 4, NQ, NQ, r, BLK), BF) for r in heights],
            [pltpu.VMEM((2, 3, 4, NQ, r, BLK), BF) for r in heights],
            [pltpu.VMEM((2, 4, NQ, r, BLK), BF) for r in heights],
            [pltpu.VMEM((2, 3, 4, r, BLK), BF) for r in heights],
            pltpu.VMEM((8, 128), jnp.int32),
            pltpu.SMEM((8, 128), jnp.int32),
            pltpu.SMEM((ROWS, SLOTS), jnp.int32),
            pltpu.SMEM((ROWS,), jnp.int32),
            dma((7,)),
            dma((2,)), dma((32,)),
            dma((2,)), dma((2,)),
            dma((2,)), dma((4,)),
            dma((2,)), dma((16,)),
            dma((8,)), dma((16,)),
        ],
        compiler_params=pltpu.CompilerParams(
            collective_id=0, has_side_effects=True, vmem_limit_bytes=63 * 1024 * 1024
        ),
        cost_estimate=pl.CostEstimate(flops=1_409_286_144, bytes_accessed=8_000_000, transcendentals=114_688),
    )(
        columns, counts,
        inputs.T.reshape(U, 64, BLK), out_grad.T.reshape(U, 64, BLK),
        w_in.reshape(NB, BLK, BLK), w_out.reshape(NB, BLK, BLK),
    )
    out, ing, gwin, gwout = pl.pallas_call(
        finish,
        out_shape=shapes,
        in_specs=[vm] * 4,
        out_specs=(vm,) * 4,
        compiler_params=pltpu.CompilerParams(vmem_limit_bytes=63 * 1024 * 1024),
        cost_estimate=pl.CostEstimate(flops=0, bytes_accessed=1_400_000, transcendentals=0),
    )(*res)
    return (out.T, ing.T, gwin.reshape(ROWS, SLOTS, 8, BLK), gwout.reshape(ROWS, SLOTS, 8, BLK))


def solution(mesh):
    return jax.shard_map(
        on_device,
        mesh=mesh,
        in_specs=(
            P("dp", "tensor"),
            P("dp", "tensor"),
            P("tensor", None, None, None),
            P("tensor", None, None, None),
            P("tensor", None),
            P("tensor"),
        ),
        out_specs=(
            P("dp", "tensor"),
            P("dp", "tensor"),
            P("tensor", None, "dp", None),
            P("tensor", None, "dp", None),
        ),
        check_vma=False,
    )
```

```python
import jax
import jax.numpy as jnp
from jax import lax
from jax.experimental import pallas as pl
from jax.experimental.pallas import tpu as pltpu
from jax.sharding import PartitionSpec as P

BLK = 128
SLOTS = 8
ROWS = 7
NB = ROWS * SLOTS
DB = 56
NZ = 8
NQ = 4
CH = 448
U = 7
SPAN = ((0, 4), (4, 3))
H = 224
GROUPS = ((0, 7),)
BF = jnp.bfloat16
F32 = jnp.float32
MESH = pl.DeviceIdType.MESH
C0 = 0.7978845608028654
C1 = 0.044715
ORDER = (4, 3, -3, 2, -2, 1, -1, 0)
HALVES = (False, False)
FIRST = 3
NT = (((1,), (1,)), ((), ()))
PLAN = (
    ("ag0", 0, 0), ("ag0", 0, 1), ("turn",), ("ag0", 1, 0), ("ag0", 1, 1), ("agw", 0, 0, 0), ("agf", 0, 0, 0),
    ("agw", 0, 0, 1), ("agw", 1, 0, 0), ("agf", 1, 0, 0), ("agf", 0, 0, 1), ("agw", 0, 1, 0), ("agf", 0, 1, 0),
    ("agw", 1, 0, 1), ("agf", 1, 0, 1), ("own", 0), ("agw", 1, 1, 0), ("agf", 1, 1, 0), ("tabl",), ("ags", 1, 0),
    ("agw", 0, 1, 1), ("own", 1), ("ags", 0, 0), ("agf", 0, 1, 1), ("agw", 0, 2, 0), ("agf", 0, 2, 0),
    ("agw", 1, 1, 1), ("ags", 0, 1), ("agf", 1, 1, 1), ("agw", 1, 2, 0), ("agf", 1, 2, 0), ("agw", 0, 2, 1),
    ("ags", 0, 2), ("ags", 1, 1), ("agw", 0, 3, 0), ("ags", 0, 3), ("agw", 1, 2, 1), ("ags", 1, 2), ("agw", 1, 3, 0),
    ("ags", 1, 3), ("gath", 0), ("H", 0, 4), ("H", 4, 7), ("S", 0), ("tab",), ("P", 0), ("gath", 1), ("GH",),
    ("GO", 0), ("wm", 0, 0, 0, 0), ("S", 1), ("P", 1), ("zf", 0), ("wm", 0, 0, 0, 2), ("GI", 0), ("zf", 1),
    ("wm", 1, 0, 0, 0), ("wm", 1, 0, 0, 2), ("zn", 0, 3), ("zn", 1, 3), ("wp", 0, 0, 0), ("wp", 1, 0, 0),
    ("zn", 0, 2), ("zn", 1, 2), ("wd", 0, 0, 0), ("wm", 0, 1, 0, 0), ("wm", 0, 1, 0, 2), ("zn", 0, 1),
    ("wd", 1, 0, 0), ("wm", 1, 1, 0, 0), ("zn", 1, 1), ("wp", 0, 1, 0), ("wm", 1, 1, 0, 2), ("wp", 1, 1, 0),
    ("ag_sent",), ("w_sent", 0, 0), ("w_sent", 1, 0), ("wd", 0, 1, 0), ("zl", 0), ("zl", 1), ("wd", 1, 1, 0),
    ("z_sent", 0), ("z_sent", 1), ("w_sent", 0, 1), ("w_sent", 1, 1),
)


def cat(parts, axis):
    return jnp.concatenate(parts, axis=axis)


def dot(a, b):
    return jnp.dot(a, b, preferred_element_type=F32)


def kernel(
    col_hbm, cnt_hbm, x_hbm, g_hbm, win_hbm, wout_hbm,
    act_ref, grad_ref,
    xg, gg, win, wout, wint, woutt, dgelu, hid, gpre, cbuf, run, part, sib, zb,
    wgts, wps, reds, w2s, tabv, tab, col_ref, cnt_ref,
    lsem, ag_s, ag_r, sb_s, sb_r, ss_s, ss_r, zs, zr, xs, xr,
):
    dp = lax.axis_index("dp")
    tn = lax.axis_index("tensor")
    yy, xx = dp // NQ, dp % NQ
    z, core = tn // 2, tn % 2

    zat = [z] + [(z + i) % NZ for i in range(1, NZ)]
    yat = [yy] + [(yy + i) % NQ for i in range(1, NQ)]
    xat = [xx] + [(xx + i) % NQ for i in range(1, NQ)]
    other = 1 - core
    chunk = [[zat[i] * 2 + core for i in range(NZ)], [zat[i] * 2 + other for i in range(NZ)]]
    first = [[t * U for t in half] for half in chunk]
    zdevs = {i: {"dp": dp, "tensor": chunk[0][i % NZ]} for i in (1, -1)}
    sdev = {"dp": dp, "tensor": chunk[1][0]}
    ydevs = {i: {"dp": yat[i % NQ] * NQ + xx, "tensor": tn} for i in (1, -1)}
    xdevs = {i: {"dp": yy * NQ + xat[i % NQ], "tensor": tn} for i in (1, -1)}
    zdev, ydev, xdev = zdevs.get, ydevs.get, xdevs.get
    own_row, sib_row = core * CH, other * CH

    def landed(view, rsem):
        rcopy(view, view, lsem.at[0], rsem, sdev).wait_recv()

    def sent(view, ssem):
        rcopy(view, view, ssem, lsem.at[0], sdev).wait_send()

    def rcopy(src, dst, ssem, rsem, dev):
        return pltpu.make_async_remote_copy(
            src_ref=src, dst_ref=dst, send_sem=ssem, recv_sem=rsem,
            device_id=dev, device_id_type=MESH,
        )

    def go(copy):
        copy.start()

    barrier = pltpu.get_barrier_semaphore()
    for dev in (sdev, zdev(1), zdev(-1), xdev(1), xdev(-1), ydev(1), ydev(-1)):
        pl.semaphore_signal(barrier, inc=1, device_id=dev, device_id_type=MESH)

    fields = (xg, gg)
    own = pl.ds(first[0][0], U)
    local = [
        pltpu.make_async_copy(x_hbm, xg.at[own], lsem.at[0]),
        pltpu.make_async_copy(g_hbm, gg.at[own], lsem.at[1]),
        pltpu.make_async_copy(win_hbm, win, lsem.at[2]),
        pltpu.make_async_copy(wout_hbm, wout, lsem.at[3]),
        pltpu.make_async_copy(col_hbm, col_ref, lsem.at[5]),
        pltpu.make_async_copy(cnt_hbm, cnt_ref, lsem.at[6]),
    ]
    for c in local:
        c.start()

    def live_col(n, s):
        return jnp.where(s < cnt_ref[n], col_ref[n, s], DB)

    def make_table():
        sub = lax.broadcasted_iota(jnp.int32, (8, 128), 0)
        lan = lax.broadcasted_iota(jnp.int32, (8, 128), 1)
        down = []
        across = jnp.full((8, 128), 1000, jnp.int32)
        for n in range(ROWS):
            v = jnp.zeros((8, 128), jnp.int32)
            for s in range(SLOTS):
                c = live_col(n, s)
                v = jnp.where(sub == s, c, v)
                across = jnp.where(lan == n * SLOTS + s, c, across)
            down.append(v)
        across = across * 64 + lan

        def add_rows(parts):
            t = parts[0]
            for v in parts[1:]:
                t = t + v
            for sh in (4, 2, 1):
                t = t + pltpu.roll(t, sh, 0)
            return t

        def count(v):
            return jnp.where(v, 1, 0)

        spots = [jnp.full((8, 128), n * SLOTS, jnp.int32) + sub for n in range(ROWS)]
        ranks = []
        for n in range(ROWS):
            t = count(across < down[n] * 64 + spots[n])
            for sh in (64, 32, 16, 8, 4, 2, 1):
                t = t + pltpu.roll(t, sh, 1)
            ranks.append(t)
        perm = add_rows([jnp.where(ranks[n] == lan, spots[n], 0) for n in range(ROWS)])
        cols = add_rows([jnp.where(ranks[n] == lan, down[n], 0) for n in range(ROWS)])
        same = count((cols == pltpu.roll(cols, 1, 1)) & (lan > 0))
        upto = add_rows([count(down[n] <= lan) for n in range(ROWS)])
        here = add_rows([count(down[n] == lan) for n in range(ROWS)])
        last = jnp.where(here > 0, upto - 1, NB)
        tabv[...] = jnp.where(sub == 0, perm, jnp.where(sub == 1, same, last))

    for ref in fields:
        ref[2 * DB] = jnp.zeros((64, BLK), BF)
        ref[2 * DB + 1] = jnp.zeros((64, BLK), BF)
    run[NB] = jnp.zeros((BLK, BLK), BF)

    def piece(ref, side, step, lo=0, n=U):
        return ref.at[pl.ds(first[side][step % NZ] + lo, n)]

    def wrap(step):
        return zat[step % NZ]

    def ag_send(a, way, k, h):
        v = piece(fields[a], 0, -k if way == 0 else k, *SPAN[h])
        src = (x_hbm, g_hbm)[a].at[pl.ds(*SPAN[h])] if k == 0 else v
        i = (a * 4 + k) * 2 + (0 if h == way else 1)
        return rcopy(src, v, ag_s.at[a], ag_r.at[i], zdev(1 if way == 0 else -1))

    def sb_place(j):
        if j == 0:
            return 0, (0, U)
        if j < 7:
            way, k = (j - 1) // 3, (j - 1) % 3
            return (-(k + 1) if way == 0 else k + 1), (0, U)
        return 4, SPAN[j - 7]

    def sb_copy(a, j, mine):
        step, span = sb_place(j)
        v = piece(fields[a], 0 if mine else 1, step, *span)
        src = (x_hbm, g_hbm)[a] if j == 0 else v
        return rcopy(src, v, sb_s.at[a], sb_r.at[a], sdev)

    def part_of(way, i):
        return way if i == 0 else 1 - way

    def ag_first(a, i):
        for way in range(2):
            go(ag_send(a, way, 0, part_of(way, i)))

    def ag_wait(a, k, i):
        landed(fields[a].at[pl.ds(0, U)], ag_r.at[(a * 4 + k) * 2 + i])

    def ag_pass(a, k, i):
        for way in range(2):
            go(ag_send(a, way, k + 1, part_of(way, i)))

    def ag_own(a):
        go(sb_copy(a, 0, True))

    def ag_sib(a, k):
        for way in range(2):
            go(sb_copy(a, 7 + way if k == 3 else 1 + 3 * way + k, True))

    def gathered(a):
        local[a].wait()
        landed(fields[a].at[pl.ds(0, NZ * U)], sb_r.at[a])

    def turn():
        def body(n, carry):
            for s in range(SLOTS):
                i = n * SLOTS + s
                wint[n, :, s * BLK:(s + 1) * BLK] = win[i].T
                woutt[i] = wout[i].T
            return carry

        lax.fori_loop(0, ROWS, body, 0)

    def listed(ref, n):
        parts = []
        for s in range(SLOTS):
            i = live_col(n, s) * 2
            parts += [ref[i], ref[i + 1]]
        return cat(parts, 0)

    def tall(ref, n):
        return ref[n * SLOTS:(n + 1) * SLOTS].reshape(SLOTS * BLK, BLK)

    def hidden(lo, hi):
        for n in range(lo, hi):
            pre = dot(wint[n], listed(xg, n))
            sq = pre * pre
            th = jnp.tanh(C0 * pre * (1.0 + C1 * sq))
            half = 0.5 * (1.0 + th)
            dgelu[n] = half + 0.5 * pre * (1.0 - th * th) * (C0 * (1.0 + 3.0 * C1 * sq))
            hid[n] = (pre * half).astype(BF)

    def shares(a):
        w, act = ((woutt, hid), (win, gpre))[a]
        for n in range(ROWS):
            cbuf[n * SLOTS:(n + 1) * SLOTS] = dot(tall(w, n), act[n]).reshape(SLOTS, BLK, BLK)

    def sib_copy(a, g):
        span = pl.ds(0, FIRST) if g == 0 else pl.ds(FIRST, NZ - FIRST)
        src = part.at[a, span, pl.ds(pl.multiple_of(sib_row, 64), CH)]
        return rcopy(src, sib.at[a, span], ss_s.at[a], ss_r.at[a * 2 + g], sdev)

    def place(a):
        def add(r, acc):
            acc = acc * tab[1, r].astype(F32) + cbuf[tab[0, r]]
            run[r] = acc.astype(BF)
            return acc

        lax.fori_loop(0, NB, add, jnp.zeros((BLK, BLK), F32), unroll=4)
        for j, step in enumerate(ORDER):
            zz = wrap(step)
            for k in range(7):
                part[a, j, BLK * k:BLK * (k + 1), :] = run[tab[2, zz * 7 + k]]
            if j == FIRST - 1:
                go(sib_copy(a, 0))
        go(sib_copy(a, 1))

    met = set()

    def chip_sum(a, step, h):
        j = ORDER.index(step if step in ORDER else step + NZ)
        g = 0 if j < FIRST else 1
        if (a, g) not in met:
            met.add((a, g))
            sib_copy(a, g).wait_recv()
        src = part.at[a, j, pl.ds(pl.multiple_of(own_row + h * H, 32), H)]
        return src, src[...].astype(F32) + sib[a, j, h * H:(h + 1) * H].astype(F32)

    def z_half(ref, way, i):
        if i is None:
            return ref
        return ref.at[pl.ds((way if i == 0 else 1 - way) * H, H)]

    def z_sem(a, r, i):
        return zr.at[(a * 4 + r) * 2 + (i or 0)]

    def z_copy(src, a, way, r, i):
        dst = z_half(zb.at[a, way, r], way, i)
        return rcopy(src, dst, zs.at[a], z_sem(a, r, i), zdev(1 if way == 0 else -1))

    def z_wait(a, r, i):
        view = zb.at[a, :, r] if i is None else zb.at[a, :, r, pl.ds(0, H)]
        landed(view, z_sem(a, r, i))

    def z_start(a, r):
        copies = []
        for way in range(2):
            src, total = chip_sum(a, r + 1 if way == 0 else -(r + 1), way if r == 3 else 1 - way)
            src[...] = total.astype(BF)
            copies.append(z_copy(src, a, way, r, 3 - r))
        for c in copies:
            go(c)

    def z_first(a):
        z_start(a, 3)

    def z_near(a):
        z_start(a, 2)

    def z_next(a, r, i=None):
        z_wait(a, r, 0 if r == 3 else i)
        for way in range(2):
            for h in range(2):
                if i is not None and h != (way if i == 0 else 1 - way):
                    continue
                src, total = chip_sum(a, r if way == 0 else -r, h)
                buf = zb.at[a, way, r, pl.ds(h * H, H)]
                if r < 3 or h == way:
                    total = total + buf[...].astype(F32)
                buf[...] = total.astype(BF)
        for way in range(2):
            go(z_copy(z_half(zb.at[a, way, r], way, i), a, way, r - 1, i))

    def z_last(a):
        dst = act_ref.at[a]
        for i in (0, 1) if HALVES[a] else (None,):
            z_wait(a, 0, i)
        for h in range(2):
            src, total = chip_sum(a, 0, h)
            for way in range(2):
                total = total + zb[a, way, 0, h * H:(h + 1) * H].astype(F32)
            dst[h * H:(h + 1) * H, :] = total.astype(BF)

    coords = ((yat, xat), (xat, yat))
    devs = ((ydev, xdev), (xdev, ydev))

    def w_dst(a, ph, p, g, m):
        return wps[g].at[a, m, p] if ph == 0 else w2s[g].at[a, m, p]

    def w_sem(a, ph, g, m):
        return xr.at[((a * 2 + ph) * len(GROUPS) + g) * 2 + (0 if m == 0 else 1)]

    def w_copy(src, a, ph, p, g, m):
        sign = 1 if p % 2 == 0 else -1
        return rcopy(
            src, w_dst(a, ph, p, g, m), xs.at[(a * 2 + ph) * len(GROUPS) + g], w_sem(a, ph, g, m),
            devs[p // 2][ph](sign if m < 2 else -sign)
        )

    def w_landed(a, ph, g, m):
        ref = (wps if ph == 0 else w2s)[g]
        landed(ref.at[a, 0] if m == 0 else ref.at[a, pl.ds(1, 2)], w_sem(a, ph, g, m))

    def w_src(a, ph, p, g, step):
        c = coords[p // 2][ph][(step if p % 2 == 0 else -step) % NQ]
        return (wgts if ph == 0 else reds)[g].at[a, p, c]

    def w_send(a, ph, g, m):
        for p in range(4):
            go(w_copy(w_src(a, ph, p, g, 2 if m == 0 else -1), a, ph, p, g, m))

    def w_pass(a, ph, g):
        w_landed(a, ph, g, 0)
        for p in range(4):
            buf = w_dst(a, ph, p, g, 0)
            mine = w_src(a, ph, p, g, 1)
            buf[...] = (buf[...].astype(F32) + mine[...].astype(F32)).astype(BF)
        for p in range(4):
            go(w_copy(w_dst(a, ph, p, g, 0), a, ph, p, g, 1))

    def w_done(a, ph, g):
        dst = grad_ref.at[a]
        lo, hi = GROUPS[g]
        w_landed(a, ph, g, 1)
        for p in range(4):
            total = w_src(a, ph, p, g, 0)[...].astype(F32)
            for m in (2, 1):
                buf = w_dst(a, ph, p, g, m)
                total = total + buf[...].astype(F32)
            if ph == 0:
                reds[g][a, p] = total.astype(BF)
            else:
                for n in range(lo, hi):
                    dst[n * 64 + p * 16:n * 64 + p * 16 + 16, :] = total[(n - lo) * 16:(n - lo) * 16 + 16]

    def store(a, n, p, both):
        both = both.astype(BF).reshape(NQ, NQ, 16, BLK)
        g = [lo <= n < hi for lo, hi in GROUPS].index(True)
        row = (n - GROUPS[g][0]) * 16
        if p < 2:
            wgts[g][a, p, :, :, row:row + 16, :] = both
        else:
            for i in range(NQ):
                for j in range(NQ):
                    wgts[g][a, p, i, j, row:row + 16, :] = both[j, i]

    def backward_hidden():
        for n in range(ROWS):
            gh = dot(cat([wout[n * SLOTS + s] for s in range(SLOTS)], 1), listed(gg, n))
            gpre[n] = (gh * dgelu[n]).astype(BF)

    def backward_out(g):
        for n in range(*GROUPS[g]):
            gw = lax.dot_general(hid[n], listed(gg, n), NT, preferred_element_type=F32)
            for p in range(4):
                one = gw[:, 2 * p * BLK:(2 * p + 1) * BLK].reshape(16, 8, BLK)
                two = gw[:, (2 * p + 1) * BLK:(2 * p + 2) * BLK].reshape(16, 8, BLK)
                store(0, n, p, cat([one, two], 1))

    def backward_in(g):
        for n in range(*GROUPS[g]):
            gw = lax.dot_general(listed(xg, n), gpre[n], NT, preferred_element_type=F32)
            gw = gw.reshape(SLOTS, 16, 8, BLK)
            for p in range(4):
                store(1, n, p, cat([gw[2 * p], gw[2 * p + 1]], 1))

    def ag_sent():
        for a in range(2):
            sent(fields[a].at[pl.ds(0, 7 * U)], ag_s.at[a])
            sent(fields[a].at[pl.ds(0, NZ * U)], sb_s.at[a])

    def z_sent(a):
        sent(sib.at[a], ss_s.at[a])
        sent(sib.at[a, pl.ds(0, 7)], zs.at[a])

    def w_sent(a, ph):
        for g in range(len(GROUPS)):
            sent((wps if ph == 0 else w2s)[g].at[a], xs.at[(a * 2 + ph) * len(GROUPS) + g])

    def make():
        local[4].wait()
        local[5].wait()
        make_table()
        tcopy.start()

    def turned():
        local[2].wait()
        local[3].wait()
        turn()

    tcopy = pltpu.make_async_copy(tabv, tab, lsem.at[4])
    tasks = {
        "ag0": ag_first, "agw": ag_wait, "agf": ag_pass, "own": ag_own, "ags": ag_sib, "gath": gathered,
        "tabl": make, "turn": turned, "H": hidden, "GH": backward_hidden, "GO": backward_out,
        "GI": backward_in, "S": shares, "P": place, "zf": z_first, "zg": z_near, "zn": z_next, "zl": z_last,
        "wm": w_send, "wp": w_pass, "wd": w_done, "tab": tcopy.wait, "ag_sent": ag_sent, "z_sent": z_sent, "w_sent": w_sent,
    }
    pl.semaphore_wait(barrier, 7)
    for name, *args in PLAN:
        tasks[name](*args)


def on_device(inputs, out_grad, w_in, w_out, columns, counts):
    vm = pl.BlockSpec(memory_space=pltpu.VMEM)
    hbm = pl.BlockSpec(memory_space=pltpu.HBM)
    dma = pltpu.SemaphoreType.DMA
    heights = [(hi - lo) * 16 for lo, hi in GROUPS]
    shapes = (jax.ShapeDtypeStruct((2, CH, BLK), BF), jax.ShapeDtypeStruct((2, CH, BLK), F32))
    act, grad = pl.pallas_call(
        kernel,
        out_shape=shapes,
        in_specs=[hbm] * 6,
        out_specs=(vm, vm),
        scratch_shapes=[
            pltpu.VMEM((2 * DB + 2, 64, BLK), BF),
            pltpu.VMEM((2 * DB + 2, 64, BLK), BF),
            pltpu.VMEM((NB, BLK, BLK), BF),
            pltpu.VMEM((NB, BLK, BLK), BF),
            pltpu.VMEM((ROWS, BLK, SLOTS * BLK), BF),
            pltpu.VMEM((NB, BLK, BLK), BF),
            pltpu.VMEM((ROWS, BLK, 128), F32),
            pltpu.VMEM((ROWS, BLK, 128), BF),
            pltpu.VMEM((ROWS, BLK, 128), BF),
            pltpu.VMEM((NB, BLK, 128), F32),
            pltpu.VMEM((NB + 1, BLK, 128), BF),
            pltpu.VMEM((2, NZ, 2 * CH, BLK), BF),
            pltpu.VMEM((2, NZ, CH, BLK), BF),
            pltpu.VMEM((2, 2, 4, CH, BLK), BF),
            [pltpu.VMEM((2, 4, NQ, NQ, r, BLK), BF) for r in heights],
            [pltpu.VMEM((2, 3, 4, NQ, r, BLK), BF) for r in heights],
            [pltpu.VMEM((2, 4, NQ, r, BLK), BF) for r in heights],
            [pltpu.VMEM((2, 3, 4, r, BLK), BF) for r in heights],
            pltpu.VMEM((8, 128), jnp.int32),
            pltpu.SMEM((8, 128), jnp.int32),
            pltpu.SMEM((ROWS, SLOTS), jnp.int32),
            pltpu.SMEM((ROWS,), jnp.int32),
            dma((7,)),
            dma((2,)), dma((16,)),
            dma((2,)), dma((2,)),
            dma((2,)), dma((4,)),
            dma((2,)), dma((16,)),
            dma((4,)), dma((8,)),
        ],
        compiler_params=pltpu.CompilerParams(
            collective_id=0, has_side_effects=True, vmem_limit_bytes=63 * 1024 * 1024
        ),
        cost_estimate=pl.CostEstimate(flops=1_409_286_144, bytes_accessed=8_000_000, transcendentals=114_688),
    )(
        columns, counts,
        inputs.T.reshape(U, 64, BLK), out_grad.T.reshape(U, 64, BLK),
        w_in.reshape(NB, BLK, BLK), w_out.reshape(NB, BLK, BLK),
    )
    shape = (ROWS, SLOTS, 8, BLK)
    return act[0].T, act[1].T, grad[1].reshape(shape), grad[0].reshape(shape)


def solution(mesh):
    return jax.shard_map(
        on_device,
        mesh=mesh,
        in_specs=(
            P("dp", "tensor"),
            P("dp", "tensor"),
            P("tensor", None, None, None),
            P("tensor", None, None, None),
            P("tensor", None),
            P("tensor"),
        ),
        out_specs=(
            P("dp", "tensor"),
            P("dp", "tensor"),
            P("tensor", None, "dp", None),
            P("tensor", None, "dp", None),
        ),
        check_vma=False,
    )
```

```python
import jax
import jax.numpy as jnp
from jax import lax
from jax.experimental import pallas as pl
from jax.experimental.pallas import tpu as pltpu
from jax.sharding import PartitionSpec as P

BLK = 128
SLOTS = 8
ROWS = 7
NB = ROWS * SLOTS
DB = 56
NZ = 8
NQ = 4
CH = 448
U = 7
SPAN = ((0, 4), (4, 3))
H = 224
W = 112
GROUPS = ((0, 7),)
BF = jnp.bfloat16
F32 = jnp.float32
MESH = pl.DeviceIdType.MESH
C0 = 0.7978845608028654
C1 = 0.044715
ORDER = (4, 3, -3, 2, -2, 1, -1, 0)
FIRST = 3
NT = (((1,), (1,)), ((), ()))
PLAN = (
    ("ag0", 0, 0), ("ag0", 0, 1), ("turn",), ("ag0", 1, 0), ("ag0", 1, 1), ("agw", 0, 0, 0), ("agf", 0, 0, 0),
    ("agw", 0, 0, 1), ("ags", 0, 0), ("tabl",), ("agf", 0, 0, 1), ("agw", 1, 0, 0), ("agf", 1, 0, 0),
    ("agw", 0, 1, 0), ("agf", 0, 1, 0), ("agw", 1, 0, 1), ("agf", 1, 0, 1), ("agw", 0, 1, 1), ("ags", 0, 1),
    ("own", 1), ("own", 0), ("agf", 0, 1, 1), ("agw", 1, 1, 0), ("agf", 1, 1, 0), ("ags", 1, 0), ("agw", 0, 2, 0),
    ("agf", 0, 2, 0), ("agw", 1, 1, 1), ("agw", 0, 2, 1), ("agf", 1, 1, 1), ("ags", 1, 1), ("ags", 0, 2),
    ("agw", 1, 2, 0), ("agf", 1, 2, 0), ("agw", 0, 3, 0), ("ags", 0, 3), ("gath", 0), ("H", 0, 4), ("agw", 1, 2, 1),
    ("ags", 1, 2), ("agw", 1, 3, 0), ("ags", 1, 3), ("H", 4, 7), ("S", 0), ("tab",), ("P", 0), ("gath", 1), ("GO", 0),
    ("wm", 0, 0, 0, 0), ("GH",), ("zf", 0), ("wm", 0, 0, 0, 2), ("S", 1), ("P", 1), ("GI", 0), ("wm", 1, 0, 0, 0),
    ("zf", 1), ("wp", 0, 0, 0), ("zn", 0, 3), ("zn", 1, 3), ("wm", 1, 0, 0, 2), ("wp", 1, 0, 0), ("zn", 0, 2),
    ("zn", 1, 2), ("wd", 0, 0, 0), ("wm", 0, 1, 0, 0), ("zn", 0, 1), ("wd", 1, 0, 0), ("wm", 1, 1, 0, 0),
    ("wm", 1, 1, 0, 2), ("zn", 1, 1), ("wm", 0, 1, 0, 2), ("wp", 0, 1, 0), ("wp", 1, 1, 0), ("ag_sent",),
    ("w_sent", 0, 0), ("w_sent", 1, 0), ("wd", 0, 1, 0), ("zl", 0), ("wd", 1, 1, 0), ("zl", 1), ("z_sent", 0),
    ("z_sent", 1), ("w_sent", 0, 1), ("w_sent", 1, 1),
)


def cat(parts, axis):
    return jnp.concatenate(parts, axis=axis)


def dot(a, b):
    return jnp.dot(a, b, preferred_element_type=F32)


def kernel(
    col_hbm, cnt_hbm, x_hbm, g_hbm, win_hbm, wout_hbm,
    out_ref, ing_ref, gwin_ref, gwout_ref,
    xg, gg, win, wout, wint, woutt, dgelu, hid, gpre, cbuf, run, part, sib, zb,
    wgt, wp, red, w2, tabv, tab, col_ref, cnt_ref,
    lsem, ag_s, ag_r, sb_s, sb_r, ss_s, ss_r, zs, zr, xs, xr,
):
    dp = lax.axis_index("dp")
    tn = lax.axis_index("tensor")
    yy, xx = dp // NQ, dp % NQ
    z, core = tn // 2, tn % 2

    zat = [z] + [(z + i) % NZ for i in range(1, NZ)]
    yat = [yy] + [(yy + i) % NQ for i in range(1, NQ)]
    xat = [xx] + [(xx + i) % NQ for i in range(1, NQ)]
    other = 1 - core
    chunk = [[zat[i] * 2 + core for i in range(NZ)], [zat[i] * 2 + other for i in range(NZ)]]
    first = [[t * U for t in half] for half in chunk]
    zdevs = {i: {"dp": dp, "tensor": chunk[0][i % NZ]} for i in (1, -1)}
    sdev = {"dp": dp, "tensor": chunk[1][0]}
    ydevs = {i: {"dp": yat[i % NQ] * NQ + xx, "tensor": tn} for i in (1, -1)}
    xdevs = {i: {"dp": yy * NQ + xat[i % NQ], "tensor": tn} for i in (1, -1)}
    zdev, ydev, xdev = zdevs.get, ydevs.get, xdevs.get
    own_row, sib_row = core * CH, other * CH

    def landed(view, rsem):
        rcopy(view, view, lsem.at[0], rsem, sdev).wait_recv()

    def sent(view, ssem):
        rcopy(view, view, ssem, lsem.at[0], sdev).wait_send()

    def rcopy(src, dst, ssem, rsem, dev):
        return pltpu.make_async_remote_copy(
            src_ref=src, dst_ref=dst, send_sem=ssem, recv_sem=rsem,
            device_id=dev, device_id_type=MESH,
        )

    def go(copy):
        copy.start()

    barrier = pltpu.get_barrier_semaphore()
    for dev in (sdev, zdev(1), zdev(-1), xdev(1), xdev(-1), ydev(1), ydev(-1)):
        pl.semaphore_signal(barrier, inc=1, device_id=dev, device_id_type=MESH)

    fields = (xg, gg)
    own = pl.ds(first[0][0], U)
    local = [
        pltpu.make_async_copy(x_hbm, xg.at[own], lsem.at[0]),
        pltpu.make_async_copy(g_hbm, gg.at[own], lsem.at[1]),
        pltpu.make_async_copy(win_hbm, win, lsem.at[2]),
        pltpu.make_async_copy(wout_hbm, wout, lsem.at[3]),
        pltpu.make_async_copy(col_hbm, col_ref, lsem.at[5]),
        pltpu.make_async_copy(cnt_hbm, cnt_ref, lsem.at[6]),
    ]
    for c in local:
        c.start()

    def live_col(n, s):
        return jnp.where(s < cnt_ref[n], col_ref[n, s], DB)

    def make_table():
        sub = lax.broadcasted_iota(jnp.int32, (8, 128), 0)
        lan = lax.broadcasted_iota(jnp.int32, (8, 128), 1)
        down = []
        across = jnp.full((8, 128), 1000, jnp.int32)
        for n in range(ROWS):
            v = jnp.zeros((8, 128), jnp.int32)
            for s in range(SLOTS):
                c = live_col(n, s)
                v = jnp.where(sub == s, c, v)
                across = jnp.where(lan == n * SLOTS + s, c, across)
            down.append(v)
        across = across * 64 + lan

        def add_rows(parts):
            t = parts[0]
            for v in parts[1:]:
                t = t + v
            for sh in (4, 2, 1):
                t = t + pltpu.roll(t, sh, 0)
            return t

        def count(v):
            return jnp.where(v, 1, 0)

        spots = [jnp.full((8, 128), n * SLOTS, jnp.int32) + sub for n in range(ROWS)]
        ranks = []
        for n in range(ROWS):
            t = count(across < down[n] * 64 + spots[n])
            for sh in (64, 32, 16, 8, 4, 2, 1):
                t = t + pltpu.roll(t, sh, 1)
            ranks.append(t)
        perm = add_rows([jnp.where(ranks[n] == lan, spots[n], 0) for n in range(ROWS)])
        cols = add_rows([jnp.where(ranks[n] == lan, down[n], 0) for n in range(ROWS)])
        same = count((cols == pltpu.roll(cols, 1, 1)) & (lan > 0))
        upto = add_rows([count(down[n] <= lan) for n in range(ROWS)])
        here = add_rows([count(down[n] == lan) for n in range(ROWS)])
        last = jnp.where(here > 0, upto - 1, NB)
        tabv[...] = jnp.where(sub == 0, perm, jnp.where(sub == 1, same, last))

    for ref in fields:
        ref[2 * DB] = jnp.zeros((64, BLK), BF)
        ref[2 * DB + 1] = jnp.zeros((64, BLK), BF)
    run[NB] = jnp.zeros((BLK, BLK), BF)

    def piece(ref, side, step, lo=0, n=U):
        return ref.at[pl.ds(first[side][step % NZ] + lo, n)]

    def wrap(step):
        return zat[step % NZ]

    def ag_copy(a, way, k, h):
        step = -(k + 1) if way == 0 else k + 1
        v = piece(fields[a], 0, step, *SPAN[h])
        i = ((a * 2 + way) * 4 + k) * 2 + h
        return rcopy(v, v, ag_s.at[a], ag_r.at[i], zdev(1 if way == 0 else -1))

    def ag_send(a, way, k, h):
        step = -k if way == 0 else k
        v = piece(fields[a], 0, step, *SPAN[h])
        i = ((a * 2 + way) * 4 + k) * 2 + h
        return rcopy(v, v, ag_s.at[a], ag_r.at[i], zdev(1 if way == 0 else -1))

    def sb_place(j):
        if j == 0:
            return 0, (0, U)
        if j < 7:
            way, k = (j - 1) // 3, (j - 1) % 3
            return (-(k + 1) if way == 0 else k + 1), (0, U)
        return 4, SPAN[j - 7]

    def sb_copy(a, j, mine):
        step, span = sb_place(j)
        v = piece(fields[a], 0 if mine else 1, step, *span)
        return rcopy(v, v, sb_s.at[a], sb_r.at[a], sdev)

    def part_of(way, i):
        return way if i == 0 else 1 - way

    def ag_first(a, i):
        for way in range(2):
            go(ag_send(a, way, 0, part_of(way, i)))

    def ag_wait(a, k, i):
        for way in range(2):
            ag_copy(a, way, k, part_of(way, i)).wait_recv()

    def ag_pass(a, k, i):
        for way in range(2):
            go(ag_send(a, way, k + 1, part_of(way, i)))

    def ag_own(a):
        go(sb_copy(a, 0, True))

    def ag_sib(a, k):
        for way in range(2):
            go(sb_copy(a, 7 + way if k == 3 else 1 + 3 * way + k, True))

    def gathered(a):
        landed(fields[a].at[pl.ds(0, NZ * U)], sb_r.at[a])

    def turn():
        def body(n, carry):
            for s in range(SLOTS):
                i = n * SLOTS + s
                wint[n, :, s * BLK:(s + 1) * BLK] = win[i].T
                woutt[i] = wout[i].T
            return carry

        lax.fori_loop(0, ROWS, body, 0)

    def listed(ref, n):
        parts = []
        for s in range(SLOTS):
            i = live_col(n, s) * 2
            parts += [ref[i], ref[i + 1]]
        return cat(parts, 0)

    def tall(ref, n):
        return ref[n * SLOTS:(n + 1) * SLOTS].reshape(SLOTS * BLK, BLK)

    def hidden(lo, hi):
        for n in range(lo, hi):
            pre = dot(wint[n], listed(xg, n))
            sq = pre * pre
            th = jnp.tanh(C0 * pre * (1.0 + C1 * sq))
            half = 0.5 * (1.0 + th)
            dgelu[n] = half + 0.5 * pre * (1.0 - th * th) * (C0 * (1.0 + 3.0 * C1 * sq))
            hid[n] = (pre * half).astype(BF)

    def shares(a):
        w, act = ((woutt, hid), (win, gpre))[a]
        for n in range(ROWS):
            cbuf[n * SLOTS:(n + 1) * SLOTS] = dot(tall(w, n), act[n]).reshape(SLOTS, BLK, BLK)

    def sib_copy(a, g):
        span = pl.ds(0, FIRST) if g == 0 else pl.ds(FIRST, NZ - FIRST)
        src = part.at[a, span, pl.ds(pl.multiple_of(sib_row, 64), CH)]
        return rcopy(src, sib.at[a, span], ss_s.at[a], ss_r.at[a * 2 + g], sdev)

    def place(a):
        def add(r, acc):
            acc = acc * tab[1, r].astype(F32) + cbuf[tab[0, r]]
            run[r] = acc.astype(BF)
            return acc

        lax.fori_loop(0, NB, add, jnp.zeros((BLK, BLK), F32), unroll=4)
        for j, step in enumerate(ORDER):
            zz = wrap(step)
            for k in range(7):
                part[a, j, BLK * k:BLK * (k + 1), :] = run[tab[2, zz * 7 + k]]
            if j == FIRST - 1:
                go(sib_copy(a, 0))
        go(sib_copy(a, 1))

    met = set()

    def chip_sum(a, step, h):
        j = ORDER.index(step if step in ORDER else step + NZ)
        g = 0 if j < FIRST else 1
        if (a, g) not in met:
            met.add((a, g))
            sib_copy(a, g).wait_recv()
        src = part.at[a, j, pl.ds(pl.multiple_of(own_row + h * H, 32), H)]
        return src, src[...].astype(F32) + sib[a, j, h * H:(h + 1) * H].astype(F32)

    def z_copy(src, a, way, r):
        dst = zb.at[a, way, r]
        if r == 3:
            dst = dst.at[pl.ds(way * H, H)]
        return rcopy(src, dst, zs.at[a], zr.at[a * 4 + r], zdev(1 if way == 0 else -1))

    def z_first(a):
        for way in range(2):
            src, total = chip_sum(a, 4 if way == 0 else -4, way)
            src[...] = total.astype(BF)
            go(z_copy(src, a, way, 3))

    def z_next(a, r):
        if r == 3:
            landed(zb.at[a, :, r, pl.ds(0, H)], zr.at[a * 4 + r])
        else:
            landed(zb.at[a, :, r], zr.at[a * 4 + r])
        for way in range(2):
            for h in range(2):
                src, total = chip_sum(a, r if way == 0 else -r, h)
                buf = zb.at[a, way, r, pl.ds(h * H, H)]
                if r < 3 or h == way:
                    total = total + buf[...].astype(F32)
                buf[...] = total.astype(BF)
            go(z_copy(zb.at[a, way, r], a, way, r - 1))

    def z_last(a):
        dst = (out_ref, ing_ref)[a]
        landed(zb.at[a, :, 0], zr.at[a * 4])
        for h in range(2):
            src, total = chip_sum(a, 0, h)
            for way in range(2):
                total = total + zb[a, way, 0, h * H:(h + 1) * H].astype(F32)
            dst[h * H:(h + 1) * H, :] = total.astype(BF)

    coords = ((yat, xat), (xat, yat))
    devs = ((ydev, xdev), (xdev, ydev))

    def lines(p, g):
        lo, hi = GROUPS[g]
        return pl.ds(p * W + lo * 16, (hi - lo) * 16)

    def w_dst(a, ph, p, g, m):
        return wp.at[a, m, :, lines(p, g)] if ph == 0 else w2.at[a, m, lines(p, g)]

    def w_copy(src, a, ph, p, g, m):
        sign = 1 if p % 2 == 0 else -1
        i = ((a * 2 + ph) * len(GROUPS) + g) * 2 + (0 if m == 0 else 1)
        return rcopy(
            src, w_dst(a, ph, p, g, m), xs.at[a * 2 + ph], xr.at[i], devs[p // 2][ph](sign if m < 2 else -sign)
        )

    def w_landed(a, ph, g, m):
        i = ((a * 2 + ph) * len(GROUPS) + g) * 2 + (0 if m == 0 else 1)
        lo, hi = GROUPS[g]
        span = pl.ds(0, (hi - lo) * 64)
        if m == 0:
            view = wp.at[a, 0, :, span] if ph == 0 else w2.at[a, 0, span]
        else:
            view = wp.at[a, pl.ds(1, 2), :, span] if ph == 0 else w2.at[a, pl.ds(1, 2), span]
        landed(view, xr.at[i])

    def w_src(a, ph, p, g, step):
        c = coords[p // 2][ph][(step if p % 2 == 0 else -step) % NQ]
        if ph == 0:
            return wgt.at[a, c, :, lines(p, g)]
        return red.at[a, c, lines(p, g)]

    def w_send(a, ph, g, m):
        for p in range(4):
            go(w_copy(w_src(a, ph, p, g, 2 if m == 0 else -1), a, ph, p, g, m))

    def w_pass(a, ph, g):
        w_landed(a, ph, g, 0)
        for p in range(4):
            buf = w_dst(a, ph, p, g, 0)
            mine = w_src(a, ph, p, g, 1)
            buf[...] = (buf[...].astype(F32) + mine[...].astype(F32)).astype(BF)
            go(w_copy(buf, a, ph, p, g, 1))

    def w_done(a, ph, g):
        dst = (gwout_ref, gwin_ref)[a]
        lo, hi = GROUPS[g]
        w_landed(a, ph, g, 1)
        for p in range(4):
            total = w_src(a, ph, p, g, 0)[...].astype(F32)
            for m in (2, 1):
                buf = w_dst(a, ph, p, g, m)
                total = total + buf[...].astype(F32)
            if ph == 0:
                red[a, :, lines(p, g)] = total.astype(BF)
            else:
                for n in range(lo, hi):
                    dst[n * 64 + p * 16:n * 64 + p * 16 + 16, :] = total[(n - lo) * 16:(n - lo) * 16 + 16]

    def store(a, n, p, both):
        both = both.astype(BF).reshape(NQ, NQ, 16, BLK)
        row = p * W + n * 16
        if p < 2:
            wgt[a, :, :, row:row + 16, :] = both
        else:
            for i in range(NQ):
                for j in range(NQ):
                    wgt[a, i, j, row:row + 16, :] = both[j, i]

    def backward_hidden():
        for n in range(ROWS):
            gh = dot(cat([wout[n * SLOTS + s] for s in range(SLOTS)], 1), listed(gg, n))
            gpre[n] = (gh * dgelu[n]).astype(BF)

    def backward_out(g):
        for n in range(*GROUPS[g]):
            gw = lax.dot_general(hid[n], listed(gg, n), NT, preferred_element_type=F32)
            for p in range(4):
                one = gw[:, 2 * p * BLK:(2 * p + 1) * BLK].reshape(16, 8, BLK)
                two = gw[:, (2 * p + 1) * BLK:(2 * p + 2) * BLK].reshape(16, 8, BLK)
                store(0, n, p, cat([one, two], 1))

    def backward_in(g):
        for n in range(*GROUPS[g]):
            gw = lax.dot_general(listed(xg, n), gpre[n], NT, preferred_element_type=F32)
            gw = gw.reshape(SLOTS, 16, 8, BLK)
            for p in range(4):
                store(1, n, p, cat([gw[2 * p], gw[2 * p + 1]], 1))

    def ag_sent():
        for a in range(2):
            sent(fields[a].at[pl.ds(0, 7 * U)], ag_s.at[a])
            sent(fields[a].at[pl.ds(0, NZ * U)], sb_s.at[a])

    def z_sent(a):
        sent(sib.at[a], ss_s.at[a])
        sent(sib.at[a, pl.ds(0, 7)], zs.at[a])

    def w_sent(a, ph):
        sent(wp.at[a] if ph == 0 else w2.at[a], xs.at[a * 2 + ph])

    def make():
        local[4].wait()
        local[5].wait()
        make_table()
        tcopy.start()

    def turned():
        local[2].wait()
        local[3].wait()
        turn()

    tcopy = pltpu.make_async_copy(tabv, tab, lsem.at[4])
    tasks = {
        "ag0": ag_first, "agw": ag_wait, "agf": ag_pass, "own": ag_own, "ags": ag_sib, "gath": gathered,
        "tabl": make, "turn": turned, "H": hidden, "GH": backward_hidden, "GO": backward_out,
        "GI": backward_in, "S": shares, "P": place, "zf": z_first, "zn": z_next, "zl": z_last,
        "wm": w_send, "wp": w_pass, "wd": w_done, "tab": tcopy.wait, "ag_sent": ag_sent, "z_sent": z_sent, "w_sent": w_sent,
    }
    local[0].wait()
    local[1].wait()
    pl.semaphore_wait(barrier, 7)
    for name, *args in PLAN:
        tasks[name](*args)


def finish(*refs):
    for i in range(4):
        refs[4 + i][...] = refs[i][...]


def on_device(inputs, out_grad, w_in, w_out, columns, counts):
    vm = pl.BlockSpec(memory_space=pltpu.VMEM)
    hbm = pl.BlockSpec(memory_space=pltpu.HBM)
    dma = pltpu.SemaphoreType.DMA
    shapes = (
        jax.ShapeDtypeStruct((CH, BLK), BF),
        jax.ShapeDtypeStruct((CH, BLK), BF),
        jax.ShapeDtypeStruct((CH, BLK), F32),
        jax.ShapeDtypeStruct((CH, BLK), F32),
    )
    res = pl.pallas_call(
        kernel,
        out_shape=shapes,
        in_specs=[hbm] * 6,
        out_specs=(vm, vm, vm, vm),
        scratch_shapes=[
            pltpu.VMEM((2 * DB + 2, 64, BLK), BF),
            pltpu.VMEM((2 * DB + 2, 64, BLK), BF),
            pltpu.VMEM((NB, BLK, BLK), BF),
            pltpu.VMEM((NB, BLK, BLK), BF),
            pltpu.VMEM((ROWS, BLK, SLOTS * BLK), BF),
            pltpu.VMEM((NB, BLK, BLK), BF),
            pltpu.VMEM((ROWS, BLK, 128), F32),
            pltpu.VMEM((ROWS, BLK, 128), BF),
            pltpu.VMEM((ROWS, BLK, 128), BF),
            pltpu.VMEM((NB, BLK, 128), F32),
            pltpu.VMEM((NB + 1, BLK, 128), BF),
            pltpu.VMEM((2, NZ, 2 * CH, BLK), BF),
            pltpu.VMEM((2, NZ, CH, BLK), BF),
            pltpu.VMEM((2, 2, 4, CH, BLK), BF),
            pltpu.VMEM((2, NQ, NQ, CH, BLK), BF),
            pltpu.VMEM((2, 3, NQ, CH, BLK), BF),
            pltpu.VMEM((2, NQ, CH, BLK), BF),
            pltpu.VMEM((2, 3, CH, BLK), BF),
            pltpu.VMEM((8, 128), jnp.int32),
            pltpu.SMEM((8, 128), jnp.int32),
            pltpu.SMEM((ROWS, SLOTS), jnp.int32),
            pltpu.SMEM((ROWS,), jnp.int32),
            dma((7,)),
            dma((2,)), dma((32,)),
            dma((2,)), dma((2,)),
            dma((2,)), dma((4,)),
            dma((2,)), dma((8,)),
            dma((4,)), dma((8,)),
        ],
        compiler_params=pltpu.CompilerParams(
            collective_id=0, has_side_effects=True, vmem_limit_bytes=63 * 1024 * 1024
        ),
        cost_estimate=pl.CostEstimate(flops=1_409_286_144, bytes_accessed=8_000_000, transcendentals=114_688),
    )(
        columns, counts,
        inputs.T.reshape(U, 64, BLK), out_grad.T.reshape(U, 64, BLK),
        w_in.reshape(NB, BLK, BLK), w_out.reshape(NB, BLK, BLK),
    )
    out, ing, gwin, gwout = pl.pallas_call(
        finish,
        out_shape=shapes,
        in_specs=[vm] * 4,
        out_specs=(vm,) * 4,
        compiler_params=pltpu.CompilerParams(vmem_limit_bytes=63 * 1024 * 1024),
        cost_estimate=pl.CostEstimate(flops=0, bytes_accessed=1_400_000, transcendentals=0),
    )(*res)
    return (out.T, ing.T, gwin.reshape(ROWS, SLOTS, 8, BLK), gwout.reshape(ROWS, SLOTS, 8, BLK))


def solution(mesh):
    return jax.shard_map(
        on_device,
        mesh=mesh,
        in_specs=(
            P("dp", "tensor"),
            P("dp", "tensor"),
            P("tensor", None, None, None),
            P("tensor", None, None, None),
            P("tensor", None),
            P("tensor"),
        ),
        out_specs=(
            P("dp", "tensor"),
            P("dp", "tensor"),
            P("tensor", None, "dp", None),
            P("tensor", None, "dp", None),
        ),
        check_vma=False,
    )
```

```python
import jax
import jax.numpy as jnp
from jax import lax
from jax.experimental import pallas as pl
from jax.experimental.pallas import tpu as pltpu
from jax.sharding import PartitionSpec as P

BLK = 128
SLOTS = 8
ROWS = 7
NB = ROWS * SLOTS
DB = 56
NZ = 8
NQ = 4
CH = 448
U = 7
SPAN = ((0, 4), (4, 3))
H = 224
GROUPS = ((0, 7),)
BF = jnp.bfloat16
F32 = jnp.float32
MESH = pl.DeviceIdType.MESH
C0 = 0.7978845608028654
C1 = 0.044715
ORDER = (4, 3, -3, 2, -2, 1, -1, 0)
HALVES = (True, True)
FIRST = 3
NT = (((1,), (1,)), ((), ()))
PLAN = (
    ("ag0", 0, 0), ("ag0", 0, 1), ("turn",), ("own", 1), ("ag0", 1, 0), ("ag0", 1, 1), ("agw", 0, 0, 0),
    ("agf", 0, 0, 0), ("agw", 0, 0, 1), ("agf", 0, 0, 1), ("agw", 1, 0, 0), ("agf", 1, 0, 0), ("agw", 1, 0, 1),
    ("own", 0), ("agw", 0, 1, 0), ("agf", 0, 1, 0), ("tabl",), ("agf", 1, 0, 1), ("agw", 1, 1, 0), ("agf", 1, 1, 0),
    ("ags", 1, 0), ("ags", 0, 0), ("agw", 0, 1, 1), ("agf", 0, 1, 1), ("agw", 0, 2, 0), ("agf", 0, 2, 0),
    ("agw", 1, 1, 1), ("agf", 1, 1, 1), ("agw", 1, 2, 0), ("agf", 1, 2, 0), ("ags", 1, 1), ("agw", 0, 2, 1),
    ("ags", 0, 2), ("ags", 0, 1), ("agw", 0, 3, 0), ("ags", 0, 3), ("agw", 1, 2, 1), ("ags", 1, 2), ("agw", 1, 3, 0),
    ("ags", 1, 3), ("gath", 0), ("H", 0, 4), ("H", 4, 7), ("S", 0), ("tab",), ("P", 0), ("gath", 1), ("GO", 0),
    ("wm", 0, 0, 0, 0), ("GH",), ("wm", 0, 0, 0, 2), ("zf", 0), ("GI", 0), ("wm", 1, 0, 0, 0), ("S", 1), ("P", 1),
    ("zg", 0), ("zn", 0, 3, 0), ("wp", 0, 0, 0), ("zf", 1), ("wm", 1, 0, 0, 2), ("zg", 1), ("zn", 0, 2, 1),
    ("wp", 1, 0, 0), ("zn", 0, 2, 0), ("zn", 1, 3, 0), ("zn", 1, 2, 1), ("wd", 0, 0, 0), ("wm", 0, 1, 0, 0),
    ("zn", 0, 1, 1), ("zn", 1, 2, 0), ("wd", 1, 0, 0), ("wm", 1, 1, 0, 0), ("zn", 1, 1, 1), ("zn", 0, 1, 0),
    ("wm", 1, 1, 0, 2), ("wp", 0, 1, 0), ("wm", 0, 1, 0, 2), ("zn", 1, 1, 0), ("wp", 1, 1, 0), ("ag_sent",),
    ("w_sent", 0, 0), ("w_sent", 1, 0), ("wd", 0, 1, 0), ("zl", 0), ("zl", 1), ("wd", 1, 1, 0), ("z_sent", 0),
    ("z_sent", 1), ("w_sent", 0, 1), ("w_sent", 1, 1),
)


def cat(parts, axis):
    return jnp.concatenate(parts, axis=axis)


def dot(a, b):
    return jnp.dot(a, b, preferred_element_type=F32)


def kernel(
    col_hbm, cnt_hbm, x_hbm, g_hbm, win_hbm, wout_hbm,
    out_ref, ing_ref, gwin_ref, gwout_ref,
    xg, gg, win, wout, wint, woutt, dgelu, hid, gpre, cbuf, run, part, sib, zb,
    wgts, wps, reds, w2s, tabv, tab, col_ref, cnt_ref,
    lsem, ag_s, ag_r, sb_s, sb_r, ss_s, ss_r, zs, zr, xs, xr,
):
    dp = lax.axis_index("dp")
    tn = lax.axis_index("tensor")
    yy, xx = dp // NQ, dp % NQ
    z, core = tn // 2, tn % 2

    zat = [z] + [(z + i) % NZ for i in range(1, NZ)]
    yat = [yy] + [(yy + i) % NQ for i in range(1, NQ)]
    xat = [xx] + [(xx + i) % NQ for i in range(1, NQ)]
    other = 1 - core
    chunk = [[zat[i] * 2 + core for i in range(NZ)], [zat[i] * 2 + other for i in range(NZ)]]
    first = [[t * U for t in half] for half in chunk]
    zdevs = {i: {"dp": dp, "tensor": chunk[0][i % NZ]} for i in (1, -1)}
    sdev = {"dp": dp, "tensor": chunk[1][0]}
    ydevs = {i: {"dp": yat[i % NQ] * NQ + xx, "tensor": tn} for i in (1, -1)}
    xdevs = {i: {"dp": yy * NQ + xat[i % NQ], "tensor": tn} for i in (1, -1)}
    zdev, ydev, xdev = zdevs.get, ydevs.get, xdevs.get
    own_row, sib_row = core * CH, other * CH

    def landed(view, rsem):
        rcopy(view, view, lsem.at[0], rsem, sdev).wait_recv()

    def sent(view, ssem):
        rcopy(view, view, ssem, lsem.at[0], sdev).wait_send()

    def rcopy(src, dst, ssem, rsem, dev):
        return pltpu.make_async_remote_copy(
            src_ref=src, dst_ref=dst, send_sem=ssem, recv_sem=rsem,
            device_id=dev, device_id_type=MESH,
        )

    def go(copy):
        copy.start()

    barrier = pltpu.get_barrier_semaphore()
    for dev in (sdev, zdev(1), zdev(-1), xdev(1), xdev(-1), ydev(1), ydev(-1)):
        pl.semaphore_signal(barrier, inc=1, device_id=dev, device_id_type=MESH)

    fields = (xg, gg)
    own = pl.ds(first[0][0], U)
    local = [
        pltpu.make_async_copy(x_hbm, xg.at[own], lsem.at[0]),
        pltpu.make_async_copy(g_hbm, gg.at[own], lsem.at[1]),
        pltpu.make_async_copy(win_hbm, win, lsem.at[2]),
        pltpu.make_async_copy(wout_hbm, wout, lsem.at[3]),
        pltpu.make_async_copy(col_hbm, col_ref, lsem.at[5]),
        pltpu.make_async_copy(cnt_hbm, cnt_ref, lsem.at[6]),
    ]
    for c in local:
        c.start()

    def live_col(n, s):
        return jnp.where(s < cnt_ref[n], col_ref[n, s], DB)

    def make_table():
        sub = lax.broadcasted_iota(jnp.int32, (8, 128), 0)
        lan = lax.broadcasted_iota(jnp.int32, (8, 128), 1)
        down = []
        across = jnp.full((8, 128), 1000, jnp.int32)
        for n in range(ROWS):
            v = jnp.zeros((8, 128), jnp.int32)
            for s in range(SLOTS):
                c = live_col(n, s)
                v = jnp.where(sub == s, c, v)
                across = jnp.where(lan == n * SLOTS + s, c, across)
            down.append(v)
        across = across * 64 + lan

        def add_rows(parts):
            t = parts[0]
            for v in parts[1:]:
                t = t + v
            for sh in (4, 2, 1):
                t = t + pltpu.roll(t, sh, 0)
            return t

        def count(v):
            return jnp.where(v, 1, 0)

        spots = [jnp.full((8, 128), n * SLOTS, jnp.int32) + sub for n in range(ROWS)]
        ranks = []
        for n in range(ROWS):
            t = count(across < down[n] * 64 + spots[n])
            for sh in (64, 32, 16, 8, 4, 2, 1):
                t = t + pltpu.roll(t, sh, 1)
            ranks.append(t)
        perm = add_rows([jnp.where(ranks[n] == lan, spots[n], 0) for n in range(ROWS)])
        cols = add_rows([jnp.where(ranks[n] == lan, down[n], 0) for n in range(ROWS)])
        same = count((cols == pltpu.roll(cols, 1, 1)) & (lan > 0))
        upto = add_rows([count(down[n] <= lan) for n in range(ROWS)])
        here = add_rows([count(down[n] == lan) for n in range(ROWS)])
        last = jnp.where(here > 0, upto - 1, NB)
        tabv[...] = jnp.where(sub == 0, perm, jnp.where(sub == 1, same, last))

    for ref in fields:
        ref[2 * DB] = jnp.zeros((64, BLK), BF)
        ref[2 * DB + 1] = jnp.zeros((64, BLK), BF)
    run[NB] = jnp.zeros((BLK, BLK), BF)

    def piece(ref, side, step, lo=0, n=U):
        return ref.at[pl.ds(first[side][step % NZ] + lo, n)]

    def wrap(step):
        return zat[step % NZ]

    def ag_send(a, way, k, h):
        v = piece(fields[a], 0, -k if way == 0 else k, *SPAN[h])
        src = (x_hbm, g_hbm)[a].at[pl.ds(*SPAN[h])] if k == 0 else v
        i = (a * 4 + k) * 2 + (0 if h == way else 1)
        return rcopy(src, v, ag_s.at[a], ag_r.at[i], zdev(1 if way == 0 else -1))

    def sb_place(j):
        if j == 0:
            return 0, (0, U)
        if j < 7:
            way, k = (j - 1) // 3, (j - 1) % 3
            return (-(k + 1) if way == 0 else k + 1), (0, U)
        return 4, SPAN[j - 7]

    def sb_copy(a, j, mine):
        step, span = sb_place(j)
        v = piece(fields[a], 0 if mine else 1, step, *span)
        src = (x_hbm, g_hbm)[a] if j == 0 else v
        return rcopy(src, v, sb_s.at[a], sb_r.at[a], sdev)

    def part_of(way, i):
        return way if i == 0 else 1 - way

    def ag_first(a, i):
        for way in range(2):
            go(ag_send(a, way, 0, part_of(way, i)))

    def ag_wait(a, k, i):
        landed(fields[a].at[pl.ds(0, U)], ag_r.at[(a * 4 + k) * 2 + i])

    def ag_pass(a, k, i):
        for way in range(2):
            go(ag_send(a, way, k + 1, part_of(way, i)))

    def ag_own(a):
        go(sb_copy(a, 0, True))

    def ag_sib(a, k):
        for way in range(2):
            go(sb_copy(a, 7 + way if k == 3 else 1 + 3 * way + k, True))

    def gathered(a):
        local[a].wait()
        landed(fields[a].at[pl.ds(0, NZ * U)], sb_r.at[a])

    def turn():
        def body(n, carry):
            for s in range(SLOTS):
                i = n * SLOTS + s
                wint[n, :, s * BLK:(s + 1) * BLK] = win[i].T
                woutt[i] = wout[i].T
            return carry

        lax.fori_loop(0, ROWS, body, 0)

    def listed(ref, n):
        parts = []
        for s in range(SLOTS):
            i = live_col(n, s) * 2
            parts += [ref[i], ref[i + 1]]
        return cat(parts, 0)

    def tall(ref, n):
        return ref[n * SLOTS:(n + 1) * SLOTS].reshape(SLOTS * BLK, BLK)

    def hidden(lo, hi):
        for n in range(lo, hi):
            pre = dot(wint[n], listed(xg, n))
            sq = pre * pre
            th = jnp.tanh(C0 * pre * (1.0 + C1 * sq))
            half = 0.5 * (1.0 + th)
            dgelu[n] = half + 0.5 * pre * (1.0 - th * th) * (C0 * (1.0 + 3.0 * C1 * sq))
            hid[n] = (pre * half).astype(BF)

    def shares(a):
        w, act = ((woutt, hid), (win, gpre))[a]
        for n in range(ROWS):
            cbuf[n * SLOTS:(n + 1) * SLOTS] = dot(tall(w, n), act[n]).reshape(SLOTS, BLK, BLK)

    def sib_copy(a, g):
        span = pl.ds(0, FIRST) if g == 0 else pl.ds(FIRST, NZ - FIRST)
        src = part.at[a, span, pl.ds(pl.multiple_of(sib_row, 64), CH)]
        return rcopy(src, sib.at[a, span], ss_s.at[a], ss_r.at[a * 2 + g], sdev)

    def place(a):
        def add(r, acc):
            acc = acc * tab[1, r].astype(F32) + cbuf[tab[0, r]]
            run[r] = acc.astype(BF)
            return acc

        lax.fori_loop(0, NB, add, jnp.zeros((BLK, BLK), F32), unroll=4)
        for j, step in enumerate(ORDER):
            zz = wrap(step)
            for k in range(7):
                part[a, j, BLK * k:BLK * (k + 1), :] = run[tab[2, zz * 7 + k]]
            if j == FIRST - 1:
                go(sib_copy(a, 0))
        go(sib_copy(a, 1))

    met = set()

    def chip_sum(a, step, h):
        j = ORDER.index(step if step in ORDER else step + NZ)
        g = 0 if j < FIRST else 1
        if (a, g) not in met:
            met.add((a, g))
            sib_copy(a, g).wait_recv()
        src = part.at[a, j, pl.ds(pl.multiple_of(own_row + h * H, 32), H)]
        return src, src[...].astype(F32) + sib[a, j, h * H:(h + 1) * H].astype(F32)

    def z_half(ref, way, i):
        if i is None:
            return ref
        return ref.at[pl.ds((way if i == 0 else 1 - way) * H, H)]

    def z_sem(a, r, i):
        return zr.at[(a * 4 + r) * 2 + (i or 0)]

    def z_copy(src, a, way, r, i):
        dst = z_half(zb.at[a, way, r], way, i)
        return rcopy(src, dst, zs.at[a], z_sem(a, r, i), zdev(1 if way == 0 else -1))

    def z_wait(a, r, i):
        view = zb.at[a, :, r] if i is None else zb.at[a, :, r, pl.ds(0, H)]
        landed(view, z_sem(a, r, i))

    def z_start(a, r):
        for way in range(2):
            src, total = chip_sum(a, r + 1 if way == 0 else -(r + 1), way if r == 3 else 1 - way)
            src[...] = total.astype(BF)
            go(z_copy(src, a, way, r, 3 - r))

    def z_first(a):
        z_start(a, 3)

    def z_near(a):
        z_start(a, 2)

    def z_next(a, r, i=None):
        z_wait(a, r, 0 if r == 3 else i)
        for way in range(2):
            for h in range(2):
                if i is not None and h != (way if i == 0 else 1 - way):
                    continue
                src, total = chip_sum(a, r if way == 0 else -r, h)
                buf = zb.at[a, way, r, pl.ds(h * H, H)]
                if r < 3 or h == way:
                    total = total + buf[...].astype(F32)
                buf[...] = total.astype(BF)
            go(z_copy(z_half(zb.at[a, way, r], way, i), a, way, r - 1, i))

    def z_last(a):
        dst = (out_ref, ing_ref)[a]
        for i in (0, 1) if HALVES[a] else (None,):
            z_wait(a, 0, i)
        for h in range(2):
            src, total = chip_sum(a, 0, h)
            for way in range(2):
                total = total + zb[a, way, 0, h * H:(h + 1) * H].astype(F32)
            dst[h * H:(h + 1) * H, :] = total.astype(BF)

    coords = ((yat, xat), (xat, yat))
    devs = ((ydev, xdev), (xdev, ydev))

    def w_dst(a, ph, p, g, m):
        return wps[g].at[a, m, p] if ph == 0 else w2s[g].at[a, m, p]

    def w_sem(a, ph, g, m):
        return xr.at[((a * 2 + ph) * len(GROUPS) + g) * 2 + (0 if m == 0 else 1)]

    def w_copy(src, a, ph, p, g, m):
        sign = 1 if p % 2 == 0 else -1
        return rcopy(
            src, w_dst(a, ph, p, g, m), xs.at[(a * 2 + ph) * len(GROUPS) + g], w_sem(a, ph, g, m),
            devs[p // 2][ph](sign if m < 2 else -sign)
        )

    def w_landed(a, ph, g, m):
        ref = (wps if ph == 0 else w2s)[g]
        landed(ref.at[a, 0] if m == 0 else ref.at[a, pl.ds(1, 2)], w_sem(a, ph, g, m))

    def w_src(a, ph, p, g, step):
        c = coords[p // 2][ph][(step if p % 2 == 0 else -step) % NQ]
        return (wgts if ph == 0 else reds)[g].at[a, p, c]

    def w_send(a, ph, g, m):
        for p in range(4):
            go(w_copy(w_src(a, ph, p, g, 2 if m == 0 else -1), a, ph, p, g, m))

    def w_pass(a, ph, g):
        w_landed(a, ph, g, 0)
        for p in range(4):
            buf = w_dst(a, ph, p, g, 0)
            mine = w_src(a, ph, p, g, 1)
            buf[...] = (buf[...].astype(F32) + mine[...].astype(F32)).astype(BF)
            go(w_copy(buf, a, ph, p, g, 1))

    def w_done(a, ph, g):
        dst = (gwout_ref, gwin_ref)[a]
        lo, hi = GROUPS[g]
        w_landed(a, ph, g, 1)
        for p in range(4):
            total = w_src(a, ph, p, g, 0)[...].astype(F32)
            for m in (2, 1):
                buf = w_dst(a, ph, p, g, m)
                total = total + buf[...].astype(F32)
            if ph == 0:
                reds[g][a, p] = total.astype(BF)
            else:
                for n in range(lo, hi):
                    dst[n * 64 + p * 16:n * 64 + p * 16 + 16, :] = total[(n - lo) * 16:(n - lo) * 16 + 16]

    def store(a, n, p, both):
        both = both.astype(BF).reshape(NQ, NQ, 16, BLK)
        g = [lo <= n < hi for lo, hi in GROUPS].index(True)
        row = (n - GROUPS[g][0]) * 16
        if p < 2:
            wgts[g][a, p, :, :, row:row + 16, :] = both
        else:
            for i in range(NQ):
                for j in range(NQ):
                    wgts[g][a, p, i, j, row:row + 16, :] = both[j, i]

    def backward_hidden():
        for n in range(ROWS):
            gh = dot(cat([wout[n * SLOTS + s] for s in range(SLOTS)], 1), listed(gg, n))
            gpre[n] = (gh * dgelu[n]).astype(BF)

    def backward_out(g):
        for n in range(*GROUPS[g]):
            gw = lax.dot_general(hid[n], listed(gg, n), NT, preferred_element_type=F32)
            for p in range(4):
                one = gw[:, 2 * p * BLK:(2 * p + 1) * BLK].reshape(16, 8, BLK)
                two = gw[:, (2 * p + 1) * BLK:(2 * p + 2) * BLK].reshape(16, 8, BLK)
                store(0, n, p, cat([one, two], 1))

    def backward_in(g):
        for n in range(*GROUPS[g]):
            gw = lax.dot_general(listed(xg, n), gpre[n], NT, preferred_element_type=F32)
            gw = gw.reshape(SLOTS, 16, 8, BLK)
            for p in range(4):
                store(1, n, p, cat([gw[2 * p], gw[2 * p + 1]], 1))

    def ag_sent():
        for a in range(2):
            sent(fields[a].at[pl.ds(0, 7 * U)], ag_s.at[a])
            sent(fields[a].at[pl.ds(0, NZ * U)], sb_s.at[a])

    def z_sent(a):
        sent(sib.at[a], ss_s.at[a])
        sent(sib.at[a, pl.ds(0, 7)], zs.at[a])

    def w_sent(a, ph):
        for g in range(len(GROUPS)):
            sent((wps if ph == 0 else w2s)[g].at[a], xs.at[(a * 2 + ph) * len(GROUPS) + g])

    def make():
        local[4].wait()
        local[5].wait()
        make_table()
        tcopy.start()

    def turned():
        local[2].wait()
        local[3].wait()
        turn()

    tcopy = pltpu.make_async_copy(tabv, tab, lsem.at[4])
    tasks = {
        "ag0": ag_first, "agw": ag_wait, "agf": ag_pass, "own": ag_own, "ags": ag_sib, "gath": gathered,
        "tabl": make, "turn": turned, "H": hidden, "GH": backward_hidden, "GO": backward_out,
        "GI": backward_in, "S": shares, "P": place, "zf": z_first, "zg": z_near, "zn": z_next, "zl": z_last,
        "wm": w_send, "wp": w_pass, "wd": w_done, "tab": tcopy.wait, "ag_sent": ag_sent, "z_sent": z_sent, "w_sent": w_sent,
    }
    pl.semaphore_wait(barrier, 7)
    for name, *args in PLAN:
        tasks[name](*args)


def finish(*refs):
    for i in range(4):
        refs[4 + i][...] = refs[i][...]


def on_device(inputs, out_grad, w_in, w_out, columns, counts):
    vm = pl.BlockSpec(memory_space=pltpu.VMEM)
    hbm = pl.BlockSpec(memory_space=pltpu.HBM)
    dma = pltpu.SemaphoreType.DMA
    heights = [(hi - lo) * 16 for lo, hi in GROUPS]
    shapes = (
        jax.ShapeDtypeStruct((CH, BLK), BF),
        jax.ShapeDtypeStruct((CH, BLK), BF),
        jax.ShapeDtypeStruct((CH, BLK), F32),
        jax.ShapeDtypeStruct((CH, BLK), F32),
    )
    res = pl.pallas_call(
        kernel,
        out_shape=shapes,
        in_specs=[hbm] * 6,
        out_specs=(vm, vm, vm, vm),
        scratch_shapes=[
            pltpu.VMEM((2 * DB + 2, 64, BLK), BF),
            pltpu.VMEM((2 * DB + 2, 64, BLK), BF),
            pltpu.VMEM((NB, BLK, BLK), BF),
            pltpu.VMEM((NB, BLK, BLK), BF),
            pltpu.VMEM((ROWS, BLK, SLOTS * BLK), BF),
            pltpu.VMEM((NB, BLK, BLK), BF),
            pltpu.VMEM((ROWS, BLK, 128), F32),
            pltpu.VMEM((ROWS, BLK, 128), BF),
            pltpu.VMEM((ROWS, BLK, 128), BF),
            pltpu.VMEM((NB, BLK, 128), F32),
            pltpu.VMEM((NB + 1, BLK, 128), BF),
            pltpu.VMEM((2, NZ, 2 * CH, BLK), BF),
            pltpu.VMEM((2, NZ, CH, BLK), BF),
            pltpu.VMEM((2, 2, 4, CH, BLK), BF),
            [pltpu.VMEM((2, 4, NQ, NQ, r, BLK), BF) for r in heights],
            [pltpu.VMEM((2, 3, 4, NQ, r, BLK), BF) for r in heights],
            [pltpu.VMEM((2, 4, NQ, r, BLK), BF) for r in heights],
            [pltpu.VMEM((2, 3, 4, r, BLK), BF) for r in heights],
            pltpu.VMEM((8, 128), jnp.int32),
            pltpu.SMEM((8, 128), jnp.int32),
            pltpu.SMEM((ROWS, SLOTS), jnp.int32),
            pltpu.SMEM((ROWS,), jnp.int32),
            dma((7,)),
            dma((2,)), dma((16,)),
            dma((2,)), dma((2,)),
            dma((2,)), dma((4,)),
            dma((2,)), dma((16,)),
            dma((4,)), dma((8,)),
        ],
        compiler_params=pltpu.CompilerParams(
            collective_id=0, has_side_effects=True, vmem_limit_bytes=63 * 1024 * 1024
        ),
        cost_estimate=pl.CostEstimate(flops=1_409_286_144, bytes_accessed=8_000_000, transcendentals=114_688),
    )(
        columns, counts,
        inputs.T.reshape(U, 64, BLK), out_grad.T.reshape(U, 64, BLK),
        w_in.reshape(NB, BLK, BLK), w_out.reshape(NB, BLK, BLK),
    )
    out, ing, gwin, gwout = pl.pallas_call(
        finish,
        out_shape=shapes,
        in_specs=[vm] * 4,
        out_specs=(vm,) * 4,
        compiler_params=pltpu.CompilerParams(vmem_limit_bytes=63 * 1024 * 1024),
        cost_estimate=pl.CostEstimate(flops=0, bytes_accessed=1_400_000, transcendentals=0),
    )(*res)
    return (out.T, ing.T, gwin.reshape(ROWS, SLOTS, 8, BLK), gwout.reshape(ROWS, SLOTS, 8, BLK))


def solution(mesh):
    return jax.shard_map(
        on_device,
        mesh=mesh,
        in_specs=(
            P("dp", "tensor"),
            P("dp", "tensor"),
            P("tensor", None, None, None),
            P("tensor", None, None, None),
            P("tensor", None),
            P("tensor"),
        ),
        out_specs=(
            P("dp", "tensor"),
            P("dp", "tensor"),
            P("tensor", None, "dp", None),
            P("tensor", None, "dp", None),
        ),
        check_vma=False,
    )
```

```python
import jax
import jax.numpy as jnp
from jax import lax
from jax.experimental import pallas as pl
from jax.experimental.pallas import tpu as pltpu
from jax.sharding import PartitionSpec as P

BLK = 128
SLOTS = 8
ROWS = 7
NB = ROWS * SLOTS
DB = 56
NZ = 8
NQ = 4
CH = 448
U = 7
SPAN = ((0, 4), (4, 3))
H = 224
GROUPS = ((0, 7),)
BF = jnp.bfloat16
F32 = jnp.float32
MESH = pl.DeviceIdType.MESH
C0 = 0.7978845608028654
C1 = 0.044715
ORDER = (4, 3, -3, 2, -2, 1, -1, 0)
HALVES = (True, True)
FIRST = 3
NT = (((1,), (1,)), ((), ()))
PLAN = (
    ("ag0", 0, 0), ("ag0", 0, 1), ("turn",), ("own", 1), ("ag0", 1, 0), ("ag0", 1, 1), ("agw", 0, 0, 0),
    ("agf", 0, 0, 0), ("agw", 0, 0, 1), ("agf", 0, 0, 1), ("agw", 1, 0, 0), ("agf", 1, 0, 0), ("agw", 1, 0, 1),
    ("own", 0), ("agw", 0, 1, 0), ("agf", 0, 1, 0), ("tabl",), ("agf", 1, 0, 1), ("agw", 1, 1, 0), ("agf", 1, 1, 0),
    ("ags", 1, 0), ("ags", 0, 0), ("agw", 0, 1, 1), ("agf", 0, 1, 1), ("agw", 0, 2, 0), ("agf", 0, 2, 0),
    ("agw", 1, 1, 1), ("agf", 1, 1, 1), ("agw", 1, 2, 0), ("agf", 1, 2, 0), ("ags", 1, 1), ("agw", 0, 2, 1),
    ("ags", 0, 2), ("ags", 0, 1), ("agw", 0, 3, 0), ("ags", 0, 3), ("agw", 1, 2, 1), ("ags", 1, 2), ("agw", 1, 3, 0),
    ("ags", 1, 3), ("gath", 0), ("H", 0, 7), ("S", 0), ("tab",), ("P", 0), ("gath", 1), ("GO", 0),
    ("wm", 0, 0, 0, 0), ("GH",), ("wm", 0, 0, 0, 2), ("zf", 0), ("GI", 0), ("wm", 1, 0, 0, 0), ("S", 1), ("P", 1),
    ("zg", 0), ("zn", 0, 3, 0), ("wp", 0, 0, 0), ("zf", 1), ("wm", 1, 0, 0, 2), ("zg", 1), ("zn", 0, 2, 1),
    ("wp", 1, 0, 0), ("zn", 0, 2, 0), ("zn", 1, 3, 0), ("zn", 1, 2, 1), ("wd", 0, 0, 0), ("wm", 0, 1, 0, 0),
    ("zn", 0, 1, 1), ("zn", 1, 2, 0), ("wd", 1, 0, 0), ("wm", 1, 1, 0, 0), ("zn", 1, 1, 1), ("zn", 0, 1, 0),
    ("wm", 1, 1, 0, 2), ("wp", 0, 1, 0), ("wm", 0, 1, 0, 2), ("zn", 1, 1, 0), ("wp", 1, 1, 0), ("ag_sent",),
    ("w_sent", 0, 0), ("w_sent", 1, 0), ("wd", 0, 1, 0), ("zl", 0), ("zl", 1), ("wd", 1, 1, 0), ("z_sent", 0),
    ("z_sent", 1), ("w_sent", 0, 1), ("w_sent", 1, 1),
)


def cat(parts, axis):
    return jnp.concatenate(parts, axis=axis)


def dot(a, b):
    return jnp.dot(a, b, preferred_element_type=F32)


def kernel(
    col_hbm, cnt_hbm, x_hbm, g_hbm, win_hbm, wout_hbm,
    out_ref, ing_ref, gwin_ref, gwout_ref,
    xg, gg, win, wout, wint, woutt, dgelu, hid, gpre, cbuf, run, part, sib, zb,
    wgts, wps, reds, w2s, tabv, tab, col_ref, cnt_ref,
    lsem, ag_s, ag_r, sb_s, sb_r, ss_s, ss_r, zs, zr, xs, xr,
):
    dp = lax.axis_index("dp")
    tn = lax.axis_index("tensor")
    yy, xx = dp // NQ, dp % NQ
    z, core = tn // 2, tn % 2

    zat = [z] + [(z + i) % NZ for i in range(1, NZ)]
    yat = [yy] + [(yy + i) % NQ for i in range(1, NQ)]
    xat = [xx] + [(xx + i) % NQ for i in range(1, NQ)]
    other = 1 - core
    chunk = [[zat[i] * 2 + core for i in range(NZ)], [zat[i] * 2 + other for i in range(NZ)]]
    first = [[t * U for t in half] for half in chunk]
    zdevs = {i: {"dp": dp, "tensor": chunk[0][i % NZ]} for i in (1, -1)}
    sdev = {"dp": dp, "tensor": chunk[1][0]}
    ydevs = {i: {"dp": yat[i % NQ] * NQ + xx, "tensor": tn} for i in (1, -1)}
    xdevs = {i: {"dp": yy * NQ + xat[i % NQ], "tensor": tn} for i in (1, -1)}
    zdev, ydev, xdev = zdevs.get, ydevs.get, xdevs.get
    own_row, sib_row = core * CH, other * CH

    def landed(view, rsem):
        rcopy(view, view, lsem.at[0], rsem, sdev).wait_recv()

    def sent(view, ssem):
        rcopy(view, view, ssem, lsem.at[0], sdev).wait_send()

    def rcopy(src, dst, ssem, rsem, dev):
        return pltpu.make_async_remote_copy(
            src_ref=src, dst_ref=dst, send_sem=ssem, recv_sem=rsem,
            device_id=dev, device_id_type=MESH,
        )

    def go(copy):
        copy.start()

    barrier = pltpu.get_barrier_semaphore()
    for dev in (sdev, zdev(1), zdev(-1), xdev(1), xdev(-1), ydev(1), ydev(-1)):
        pl.semaphore_signal(barrier, inc=1, device_id=dev, device_id_type=MESH)

    fields = (xg, gg)
    own = pl.ds(first[0][0], U)
    local = [
        pltpu.make_async_copy(x_hbm, xg.at[own], lsem.at[0]),
        pltpu.make_async_copy(g_hbm, gg.at[own], lsem.at[1]),
        pltpu.make_async_copy(win_hbm, win, lsem.at[2]),
        pltpu.make_async_copy(wout_hbm, wout, lsem.at[3]),
        pltpu.make_async_copy(col_hbm, col_ref, lsem.at[5]),
        pltpu.make_async_copy(cnt_hbm, cnt_ref, lsem.at[6]),
    ]
    for c in local:
        c.start()

    def live_col(n, s):
        return jnp.where(s < cnt_ref[n], col_ref[n, s], DB)

    def make_table():
        sub = lax.broadcasted_iota(jnp.int32, (8, 128), 0)
        lan = lax.broadcasted_iota(jnp.int32, (8, 128), 1)
        down = []
        across = jnp.full((8, 128), 1000, jnp.int32)
        for n in range(ROWS):
            v = jnp.zeros((8, 128), jnp.int32)
            for s in range(SLOTS):
                c = live_col(n, s)
                v = jnp.where(sub == s, c, v)
                across = jnp.where(lan == n * SLOTS + s, c, across)
            down.append(v)
        across = across * 64 + lan

        def add_rows(parts):
            t = parts[0]
            for v in parts[1:]:
                t = t + v
            for sh in (4, 2, 1):
                t = t + pltpu.roll(t, sh, 0)
            return t

        def count(v):
            return jnp.where(v, 1, 0)

        spots = [jnp.full((8, 128), n * SLOTS, jnp.int32) + sub for n in range(ROWS)]
        ranks = []
        for n in range(ROWS):
            t = count(across < down[n] * 64 + spots[n])
            for sh in (64, 32, 16, 8, 4, 2, 1):
                t = t + pltpu.roll(t, sh, 1)
            ranks.append(t)
        perm = add_rows([jnp.where(ranks[n] == lan, spots[n], 0) for n in range(ROWS)])
        cols = add_rows([jnp.where(ranks[n] == lan, down[n], 0) for n in range(ROWS)])
        same = count((cols == pltpu.roll(cols, 1, 1)) & (lan > 0))
        upto = add_rows([count(down[n] <= lan) for n in range(ROWS)])
        here = add_rows([count(down[n] == lan) for n in range(ROWS)])
        last = jnp.where(here > 0, upto - 1, NB)
        tabv[...] = jnp.where(sub == 0, perm, jnp.where(sub == 1, same, last))

    for ref in fields:
        ref[2 * DB] = jnp.zeros((64, BLK), BF)
        ref[2 * DB + 1] = jnp.zeros((64, BLK), BF)
    run[NB] = jnp.zeros((BLK, BLK), BF)

    def piece(ref, side, step, lo=0, n=U):
        return ref.at[pl.ds(first[side][step % NZ] + lo, n)]

    def wrap(step):
        return zat[step % NZ]

    def ag_send(a, way, k, h):
        v = piece(fields[a], 0, -k if way == 0 else k, *SPAN[h])
        src = (x_hbm, g_hbm)[a].at[pl.ds(*SPAN[h])] if k == 0 else v
        i = (a * 4 + k) * 2 + (0 if h == way else 1)
        return rcopy(src, v, ag_s.at[a], ag_r.at[i], zdev(1 if way == 0 else -1))

    def sb_place(j):
        if j == 0:
            return 0, (0, U)
        if j < 7:
            way, k = (j - 1) // 3, (j - 1) % 3
            return (-(k + 1) if way == 0 else k + 1), (0, U)
        return 4, SPAN[j - 7]

    def sb_copy(a, j, mine):
        step, span = sb_place(j)
        v = piece(fields[a], 0 if mine else 1, step, *span)
        src = (x_hbm, g_hbm)[a] if j == 0 else v
        return rcopy(src, v, sb_s.at[a], sb_r.at[a], sdev)

    def part_of(way, i):
        return way if i == 0 else 1 - way

    def ag_first(a, i):
        for way in range(2):
            go(ag_send(a, way, 0, part_of(way, i)))

    def ag_wait(a, k, i):
        landed(fields[a].at[pl.ds(0, U)], ag_r.at[(a * 4 + k) * 2 + i])

    def ag_pass(a, k, i):
        for way in range(2):
            go(ag_send(a, way, k + 1, part_of(way, i)))

    def ag_own(a):
        go(sb_copy(a, 0, True))

    def ag_sib(a, k):
        for way in range(2):
            go(sb_copy(a, 7 + way if k == 3 else 1 + 3 * way + k, True))

    def gathered(a):
        local[a].wait()
        landed(fields[a].at[pl.ds(0, NZ * U)], sb_r.at[a])

    def turn():
        def body(n, carry):
            for s in range(SLOTS):
                i = n * SLOTS + s
                wint[n, :, s * BLK:(s + 1) * BLK] = win[i].T
                woutt[i] = wout[i].T
            return carry

        lax.fori_loop(0, ROWS, body, 0)

    def listed(ref, n):
        parts = []
        for s in range(SLOTS):
            i = live_col(n, s) * 2
            parts += [ref[i], ref[i + 1]]
        return cat(parts, 0)

    def tall(ref, n):
        return ref[n * SLOTS:(n + 1) * SLOTS].reshape(SLOTS * BLK, BLK)

    def hidden(lo, hi):
        for n in range(lo, hi):
            pre = dot(wint[n], listed(xg, n))
            sq = pre * pre
            th = jnp.tanh(C0 * pre * (1.0 + C1 * sq))
            half = 0.5 * (1.0 + th)
            dgelu[n] = half + 0.5 * pre * (1.0 - th * th) * (C0 * (1.0 + 3.0 * C1 * sq))
            hid[n] = (pre * half).astype(BF)

    def shares(a):
        w, act = ((woutt, hid), (win, gpre))[a]
        for n in range(ROWS):
            cbuf[n * SLOTS:(n + 1) * SLOTS] = dot(tall(w, n), act[n]).reshape(SLOTS, BLK, BLK)

    def sib_copy(a, g):
        span = pl.ds(0, FIRST) if g == 0 else pl.ds(FIRST, NZ - FIRST)
        src = part.at[a, span, pl.ds(pl.multiple_of(sib_row, 64), CH)]
        return rcopy(src, sib.at[a, span], ss_s.at[a], ss_r.at[a * 2 + g], sdev)

    def place(a):
        def add(r, acc):
            acc = acc * tab[1, r].astype(F32) + cbuf[tab[0, r]]
            run[r] = acc.astype(BF)
            return acc

        lax.fori_loop(0, NB, add, jnp.zeros((BLK, BLK), F32), unroll=14)
        for j, step in enumerate(ORDER):
            zz = wrap(step)
            for k in range(7):
                part[a, j, BLK * k:BLK * (k + 1), :] = run[tab[2, zz * 7 + k]]
            if j == FIRST - 1:
                go(sib_copy(a, 0))
        go(sib_copy(a, 1))

    met = set()

    def chip_sum(a, step, h):
        j = ORDER.index(step if step in ORDER else step + NZ)
        g = 0 if j < FIRST else 1
        if (a, g) not in met:
            met.add((a, g))
            sib_copy(a, g).wait_recv()
        src = part.at[a, j, pl.ds(pl.multiple_of(own_row + h * H, 32), H)]
        return src, src[...].astype(F32) + sib[a, j, h * H:(h + 1) * H].astype(F32)

    def z_half(ref, way, i):
        if i is None:
            return ref
        return ref.at[pl.ds((way if i == 0 else 1 - way) * H, H)]

    def z_sem(a, r, i):
        return zr.at[(a * 4 + r) * 2 + (i or 0)]

    def z_copy(src, a, way, r, i):
        dst = z_half(zb.at[a, way, r], way, i)
        return rcopy(src, dst, zs.at[a], z_sem(a, r, i), zdev(1 if way == 0 else -1))

    def z_wait(a, r, i):
        view = zb.at[a, :, r] if i is None else zb.at[a, :, r, pl.ds(0, H)]
        landed(view, z_sem(a, r, i))

    def z_start(a, r):
        for way in range(2):
            src, total = chip_sum(a, r + 1 if way == 0 else -(r + 1), way if r == 3 else 1 - way)
            src[...] = total.astype(BF)
            go(z_copy(src, a, way, r, 3 - r))

    def z_first(a):
        z_start(a, 3)

    def z_near(a):
        z_start(a, 2)

    def z_next(a, r, i=None):
        z_wait(a, r, 0 if r == 3 else i)
        for way in range(2):
            for h in range(2):
                if i is not None and h != (way if i == 0 else 1 - way):
                    continue
                src, total = chip_sum(a, r if way == 0 else -r, h)
                buf = zb.at[a, way, r, pl.ds(h * H, H)]
                if r < 3 or h == way:
                    total = total + buf[...].astype(F32)
                buf[...] = total.astype(BF)
            go(z_copy(z_half(zb.at[a, way, r], way, i), a, way, r - 1, i))

    def z_last(a):
        dst = (out_ref, ing_ref)[a]
        for i in (0, 1) if HALVES[a] else (None,):
            z_wait(a, 0, i)
        for h in range(2):
            src, total = chip_sum(a, 0, h)
            for way in range(2):
                total = total + zb[a, way, 0, h * H:(h + 1) * H].astype(F32)
            dst[h * H:(h + 1) * H, :] = total.astype(BF)

    coords = ((yat, xat), (xat, yat))
    devs = ((ydev, xdev), (xdev, ydev))

    def w_dst(a, ph, p, g, m):
        return wps[g].at[a, m, p] if ph == 0 else w2s[g].at[a, m, p]

    def w_sem(a, ph, g, m):
        return xr.at[((a * 2 + ph) * len(GROUPS) + g) * 2 + (0 if m == 0 else 1)]

    def w_copy(src, a, ph, p, g, m):
        sign = 1 if p % 2 == 0 else -1
        return rcopy(
            src, w_dst(a, ph, p, g, m), xs.at[(a * 2 + ph) * len(GROUPS) + g], w_sem(a, ph, g, m),
            devs[p // 2][ph](sign if m < 2 else -sign)
        )

    def w_landed(a, ph, g, m):
        ref = (wps if ph == 0 else w2s)[g]
        landed(ref.at[a, 0] if m == 0 else ref.at[a, pl.ds(1, 2)], w_sem(a, ph, g, m))

    def w_src(a, ph, p, g, step):
        c = coords[p // 2][ph][(step if p % 2 == 0 else -step) % NQ]
        return (wgts if ph == 0 else reds)[g].at[a, p, c]

    def w_send(a, ph, g, m):
        for p in range(4):
            go(w_copy(w_src(a, ph, p, g, 2 if m == 0 else -1), a, ph, p, g, m))

    def w_pass(a, ph, g):
        w_landed(a, ph, g, 0)
        for p in range(4):
            buf = w_dst(a, ph, p, g, 0)
            mine = w_src(a, ph, p, g, 1)
            buf[...] = (buf[...].astype(F32) + mine[...].astype(F32)).astype(BF)
            go(w_copy(buf, a, ph, p, g, 1))

    def w_done(a, ph, g):
        dst = (gwout_ref, gwin_ref)[a]
        lo, hi = GROUPS[g]
        w_landed(a, ph, g, 1)
        for p in range(4):
            total = w_src(a, ph, p, g, 0)[...].astype(F32)
            for m in (2, 1):
                buf = w_dst(a, ph, p, g, m)
                total = total + buf[...].astype(F32)
            if ph == 0:
                reds[g][a, p] = total.astype(BF)
            else:
                for n in range(lo, hi):
                    dst[n * 64 + p * 16:n * 64 + p * 16 + 16, :] = total[(n - lo) * 16:(n - lo) * 16 + 16]

    def store(a, n, p, both):
        both = both.astype(BF).reshape(NQ, NQ, 16, BLK)
        g = [lo <= n < hi for lo, hi in GROUPS].index(True)
        row = (n - GROUPS[g][0]) * 16
        if p < 2:
            wgts[g][a, p, :, :, row:row + 16, :] = both
        else:
            for i in range(NQ):
                for j in range(NQ):
                    wgts[g][a, p, i, j, row:row + 16, :] = both[j, i]

    def backward_hidden():
        for n in range(ROWS):
            gh = dot(cat([wout[n * SLOTS + s] for s in range(SLOTS)], 1), listed(gg, n))
            gpre[n] = (gh * dgelu[n]).astype(BF)

    def backward_out(g):
        for n in range(*GROUPS[g]):
            gw = lax.dot_general(hid[n], listed(gg, n), NT, preferred_element_type=F32)
            for p in range(4):
                one = gw[:, 2 * p * BLK:(2 * p + 1) * BLK].reshape(16, 8, BLK)
                two = gw[:, (2 * p + 1) * BLK:(2 * p + 2) * BLK].reshape(16, 8, BLK)
                store(0, n, p, cat([one, two], 1))

    def backward_in(g):
        for n in range(*GROUPS[g]):
            gw = lax.dot_general(listed(xg, n), gpre[n], NT, preferred_element_type=F32)
            gw = gw.reshape(SLOTS, 16, 8, BLK)
            for p in range(4):
                store(1, n, p, cat([gw[2 * p], gw[2 * p + 1]], 1))

    def ag_sent():
        for a in range(2):
            sent(fields[a].at[pl.ds(0, 7 * U)], ag_s.at[a])
            sent(fields[a].at[pl.ds(0, NZ * U)], sb_s.at[a])

    def z_sent(a):
        sent(sib.at[a], ss_s.at[a])
        sent(sib.at[a, pl.ds(0, 7)], zs.at[a])

    def w_sent(a, ph):
        for g in range(len(GROUPS)):
            sent((wps if ph == 0 else w2s)[g].at[a], xs.at[(a * 2 + ph) * len(GROUPS) + g])

    def make():
        local[4].wait()
        local[5].wait()
        make_table()
        tcopy.start()

    def turned():
        local[2].wait()
        local[3].wait()
        turn()

    tcopy = pltpu.make_async_copy(tabv, tab, lsem.at[4])
    tasks = {
        "ag0": ag_first, "agw": ag_wait, "agf": ag_pass, "own": ag_own, "ags": ag_sib, "gath": gathered,
        "tabl": make, "turn": turned, "H": hidden, "GH": backward_hidden, "GO": backward_out,
        "GI": backward_in, "S": shares, "P": place, "zf": z_first, "zg": z_near, "zn": z_next, "zl": z_last,
        "wm": w_send, "wp": w_pass, "wd": w_done, "tab": tcopy.wait, "ag_sent": ag_sent, "z_sent": z_sent, "w_sent": w_sent,
    }
    pl.semaphore_wait(barrier, 7)
    for name, *args in PLAN:
        tasks[name](*args)


def finish(*refs):
    for i in range(4):
        refs[4 + i][...] = refs[i][...]


def on_device(inputs, out_grad, w_in, w_out, columns, counts):
    vm = pl.BlockSpec(memory_space=pltpu.VMEM)
    hbm = pl.BlockSpec(memory_space=pltpu.HBM)
    dma = pltpu.SemaphoreType.DMA
    heights = [(hi - lo) * 16 for lo, hi in GROUPS]
    shapes = (
        jax.ShapeDtypeStruct((CH, BLK), BF),
        jax.ShapeDtypeStruct((CH, BLK), BF),
        jax.ShapeDtypeStruct((CH, BLK), F32),
        jax.ShapeDtypeStruct((CH, BLK), F32),
    )
    res = pl.pallas_call(
        kernel,
        out_shape=shapes,
        in_specs=[hbm] * 6,
        out_specs=(vm, vm, vm, vm),
        scratch_shapes=[
            pltpu.VMEM((2 * DB + 2, 64, BLK), BF),
            pltpu.VMEM((2 * DB + 2, 64, BLK), BF),
            pltpu.VMEM((NB, BLK, BLK), BF),
            pltpu.VMEM((NB, BLK, BLK), BF),
            pltpu.VMEM((ROWS, BLK, SLOTS * BLK), BF),
            pltpu.VMEM((NB, BLK, BLK), BF),
            pltpu.VMEM((ROWS, BLK, 128), F32),
            pltpu.VMEM((ROWS, BLK, 128), BF),
            pltpu.VMEM((ROWS, BLK, 128), BF),
            pltpu.VMEM((NB, BLK, 128), F32),
            pltpu.VMEM((NB + 1, BLK, 128), BF),
            pltpu.VMEM((2, NZ, 2 * CH, BLK), BF),
            pltpu.VMEM((2, NZ, CH, BLK), BF),
            pltpu.VMEM((2, 2, 4, CH, BLK), BF),
            [pltpu.VMEM((2, 4, NQ, NQ, r, BLK), BF) for r in heights],
            [pltpu.VMEM((2, 3, 4, NQ, r, BLK), BF) for r in heights],
            [pltpu.VMEM((2, 4, NQ, r, BLK), BF) for r in heights],
            [pltpu.VMEM((2, 3, 4, r, BLK), BF) for r in heights],
            pltpu.VMEM((8, 128), jnp.int32),
            pltpu.SMEM((8, 128), jnp.int32),
            pltpu.SMEM((ROWS, SLOTS), jnp.int32),
            pltpu.SMEM((ROWS,), jnp.int32),
            dma((7,)),
            dma((2,)), dma((16,)),
            dma((2,)), dma((2,)),
            dma((2,)), dma((4,)),
            dma((2,)), dma((16,)),
            dma((4,)), dma((8,)),
        ],
        compiler_params=pltpu.CompilerParams(
            collective_id=0, has_side_effects=True, vmem_limit_bytes=63 * 1024 * 1024
        ),
        cost_estimate=pl.CostEstimate(flops=1_409_286_144, bytes_accessed=8_000_000, transcendentals=114_688),
    )(
        columns, counts,
        inputs.T.reshape(U, 64, BLK), out_grad.T.reshape(U, 64, BLK),
        w_in.reshape(NB, BLK, BLK), w_out.reshape(NB, BLK, BLK),
    )
    out, ing, gwin, gwout = pl.pallas_call(
        finish,
        out_shape=shapes,
        in_specs=[vm] * 4,
        out_specs=(vm,) * 4,
        compiler_params=pltpu.CompilerParams(vmem_limit_bytes=63 * 1024 * 1024),
        cost_estimate=pl.CostEstimate(flops=0, bytes_accessed=1_400_000, transcendentals=0),
    )(*res)
    return (out.T, ing.T, gwin.reshape(ROWS, SLOTS, 8, BLK), gwout.reshape(ROWS, SLOTS, 8, BLK))


def solution(mesh):
    return jax.shard_map(
        on_device,
        mesh=mesh,
        in_specs=(
            P("dp", "tensor"),
            P("dp", "tensor"),
            P("tensor", None, None, None),
            P("tensor", None, None, None),
            P("tensor", None),
            P("tensor"),
        ),
        out_specs=(
            P("dp", "tensor"),
            P("dp", "tensor"),
            P("tensor", None, "dp", None),
            P("tensor", None, "dp", None),
        ),
        check_vma=False,
    )
```
